32 devices in a mesh: groups: 2 (over y), tile: 4 (over z), sub: 2 (over x), rep: 2 (over core).
Axes of the slice: x: 2, y: 2, z: 4, core: 2. Of those that a mesh axis runs over, the one named last changes fastest.
Arguments:
- pressure: float32 [64, 32, 256], P(('groups', 'tile'), 'sub', 'rep'), parts along dimension 0, may hold values from -3 to 3
- previous_pressure: float32 [64, 32, 256], P(('groups', 'tile'), 'sub', 'rep'), parts along dimension 0, may hold values from -3 to 3
- courant_square: float32 [64, 32, 256], P(('groups', 'tile'), 'sub', 'rep'), parts along dimension 0, may hold values from 0.07 to 0.22
- node_area: float32 [12288], P(('groups', 'tile', 'sub', 'rep')), parts along dimension 0, may hold values from 0.25 to 4
- mode_shapes: bfloat16 [12288, 2048], P(('groups', 'tile', 'sub', 'rep')), parts along dimension 0, may hold values from -0.049804688 to 0.049804688
- frequency: float32 [4096], P('groups'), parts along dimension 0, may hold values from 0.4 to 1.3
- damping_ratio: float32 [4096], P('groups'), parts along dimension 0, may hold values from 0.02 to 0.4
- modal_start: float32 [2, 4096], P(None, 'groups'), parts along dimension 1, may hold values from -4 to 4
- slot_cell: int32 [8, 2, 2, 384], P(('groups', 'tile'), 'sub', 'rep'), parts along dimension 0, may hold values from 0 to 16383, as said below
- slot_owner: int32 [8, 2, 2, 384, 1], P(('groups', 'tile'), 'sub', 'rep'), parts along dimension 0, may hold values from 0 to 3; in each aligned block of 384 rows (0 to 383, 384 to 767, ..., all dimensions but the last counted through in order) at most 96 rows name the same one
- surface_count: int32 [4, 2, 4], P(('groups', 'sub'), 'rep', 'tile'), parts along dimension 0, may hold values from 1 to 384, 512 in all within a row
Outputs:
- final_pressure: float32 [64, 32, 256], P(('groups', 'tile'), 'sub', 'rep'), parts along dimension 0
- prior_pressure: float32 [64, 32, 256], P(('groups', 'tile'), 'sub', 'rep'), parts along dimension 0
- surface_accel: bfloat16 [8, 2, 2, 4, 384], P(('groups', 'tile'), 'sub', 'rep'), parts along dimension 0
- modal_state: float32 [2, 4096], P(None, ('groups', 'tile', 'sub', 'rep')), parts along dimension 1
The draws below stay inside these ranges and needn't reach their ends.
There are 2 independent parts, one for each index of `groups`. The reference program is written for one: setup_inputs(seed, part) draws one part's arguments, and reference() takes and returns one part's arrays. A program takes and returns all parts, laid end to end along the dimension named above; each array names one. Nothing has to cross between parts.
Inputs may be any that keep to these rules, and one draw needn't show every extreme that they name: `slot_cell`: slot j of a block lies in the block's cells j * (42) to (j + 1) (42) - 1, so a block's slots name distinct cells. `slot_owner`: every owner index is named by exactly 96 of the 384 slots of each block (t, s, r). `surface_count`: for fixed s and r the counts over t sum to 128 times the number of tile indices, and one of them equals 384.
All inputs are finite; a program needn't handle non-finite values. No bound on the sum of `surface_count` on one device may be relied on, other than what follows from the above.
Results may differ from the reference program's by a relative error of at most 0.0098.
Values may be sent and summed in bfloat16 or wider, within the bound.
No kernel may reach another device: no remote copies, remote signals or barrier semaphores. Data moves between devices by JAX's collectives and lax.ppermute only.
A program may use at most 64 MiB of HBM per device.

```python
import math
import jax
import jax.numpy as jnp
import numpy as np
from jax import lax

CX = 8
CY = 16
CZ = 128
STEPS = 4
SLOTS = 384
MODES = 2048
SURF_MEAN = 128
CAP = 96
CELLS = 16384
NX = 32
NY = 32
NZ = 256
NODES = 6144
N_TILE = 4
N_SUB = 2
N_REP = 2


def draw_slot_cell(key, part):
    stride = CELLS // SLOTS
    offset = jax.random.randint(key, (N_TILE, N_SUB, N_REP, SLOTS), 0, stride, dtype=jnp.int32)
    return jnp.arange(SLOTS, dtype=jnp.int32) * stride + offset


def spiked(result, key, source, target, shards_of, factor):
    def block_of(axis_at):
        return (jnp.arange(result.shape[axis_at]) // (result.shape[axis_at] // shards_of)).reshape((-1,) + (1,) * (result.ndim - 1 - axis_at))

    near = jax.random.permutation(key, shards_of)[block_of(target)]
    second = (block_of(target) + shards_of // 2) % shards_of
    return jnp.where((block_of(source) == near) | (block_of(source) == second), factor * result, result)


def level_of(stream_key, dims, shards, low, largest):
    level = 1.0
    for dim, shards_of in shards:
        heights = jax.random.uniform(jax.random.fold_in(jax.random.fold_in(stream_key, 6), dim), (shards_of,), jnp.float32, low / len(shards), largest / len(shards))
        level = level * jnp.repeat(jnp.exp(heights), dims[dim] // shards_of).reshape((-1,) + (1,) * (len(dims) - 1 - dim))
    return level


def length_profile(number_of, total, bound, slope):
    portions = [(1 << 20) // math.isqrt(standing ** slope) + 1 for standing in range(2, number_of + 1)]
    rest, holding = total - bound - (number_of - 1), [1] * (number_of - 1)
    while rest > 0:
        candidates = [i for i in range(number_of - 1) if holding[i] < bound]
        mass, budget = sum([portions[i] for i in candidates]), rest
        for i in candidates:
            more = min(bound - holding[i], max(1, budget * portions[i] // mass), rest)
            holding[i] = holding[i] + more
            rest = rest - more
    return np.array([bound] + holding)


def ragged_sizes(own_key, count, total, bound, lean):
    if count == 2:
        one = jax.random.randint(own_key, (), max(1, total - bound), min(bound, total - 1) + 1)
        return jnp.stack([one, total - one])
    sizes = jnp.asarray(length_profile(count, total, bound, lean), jnp.int32)
    couples = (count - 1) // 2
    giver, receiver = sizes[1:1 + 2 * couples:2], sizes[2:2 + 2 * couples:2]
    room = jnp.minimum(giver - 1, bound - receiver)
    passed = jax.random.randint(jax.random.fold_in(own_key, 1), (couples,), 0, 1 << 20) % (room + 1)
    sizes = sizes.at[1:1 + 2 * couples:2].set(giver - passed).at[2:2 + 2 * couples:2].set(receiver + passed)
    return sizes[jax.random.permutation(jax.random.fold_in(own_key, 2), count)]


def shared_out(key, own, number, rows, number_of, top, bound, skew):
    ranking = jax.random.permutation(key, number_of)
    heavy_load, ordinary = shares(number_of, rows * top, bound, skew, True), shares(number_of, rows * top, bound, skew, False)
    places = jnp.arange(number_of)

    def named(tallies, rotation):
        used = int((tallies > 0).sum())
        fixed = max(1, used // 4)
        passed = fixed + (places - fixed + rotation * (used - fixed)) % max(1, number_of - fixed)
        return jnp.zeros((number_of,), jnp.int32).at[ranking[jnp.where(places < fixed, places, passed)]].set(jnp.asarray(tallies, jnp.int32))

    tallies = jnp.where(number % 4 == 0, named(heavy_load, number // 4), named(ordinary, number - number // 4 - 1))
    mixed = jax.random.permutation(jax.random.fold_in(own, 3), number_of)
    donor, receiver = mixed[0:number_of // 2 * 2:2], mixed[1:number_of // 2 * 2:2]
    margin = jnp.minimum(tallies[donor] - 1, bound - tallies[receiver]) // 2
    margin = jnp.where((donor == ranking[0]) | (receiver == ranking[0]) | (tallies[receiver] == 0), 0, jnp.maximum(margin, 0))
    passed = jax.random.randint(jax.random.fold_in(own, 4), (number_of // 2,), 0, 1 << 20) % (margin + 1)
    tallies = tallies.at[donor].add(-passed).at[receiver].add(passed)
    members = jnp.searchsorted(jnp.cumsum(tallies), jnp.arange(rows * top), side="right").astype(jnp.int32)
    table = members.reshape(top, rows).T
    table = table[jax.random.permutation(jax.random.fold_in(own, 1), rows)]
    rotation = jax.random.randint(jax.random.fold_in(own, 2), (rows, 1), 0, top)
    return jnp.take_along_axis(table, (jnp.arange(top)[None, :] + rotation) % top, axis=1)


def shares(amount, total, bound, skew, full):
    portions = [(1 << 20) // math.isqrt(grade ** skew) + 1 for grade in range(1, amount + 1)]
    largest = bound if full else min(bound, max(-(-total // amount), total * portions[0] // sum(portions)))
    least = 1 if total - largest >= amount - 1 else 0
    holding, spare = [largest] + [least] * (amount - 1), total - largest - least * (amount - 1)
    while spare > 0:
        free = [i for i in range(1, amount) if holding[i] < largest] or [i for i in range(1, amount) if holding[i] < bound]
        pool, left = sum([portions[i] for i in free]), spare
        for i in free:
            more = min(bound - holding[i], max(1, left * portions[i] // pool), spare)
            holding[i] = holding[i] + more
            spare = spare - more
    return np.array(holding)


def scatter_about(stream_key, extent, width, limit, cuts=(), kind=jnp.bfloat16):
    loudness = level_of(stream_key, extent, cuts, -0.22, 0.18) if cuts else 1.0
    drawn = jax.random.normal(stream_key, extent, jnp.float32) * width * loudness
    return jnp.minimum(jnp.maximum(drawn, -limit), limit).astype(kind)


def gaussian_with(key, dims, deviation, reach, split, heavy, kind=jnp.bfloat16):
    entries = deviation * jax.random.normal(key, dims, jnp.float32)
    if split:
        entries = entries * level_of(key, dims, split, -0.22, 0.18)
    return jnp.clip(spiked(entries, jax.random.fold_in(key, 3), *heavy), -reach, reach).astype(kind)


def setup_inputs(seed: int = 0, part: int = 0) -> dict:
    splits = jax.random.split(jax.random.key(seed), 12)
    part_splits = jax.random.split(jax.random.fold_in(splits[11], part), 12)
    pressure = scatter_about(part_splits[0], (NX, NY, NZ), 0.5, 3.0, ((0, 4), (1, 2), (2, 2)), jnp.float32)
    previous_pressure = scatter_about(part_splits[1], (NX, NY, NZ), 0.5, 3.0, ((0, 4), (1, 2), (2, 2)), jnp.float32)
    courant_square = jnp.clip(0.07 + 0.15 * jax.random.uniform(part_splits[2], (NX, NY, NZ), jnp.float32) ** level_of(part_splits[2], (NX, NY, NZ), ((0, 4), (1, 2), (2, 2)), -0.2, 0.2), 0.07, 0.22)
    node_area = jnp.clip(jnp.exp(math.log(4.0) - 2.7725887 * jax.random.uniform(part_splits[3], (NODES,), jnp.float32) ** level_of(part_splits[3], (NODES,), ((0, 16),), -0.2, 0.2)), 0.25, 4.0)
    mode_shapes = gaussian_with(part_splits[4], (NODES, MODES), 0.008, 0.049804688, ((0, 16),), (0, 1, 16, 2.0))
    frequency = jnp.clip(jnp.exp(jax.random.uniform(part_splits[5], (MODES,), jnp.float32, math.log(0.4), math.log(1.3))), 0.4, 1.3)
    damping_ratio = jnp.clip(jnp.exp(jax.random.uniform(part_splits[6], (MODES,), jnp.float32, math.log(0.02), math.log(0.4))), 0.02, 0.4)
    modal_start = scatter_about(part_splits[7], (2, MODES), 1.0, 4.0, (), jnp.float32)
    slot_cell = draw_slot_cell(jax.random.fold_in(jax.random.fold_in(splits[11], part), 71), part)
    slot_owner_keys = jax.random.split(jax.random.fold_in(part_splits[9], 1), N_TILE * N_SUB * N_REP * SLOTS // SLOTS)
    slot_owner_turns = jax.random.permutation(jax.random.fold_in(part_splits[9], 3), N_TILE * N_SUB * N_REP * SLOTS // SLOTS)
    slot_owner = jax.vmap(lambda own, number: shared_out(jax.random.fold_in(part_splits[9], 2), own, number, SLOTS, N_TILE, 1, CAP, 0))(slot_owner_keys, slot_owner_turns).reshape((N_TILE, N_SUB, N_REP, SLOTS, 1))
    surface_count = jax.vmap(lambda own: ragged_sizes(own, N_TILE, N_TILE * SURF_MEAN, SLOTS, 2))(jax.random.split(part_splits[10], N_SUB * N_REP)).reshape((N_SUB, N_REP, N_TILE)).astype(jnp.int32)
    return dict(pressure=pressure, previous_pressure=previous_pressure, courant_square=courant_square, node_area=node_area, mode_shapes=mode_shapes, frequency=frequency, damping_ratio=damping_ratio, modal_start=modal_start, slot_cell=slot_cell, slot_owner=slot_owner, surface_count=surface_count)


nonlinear = 0.03
viscous = 0.02


def laplace(padded):
    middle = padded[1:-1, 1:-1, 1:-1]
    summed = padded[2:, 1:-1, 1:-1] + padded[:-2, 1:-1, 1:-1]
    summed = summed + padded[1:-1, 2:, 1:-1] + padded[1:-1, :-2, 1:-1]
    summed = summed + padded[1:-1, 1:-1, 2:] + padded[1:-1, 1:-1, :-2]
    return summed - 6.0 * middle


def advance(wide_now, wide_before, coefficient):
    current = wide_now[1:-1, 1:-1, 1:-1]
    before = wide_before[1:-1, 1:-1, 1:-1]
    change = current - before
    driving = coefficient * laplace(wide_now) + viscous * laplace(wide_now - wide_before) + 2.0 * nonlinear * change * change
    return 2.0 * current - before + (1.0 + 2.0 * nonlinear * current) * driving


def routing(owners, live_count, tile_total):
    slot_total = owners.shape[0]
    bucket = slot_total // tile_total
    position = jnp.arange(slot_total, dtype=jnp.int32)
    is_live = position < live_count
    member = ((owners[:, None] == jnp.arange(tile_total, dtype=jnp.int32)[None, :]) & is_live[:, None]).astype(jnp.float32)
    earlier = (position[None, :] < position[:, None]).astype(jnp.float32)
    before = jnp.dot(earlier, member, precision=lax.Precision.HIGHEST)
    bucket_rank = jnp.sum(before * member, axis=1).astype(jnp.int32)
    target = owners * bucket + bucket_rank
    return ((target[:, None] == position[None, :]) & is_live[:, None]).astype(jnp.bfloat16)


def oscillate(forces, frequency, damping_ratio, start_state):
    def advance_mode(carried, force_row):
        displace, velocity = carried
        acceleration = force_row - 2.0 * damping_ratio * frequency * velocity - frequency * frequency * displace
        velocity = velocity + acceleration
        displace = displace + velocity
        return (displace, velocity), acceleration

    (displace, velocity), modal_accel = lax.scan(advance_mode, (start_state[0], start_state[1]), forces)
    return modal_accel, jnp.stack([displace, velocity])


def reference(pressure, previous_pressure, courant_square, node_area, mode_shapes, frequency, damping_ratio, modal_start, slot_cell, slot_owner, surface_count):
    devices = N_TILE * N_SUB * N_REP
    bucket = SLOTS // N_TILE
    cell_first = slot_cell // (CY * CZ)
    cell_second = (slot_cell // CZ) % CY
    cell_third = slot_cell % CZ
    grid_first = jnp.arange(N_TILE, dtype=jnp.int32)[:, None, None, None] * CX + cell_first
    grid_second = jnp.arange(N_SUB, dtype=jnp.int32)[None, :, None, None] * CY + cell_second
    grid_third = jnp.arange(N_REP, dtype=jnp.int32)[None, None, :, None] * CZ + cell_third
    flat_index = ((grid_first * NY + grid_second) * NZ + grid_third).astype(jnp.int32)
    counts = jnp.transpose(surface_count, (2, 0, 1))
    is_live = jnp.arange(SLOTS, dtype=jnp.int32)[None, None, None, :] < counts[..., None]
    grid_now = pressure
    grid_before = previous_pressure
    records = []
    for step_index in range(STEPS):
        updated = advance(jnp.pad(grid_now, 1), jnp.pad(grid_before, 1), courant_square)
        records.append(jnp.take(updated.reshape(-1), flat_index))
        grid_before = grid_now
        grid_now = updated
    history = jnp.where(is_live[:, :, :, None, :], jnp.stack(records, axis=3), jnp.float32(0.0)).astype(jnp.bfloat16)

    def route_for(owners, live_count):
        return routing(owners, live_count, N_TILE)

    routes = jax.vmap(route_for)(slot_owner.reshape(devices, SLOTS), counts.reshape(devices))
    loads = jnp.einsum("dns,dst->dnt", history.reshape(devices, STEPS, SLOTS).astype(jnp.float32), routes.astype(jnp.float32))
    loads = loads.astype(jnp.bfloat16).reshape(N_TILE, N_SUB, N_REP, STEPS, N_TILE, bucket)
    arrived = jnp.transpose(loads, (4, 1, 2, 3, 0, 5))
    area_rows = node_area.reshape(N_TILE, N_SUB, N_REP, 1, N_TILE, bucket)
    weighted = (arrived * area_rows).astype(jnp.bfloat16)
    weighted = jnp.transpose(weighted, (3, 0, 1, 2, 4, 5)).reshape(STEPS, NODES)
    forces = jnp.dot(weighted, mode_shapes, preferred_element_type=jnp.float32)
    modal_accel, modal_state = oscillate(forces, frequency, damping_ratio, modal_start)
    node_accel = jnp.dot(modal_accel.astype(jnp.bfloat16), mode_shapes.T, preferred_element_type=jnp.float32).astype(jnp.bfloat16)
    returned = node_accel.reshape(STEPS, N_TILE, N_SUB, N_REP, N_TILE, bucket)
    returned = jnp.transpose(returned, (4, 2, 3, 0, 1, 5)).reshape(devices, STEPS, SLOTS)
    surface = jnp.einsum("dnt,dst->dns", returned.astype(jnp.float32), routes.astype(jnp.float32))
    surface_accel = surface.astype(jnp.bfloat16).reshape(N_TILE, N_SUB, N_REP, STEPS, SLOTS)
    return grid_now, grid_before, surface_accel, modal_state
```

```python
import functools

import jax
import jax.numpy as jnp
from jax import lax
from jax.experimental import pallas as pl
from jax.experimental.pallas import tpu as pltpu
from jax.sharding import PartitionSpec as P

STEPS = 4
FIELDS = 3
SUBLANES = 8

nonlinear = 0.03
viscous = 0.02

f32 = jnp.float32
bf16 = jnp.bfloat16
VMEM = pl.BlockSpec(memory_space=pltpu.VMEM)
SMEM = pl.BlockSpec(memory_space=pltpu.SMEM)


def shift(count, by):
    return [(i, (i + by) % count) for i in range(count)]


def line(count, by):
    return [(i, i + by) for i in range(count) if 0 <= i + by < count]


def iota(shape, dim):
    return lax.broadcasted_iota(jnp.int32, shape, dim)


def dot(a, b, contract):
    return lax.dot_general(a, b, (((contract[0],), (contract[1],)), ((), ())), preferred_element_type=f32)


def call(kernel, out_shape, inputs, scratch=(), specs=None, flops=1_000_000):
    return pl.pallas_call(
        kernel,
        out_shape=out_shape,
        in_specs=specs or [VMEM] * len(inputs),
        out_specs=jax.tree.map(lambda _: VMEM, out_shape),
        scratch_shapes=list(scratch),
        cost_estimate=pl.CostEstimate(flops=flops, bytes_accessed=1_000_000, transcendentals=0),
        compiler_params=pltpu.CompilerParams(vmem_limit_bytes=32 * 1024 * 1024),
    )(*inputs)


def shape_of(dims, dtype):
    return jax.ShapeDtypeStruct(dims, dtype)


def both_ways(axis, ahead, behind):
    count = lax.axis_size(axis)
    after = lax.ppermute(behind, axis, line(count, -1))
    before = lax.ppermute(ahead, axis, line(count, 1))
    return after, before


def route_kernel(buckets, owner_ref, cell_ref, count_ref, route_ref, place_ref, *, lanes, rows):
    slots = owner_ref.shape[1]
    bucket = slots // buckets
    me = lax.axis_index("tile")
    owner = owner_ref[...]
    live = iota((1, slots), 1) < count_ref[0, 0]
    held = -(-buckets // SUBLANES) * SUBLANES
    member = jnp.where((iota((held, slots), 0) == owner) & live, 1.0, 0.0)
    earlier = jnp.where(iota((slots, slots), 0) < iota((slots, slots), 1), 1.0, 0.0).astype(bf16)
    before = dot(member.astype(bf16), earlier, (1, 0))
    rank = jnp.sum(before * member, axis=0, keepdims=True).astype(jnp.int32)
    away = owner - me
    away = jnp.where(away < 0, away + buckets, away)
    target = jnp.where(live, away * bucket + rank, -1)
    route = jnp.where(iota((slots, slots), 0) == target, 1.0, 0.0).astype(bf16)
    route_ref[...] = route
    cell = cell_ref[...]
    row = jnp.where(iota((rows, slots), 0) == cell // lanes, 1.0, 0.0)
    lane = jnp.where(iota((lanes, slots), 0) == cell % lanes, 1.0, 0.0)
    place_ref[:, :rows] = dot(route, row.astype(bf16), (1, 1)).astype(bf16)
    place_ref[:, rows:] = dot(route, lane.astype(bf16), (1, 1)).astype(bf16)


def pack_sub_kernel(ends, p_ref, q_ref, c_ref, *outs):
    layers, rows, lanes = p_ref.shape
    low = iota((SUBLANES, lanes), 0) < STEPS
    for at, ref in enumerate((p_ref, q_ref, c_ref)):
        for pair in range(layers // 2):
            tiles = []
            for layer in (2 * pair, 2 * pair + 1):
                last = pltpu.roll(ref[layer, rows - SUBLANES :, :], STEPS, 0)
                first = ref[layer, :SUBLANES, :]
                tiles.append((last, first))
            picked = [jnp.where(low, a, pltpu.roll(b, STEPS, 0)) for a, b in zip(*tiles)]
            if ends == 1:
                picked = [jnp.where(lax.axis_index("sub") == 0, picked[0], picked[1])]
            for out, value in zip(outs, picked):
                out[at, pair * SUBLANES : (pair + 1) * SUBLANES, :] = value.astype(bf16)


def side_rows(at, layer, after_ref, before_ref):
    start = layer // 2 * SUBLANES
    after = after_ref[at, start : start + SUBLANES, :].astype(f32)
    before = before_ref[at, start : start + SUBLANES, :].astype(f32)
    if layer % 2 == 0:
        before = pltpu.roll(before, STEPS, 0)
    else:
        after = pltpu.roll(after, STEPS, 0)
    me, count = lax.axis_index("sub"), lax.axis_size("sub")
    low = iota(after.shape, 0) < STEPS
    keep_after = jnp.where(me < count - 1, 1.0, 0.0)
    keep_before = jnp.where(me > 0, 1.0, 0.0)
    return jnp.where(low, after * keep_after, before * keep_before)


def pack_tile_kernel(p_ref, q_ref, c_ref, after_ref, before_ref, ahead_ref, behind_ref):
    layers = p_ref.shape[0]
    for out, base in ((ahead_ref, layers - STEPS), (behind_ref, 0)):
        for at, ref in enumerate((p_ref, q_ref, c_ref)):
            for k in range(STEPS):
                out[at * STEPS + k] = ref[base + k].astype(bf16)
            for k in range(0, STEPS, 2):
                beside = [side_rows(at, base + k + i, after_ref, before_ref) for i in range(2)]
                out[FIELDS * STEPS + (at * STEPS + k) // 2] = jnp.concatenate(beside, 0).astype(bf16)


def end_lanes(lanes):
    row = iota((2 * STEPS, lanes), 0)
    wanted = jnp.where(row < STEPS, row, lanes - 2 * STEPS + row)
    return jnp.where(iota((2 * STEPS, lanes), 1) == wanted, 1.0, 0.0).astype(bf16)


def pack_rep_kernel(p_ref, q_ref, c_ref, sub_after, sub_before, tile_after, tile_before, out_ref, wide):
    layers, rows, lanes = p_ref.shape
    beside = 2 * STEPS
    total = layers + 2 * STEPS
    picks = end_lanes(lanes)
    for at, ref in enumerate((p_ref, q_ref, c_ref)):
        for side, base in ((tile_before, 0), (tile_after, STEPS + layers)):
            wide[base * rows : (base + STEPS) * rows, :] = side[at * STEPS : (at + 1) * STEPS].reshape(STEPS * rows, lanes)
            start = total * rows + base * beside
            packed = FIELDS * STEPS + at * STEPS // 2
            wide[start : start + STEPS * beside, :] = side[packed : packed + STEPS // 2].reshape(STEPS * beside, lanes)
        for k in range(layers):
            wide[(STEPS + k) * rows : (STEPS + k + 1) * rows, :] = ref[k].astype(bf16)
        for k in range(0, layers, 2):
            start = total * rows + (STEPS + k) * beside
            pair = [side_rows(at, k + i, sub_after, sub_before) for i in range(2)]
            wide[start : start + 2 * beside, :] = jnp.concatenate(pair, 0).astype(bf16)
        width = wide.shape[0]
        out_ref[:, at * width : (at + 1) * width] = dot(picks, wide[...], (1, 1)).astype(bf16)


def window_kernel(
    p_ref, q_ref, c_ref, sub_after, sub_before, tile_after, tile_before, rep_after, rep_before, place_ref,
    final_ref, prior_ref, *rest,
):
    *sends, now, ago, coef, lapped, seen = rest
    layers, rows, lanes = p_ref.shape
    beside = 2 * STEPS
    total = layers + 2 * STEPS
    wide_rows, wide_lanes = rows + beside, 2 * lanes
    tile, tiles = lax.axis_index("tile"), lax.axis_size("tile")
    sub, subs = lax.axis_index("sub"), lax.axis_size("sub")
    rep, reps = lax.axis_index("rep"), lax.axis_size("rep")

    picks = end_lanes(lanes)
    width = total * wide_rows
    end = iota((2 * STEPS, width), 0) < STEPS
    keep_after = jnp.where(rep < reps - 1, 1.0, 0.0)
    keep_before = jnp.where(rep > 0, 1.0, 0.0)
    for at, (ref, out) in enumerate(((p_ref, now), (q_ref, ago), (c_ref, coef))):
        for k in range(layers):
            out[STEPS + k, :rows, :lanes] = ref[k]
            out[STEPS + k, rows:, :lanes] = side_rows(at, k, sub_after, sub_before)
        for side, base in ((tile_before, 0), (tile_after, STEPS + layers)):
            for k in range(STEPS):
                out[base + k, :rows, :lanes] = side[at * STEPS + k].astype(f32)
                pair = side[FIELDS * STEPS + (at * STEPS + k) // 2].astype(f32)
                out[base + k, rows:, :lanes] = pair[k % 2 * beside : (k % 2 + 1) * beside]
        after = rep_after[:, at * width : (at + 1) * width].astype(f32) * keep_after
        before = rep_before[:, at * width : (at + 1) * width].astype(f32) * keep_before
        strip = dot(jnp.where(end, after, before).astype(bf16), picks, (0, 0))
        for k in range(total):
            out[k, :rows, lanes:] = strip[k * rows : (k + 1) * rows]
            out[k, rows:, lanes:] = strip[total * rows + k * beside : total * rows + (k + 1) * beside]

    row = iota((wide_rows, wide_lanes), 0)
    lane = iota((wide_rows, wide_lanes), 1)
    inside = (row < rows) | ((row < rows + STEPS) & (sub < subs - 1)) | ((row >= rows + STEPS) & (sub > 0))
    inside &= (lane < lanes) | ((lane < lanes + STEPS) & (rep < reps - 1)) | ((lane >= wide_lanes - STEPS) & (rep > 0))
    inside = jnp.where(inside, 1.0, 0.0)
    inside_low = inside * jnp.where(tile > 0, 1.0, 0.0)
    inside_high = inside * jnp.where(tile < tiles - 1, 1.0, 0.0)

    def laplace(below, here, above):
        summed = below + above
        summed = summed + pltpu.roll(here, 1, 0) + pltpu.roll(here, wide_rows - 1, 0)
        summed = summed + pltpu.roll(here, 1, 1) + pltpu.roll(here, wide_lanes - 1, 1)
        return summed - 6.0 * here

    for k in range(1, total - 1):
        lapped[k] = laplace(ago[k - 1], ago[k], ago[k + 1])
    for step in range(STEPS):
        below = now[step]
        here = now[step + 1]
        for k in range(step + 1, total - step - 1):
            above = now[k + 1]
            before = ago[k]
            lap = laplace(below, here, above)
            change = here - before
            driving = coef[k] * lap + viscous * (lap - lapped[k]) + 2.0 * nonlinear * change * change
            updated = 2.0 * here - before + (1.0 + 2.0 * nonlinear * here) * driving
            mask = inside_low if k < STEPS else inside_high if k >= STEPS + layers else inside
            updated = updated * mask
            now[k] = updated
            ago[k] = here
            lapped[k] = lap
            own = k - STEPS
            if 0 <= own < layers:
                core = updated[:rows, :lanes]
                seen[own * rows : (own + 1) * rows, step * lanes : (step + 1) * lanes] = core.astype(bf16)
                if step == STEPS - 1:
                    final_ref[own] = core
                if step == STEPS - 2:
                    prior_ref[own] = core
            below, here = here, above

    cells = layers * rows
    steps_at = iota((SUBLANES, STEPS * lanes), 1) // lanes == iota((SUBLANES, STEPS * lanes), 0)
    steps_at = jnp.where(steps_at, 1.0, 0.0).astype(bf16)
    size = place_ref.shape[0] // len(sends)
    for at, send in enumerate(sends):
        part = place_ref[at * size : (at + 1) * size, :]
        found = dot(part[:, :cells], seen[...], (1, 0))
        lane_of = part[:, cells:].astype(f32)
        found = jnp.concatenate([found[:, i * lanes : (i + 1) * lanes] * lane_of for i in range(STEPS)], 1)
        send[...] = dot(steps_at, found.astype(bf16), (1, 1))[:STEPS].astype(bf16)


def spread(at, size, total, bucket):
    wanted = iota((size, 1), 0) + at * size + lax.axis_index("tile") * bucket
    wanted = jnp.where(wanted >= total, wanted - total, wanted)
    return jnp.where(iota((size, total), 1) == wanted, 1.0, 0.0).astype(bf16)


def project_kernel(buckets, area_ref, shapes_ref, *rest):
    *parts, out_ref = rest
    total = area_ref.shape[1]
    size = parts[0].shape[1]
    loads = 0.0
    for at, part in enumerate(parts):
        loads = loads + dot(part[...], spread(at, size, total, total // buckets), (1, 0))
    weighted = (loads * area_ref[...]).astype(bf16)
    out_ref[...] = dot(weighted, shapes_ref[...], (1, 0))


def respond_kernel(buckets, addends, freq_ref, damp_ref, start_ref, shapes_ref, *rest):
    forces_in, rest = rest[:addends], rest[addends:]
    state_ref, *sends, accel = rest
    forces = forces_in[0][...]
    for ref in forces_in[1:]:
        forces = forces + ref[...]
    frequency, damping = freq_ref[...], damp_ref[...]
    drag, stiffness = 2.0 * damping * frequency, frequency * frequency
    displace, velocity = start_ref[0:1, :], start_ref[1:2, :]
    accel[...] = jnp.zeros_like(accel)
    for step in range(STEPS):
        acceleration = forces[step : step + 1, :] - drag * velocity - stiffness * displace
        velocity = velocity + acceleration
        displace = displace + velocity
        accel[step : step + 1, :] = acceleration
    state_ref[0:1, :] = displace
    state_ref[1:2, :] = velocity
    node = dot(accel[...].astype(bf16), shapes_ref[...], (1, 1)).astype(bf16)
    total = node.shape[1]
    size = total // len(sends)
    for at, send in enumerate(sends):
        send[...] = dot(node, spread(at, size, total, total // buckets), (1, 1))[:STEPS].astype(bf16)


def return_kernel(route_ref, *rest):
    *parts, out_ref = rest
    size = parts[0].shape[1]
    surface = 0.0
    for at, part in enumerate(parts):
        surface = surface + dot(part[...], route_ref[at * size : (at + 1) * size, :], (1, 0))
    out_ref[...] = surface.astype(bf16)


def exchange(parts, buckets):
    if len(parts) == buckets:
        return [parts[0]] + [lax.ppermute(parts[-k], "tile", shift(buckets, -k)) for k in range(1, buckets)]
    me = lax.axis_index("tile")
    (whole,) = parts
    steps, total = whole.shape
    stacked = whole.reshape(steps, buckets, total // buckets).transpose(1, 0, 2)
    stacked = lax.all_to_all(jnp.roll(stacked, me, 0), "tile", 0, 0, tiled=True)
    return [jnp.roll(stacked, -me, 0).transpose(1, 0, 2).reshape(steps, total)]


def body(
    pressure,
    previous_pressure,
    courant_square,
    node_area,
    mode_shapes,
    frequency,
    damping_ratio,
    modal_start,
    slot_cell,
    slot_owner,
    surface_count,
):
    buckets, subs, reps = (lax.axis_size(axis) for axis in ("tile", "sub", "rep"))
    layers, rows, lanes = pressure.shape
    slots = slot_cell.shape[-1]
    modes = mode_shapes.shape[1]
    bucket = slots // buckets
    parts = buckets if buckets <= 4 and bucket % 16 == 0 else 1
    fields = (pressure, previous_pressure, courant_square)
    total = layers + 2 * STEPS
    wide_rows = rows + 2 * STEPS

    route, place = call(
        functools.partial(route_kernel, buckets, lanes=lanes, rows=layers * rows),
        (shape_of((slots, slots), bf16), shape_of((slots, layers * rows + lanes), bf16)),
        (slot_owner.reshape(1, slots), slot_cell.reshape(1, slots), surface_count.reshape(1, 1)),
        specs=[VMEM, VMEM, SMEM],
    )

    ends = 1 if subs == 2 else 2
    slab = shape_of((FIELDS, layers * STEPS, lanes), bf16)
    packed = call(functools.partial(pack_sub_kernel, ends), (slab,) * ends, fields)
    if subs == 2:
        sub_halo = (lax.ppermute(packed[0], "sub", shift(2, 1)),) * 2
    else:
        sub_halo = both_ways("sub", *packed)
    slab = shape_of((FIELDS * STEPS * 3 // 2, rows, lanes), bf16)
    packed = call(pack_tile_kernel, (slab, slab), (*fields, *sub_halo))
    tile_halo = both_ways("tile", *packed)
    packed = call(
        pack_rep_kernel,
        shape_of((2 * STEPS, FIELDS * total * wide_rows), bf16),
        (*fields, *sub_halo, *tile_halo),
        scratch=[pltpu.VMEM((total * wide_rows, lanes), bf16)],
    )
    if reps == 2:
        rep_halo = (lax.ppermute(packed, "rep", shift(2, 1)),) * 2
    else:
        rep_halo = both_ways("rep", packed, packed)

    wide = pltpu.VMEM((total, wide_rows, 2 * lanes), f32)
    part = shape_of((STEPS, slots // parts), bf16)
    block = shape_of(pressure.shape, f32)
    final_field, prior_field, *sends = call(
        window_kernel,
        (block, block) + (part,) * parts,
        (*fields, *sub_halo, *tile_halo, *rep_halo, place),
        scratch=[wide] * 4 + [pltpu.VMEM((layers * rows, STEPS * lanes), bf16)],
        flops=50_000_000,
    )

    forces = call(
        functools.partial(project_kernel, buckets),
        shape_of((STEPS, modes), f32),
        (node_area.reshape(1, slots), mode_shapes, *exchange(sends, buckets)),
    )
    addends = [forces]
    for axis in ("rep", "sub", "tile"):
        count = lax.axis_size(axis)
        forces = functools.reduce(jnp.add, addends)
        if count <= 4:
            addends = [forces] + [lax.ppermute(forces, axis, shift(count, k)) for k in range(1, count)]
        else:
            addends = [lax.psum(forces, axis)]

    state, *sends = call(
        functools.partial(respond_kernel, buckets, len(addends)),
        (shape_of((2, modes), f32),) + (part,) * parts,
        (frequency.reshape(1, modes), damping_ratio.reshape(1, modes), modal_start, mode_shapes, *addends),
        scratch=[pltpu.VMEM((SUBLANES, modes), f32)],
    )
    share = modes // (buckets * subs * reps)
    modal_state = lax.dynamic_slice_in_dim(state, lax.axis_index(("tile", "sub", "rep")) * share, share, 1)
    surface = call(return_kernel, shape_of((STEPS, slots), bf16), (route, *exchange(sends, buckets)))
    return (final_field, prior_field, surface.reshape(1, 1, 1, STEPS, slots), modal_state)


def solution(mesh):
    in_specs = (
        P(("groups", "tile"), "sub", "rep"),
        P(("groups", "tile"), "sub", "rep"),
        P(("groups", "tile"), "sub", "rep"),
        P(("groups", "tile", "sub", "rep")),
        P(("groups", "tile", "sub", "rep"), None),
        P("groups"),
        P("groups"),
        P(None, "groups"),
        P(("groups", "tile"), "sub", "rep", None),
        P(("groups", "tile"), "sub", "rep", None, None),
        P(("groups", "sub"), "rep", "tile"),
    )
    out_specs = (
        P(("groups", "tile"), "sub", "rep"),
        P(("groups", "tile"), "sub", "rep"),
        P(("groups", "tile"), "sub", "rep", None, None),
        P(None, ("groups", "tile", "sub", "rep")),
    )
    return jax.shard_map(body, mesh=mesh, in_specs=in_specs, out_specs=out_specs, check_vma=False)
```

```python
import functools

import jax
import jax.numpy as jnp
from jax import lax
from jax.experimental import pallas as pl
from jax.experimental.pallas import tpu as pltpu
from jax.sharding import PartitionSpec as P

STEPS = 4
FIELDS = 3
SUBLANES = 8

nonlinear = 0.03
viscous = 0.02

f32 = jnp.float32
bf16 = jnp.bfloat16
VMEM = pl.BlockSpec(memory_space=pltpu.VMEM)
HBM = pl.BlockSpec(memory_space=pltpu.HBM)


def shift(count, by):
    return [(i, (i + by) % count) for i in range(count)]


def line(count, by):
    return [(i, i + by) for i in range(count) if 0 <= i + by < count]


def iota(shape, dim):
    return lax.broadcasted_iota(jnp.int32, shape, dim)


def dot(a, b, contract):
    return lax.dot_general(a, b, (((contract[0],), (contract[1],)), ((), ())), preferred_element_type=f32)


def call(kernel, out_shape, inputs, scratch=(), specs=None, out_specs=None, micros=1.0, vmem=32):
    return pl.pallas_call(
        kernel,
        out_shape=out_shape,
        in_specs=specs or [VMEM] * len(inputs),
        out_specs=out_specs or jax.tree.map(lambda _: VMEM, out_shape),
        scratch_shapes=list(scratch),
        cost_estimate=pl.CostEstimate(flops=int(micros * 1e9), bytes_accessed=0, transcendentals=0),
        compiler_params=pltpu.CompilerParams(vmem_limit_bytes=vmem * 1024 * 1024),
    )(*inputs)


def shape_of(dims, dtype):
    return jax.ShapeDtypeStruct(dims, dtype)


def fetch(pairs, sems):
    copies = [pltpu.make_async_copy(a, b, sems.at[i]) for i, (a, b) in enumerate(pairs)]
    for copy in copies:
        copy.start()
    return copies


def both_ways(axis, ahead, behind):
    count = lax.axis_size(axis)
    after = lax.ppermute(behind, axis, line(count, -1))
    before = lax.ppermute(ahead, axis, line(count, 1))
    return after, before


def pairs(count, first):
    swaps = []
    for i in range(first, count - 1, 2):
        swaps += [(i, i + 1), (i + 1, i)]
    return swaps


def route_kernel(buckets, lanes, rows, after_ref, owner_ref, cell_ref, count_ref, route_ref, place_ref):
    slots = owner_ref.shape[1]
    bucket = slots // buckets
    me = lax.axis_index("tile")
    owner = owner_ref[...]
    live = iota((1, slots), 1) < count_ref[...]
    held = -(-buckets // SUBLANES) * SUBLANES
    member = jnp.where((iota((held, slots), 0) == owner) & live, 1.0, 0.0)
    earlier = jnp.where(iota((slots, slots), 0) < iota((slots, slots), 1), 1.0, 0.0).astype(bf16)
    before = dot(member.astype(bf16), earlier, (1, 0))
    rank = jnp.sum(before * member, axis=0, keepdims=True).astype(jnp.int32)
    away = owner - me
    away = jnp.where(away < 0, away + buckets, away)
    target = jnp.where(live, away * bucket + rank, -1)
    route = jnp.where(iota((slots, slots), 0) == target, 1.0, 0.0).astype(bf16)
    route_ref[...] = route
    cell = cell_ref[...]
    row = jnp.where(iota((rows, slots), 0) == cell // lanes, 1.0, 0.0)
    lane = jnp.where(iota((lanes, slots), 0) == cell % lanes, 1.0, 0.0)
    place_ref[:, :rows] = dot(route, row.astype(bf16), (1, 1)).astype(bf16)
    place_ref[:, rows:] = dot(route, lane.astype(bf16), (1, 1)).astype(bf16)


def pack_sub_kernel(ends, fields, *outs):
    layers, rows, lanes = fields.shape[1:]
    low = iota((SUBLANES, lanes), 0) < STEPS
    for at in range(FIELDS):
        for pair in range(layers // 2):
            tiles = []
            for layer in (2 * pair, 2 * pair + 1):
                last = pltpu.roll(fields[at, layer, rows - SUBLANES :, :], STEPS, 0)
                first = fields[at, layer, :SUBLANES, :]
                tiles.append((last, first))
            picked = [jnp.where(low, a, pltpu.roll(b, STEPS, 0)) for a, b in zip(*tiles)]
            if ends == 1:
                picked = [jnp.where(lax.axis_index("sub") == 0, picked[0], picked[1])]
            for out, value in zip(outs, picked):
                out[at, pair * SUBLANES : (pair + 1) * SUBLANES, :] = value.astype(bf16)


def side_rows(at, base, k, after_ref, before_ref):
    start = base // 2 * SUBLANES + k // 2 * SUBLANES
    if not isinstance(start, int):
        start = pl.multiple_of(start, SUBLANES)
    after = after_ref[at, pl.ds(start, SUBLANES), :].astype(f32)
    before = before_ref[at, pl.ds(start, SUBLANES), :].astype(f32)
    if k % 2 == 0:
        before = pltpu.roll(before, STEPS, 0)
    else:
        after = pltpu.roll(after, STEPS, 0)
    me, count = lax.axis_index("sub"), lax.axis_size("sub")
    low = iota(after.shape, 0) < STEPS
    keep_after = jnp.where(me < count - 1, 1.0, 0.0)
    keep_before = jnp.where(me > 0, 1.0, 0.0)
    return jnp.where(low, after * keep_after, before * keep_before)


def pack_tile_kernel(fields, after_ref, before_ref, ready_ref, *outs):
    layers = fields.shape[1]
    odd = lax.axis_index("tile") % 2
    for out, base in zip(outs, ((1 - odd) * (layers - STEPS), odd * (layers - STEPS))):
        for at in range(FIELDS):
            for k in range(STEPS):
                out[at * STEPS + k] = fields[at, base + k].astype(bf16)
            for k in range(0, STEPS, 2):
                beside = [side_rows(at, base, k + i, after_ref, before_ref) for i in range(2)]
                out[FIELDS * STEPS + (at * STEPS + k) // 2] = jnp.concatenate(beside, 0).astype(bf16)


def sides(first, second, layers):
    odd = lax.axis_index("tile") % 2
    top = STEPS + layers
    return (first, (1 - odd) * top), (second, odd * top)


def end_lanes(lanes):
    row = iota((2 * STEPS, lanes), 0)
    wanted = jnp.where(row < STEPS, row, lanes - 2 * STEPS + row)
    return jnp.where(iota((2 * STEPS, lanes), 1) == wanted, 1.0, 0.0).astype(bf16)


def pack_rep_kernel(fields, sub_after, sub_before, tile_first, tile_second, out_ref, wide):
    layers, rows, lanes = fields.shape[1:]
    beside = 2 * STEPS
    total = layers + 2 * STEPS
    picks = end_lanes(lanes)
    for at in range(FIELDS):
        for side, base in sides(tile_first, tile_second, layers):
            start = pl.multiple_of(base * rows, STEPS * rows)
            wide[pl.ds(start, STEPS * rows), :] = side[at * STEPS : (at + 1) * STEPS].reshape(STEPS * rows, lanes)
            start = pl.multiple_of(total * rows + base * beside, STEPS * beside)
            packed = FIELDS * STEPS + at * STEPS // 2
            wide[pl.ds(start, STEPS * beside), :] = side[packed : packed + STEPS // 2].reshape(STEPS * beside, lanes)
        for k in range(layers):
            wide[(STEPS + k) * rows : (STEPS + k + 1) * rows, :] = fields[at, k].astype(bf16)
        for k in range(0, layers, 2):
            start = total * rows + (STEPS + k) * beside
            pair = [side_rows(at, 0, k + i, sub_after, sub_before) for i in range(2)]
            wide[start : start + 2 * beside, :] = jnp.concatenate(pair, 0).astype(bf16)
        width = wide.shape[0]
        out_ref[:, at * width : (at + 1) * width] = dot(picks, wide[...], (1, 1)).astype(bf16)


def window_kernel(
    fields, sub_after, sub_before, tile_first, tile_second, rep_after, rep_before, place_ref, states, *rest
):
    *sends, now, ago, coef, lapped, seen = rest
    layers, rows, lanes = fields.shape[1:]
    beside = 2 * STEPS
    total = layers + 2 * STEPS
    wide_rows, wide_lanes = rows + beside, 2 * lanes
    tile, tiles = lax.axis_index("tile"), lax.axis_size("tile")
    sub, subs = lax.axis_index("sub"), lax.axis_size("sub")
    rep, reps = lax.axis_index("rep"), lax.axis_size("rep")

    picks = end_lanes(lanes)
    width = total * wide_rows
    end = iota((2 * STEPS, width), 0) < STEPS
    keep_after = jnp.where(rep < reps - 1, 1.0, 0.0)
    keep_before = jnp.where(rep > 0, 1.0, 0.0)
    for at, out in enumerate((now, ago, coef)):
        for k in range(layers):
            out[STEPS + k, :rows, :lanes] = fields[at, k]
            out[STEPS + k, rows:, :lanes] = side_rows(at, 0, k, sub_after, sub_before)
        for side, base in sides(tile_first, tile_second, layers):
            for k in range(STEPS):
                out[base + k, :rows, :lanes] = side[at * STEPS + k].astype(f32)
                pair = side[FIELDS * STEPS + (at * STEPS + k) // 2].astype(f32)
                out[base + k, rows:, :lanes] = pair[k % 2 * beside : (k % 2 + 1) * beside]
        after = rep_after[:, at * width : (at + 1) * width].astype(f32) * keep_after
        before = rep_before[:, at * width : (at + 1) * width].astype(f32) * keep_before
        strip = dot(jnp.where(end, after, before).astype(bf16), picks, (0, 0))
        for k in range(total):
            out[k, :rows, lanes:] = strip[k * rows : (k + 1) * rows]
            out[k, rows:, lanes:] = strip[total * rows + k * beside : total * rows + (k + 1) * beside]

    row = iota((wide_rows, wide_lanes), 0)
    lane = iota((wide_rows, wide_lanes), 1)
    inside = (row < rows) | ((row < rows + STEPS) & (sub < subs - 1)) | ((row >= rows + STEPS) & (sub > 0))
    inside &= (lane < lanes) | ((lane < lanes + STEPS) & (rep < reps - 1)) | ((lane >= wide_lanes - STEPS) & (rep > 0))
    inside = jnp.where(inside, 1.0, 0.0)
    inside_low = inside * jnp.where(tile > 0, 1.0, 0.0)
    inside_high = inside * jnp.where(tile < tiles - 1, 1.0, 0.0)

    def laplace(below, here, above):
        summed = below + above
        summed = summed + pltpu.roll(here, 1, 0) + pltpu.roll(here, wide_rows - 1, 0)
        summed = summed + pltpu.roll(here, 1, 1) + pltpu.roll(here, wide_lanes - 1, 1)
        return summed - 6.0 * here

    for k in range(1, total - 1):
        lapped[k] = laplace(ago[k - 1], ago[k], ago[k + 1])
    for step in range(STEPS):
        below = now[step]
        here = now[step + 1]
        for k in range(step + 1, total - step - 1):
            above = now[k + 1]
            before = ago[k]
            lap = laplace(below, here, above)
            change = here - before
            driving = coef[k] * lap + viscous * (lap - lapped[k]) + 2.0 * nonlinear * change * change
            updated = 2.0 * here - before + (1.0 + 2.0 * nonlinear * here) * driving
            mask = inside_low if k < STEPS else inside_high if k >= STEPS + layers else inside
            updated = updated * mask
            now[k] = updated
            ago[k] = here
            lapped[k] = lap
            own = k - STEPS
            if 0 <= own < layers:
                core = updated[:rows, :lanes]
                seen[own * rows : (own + 1) * rows, step * lanes : (step + 1) * lanes] = core.astype(bf16)
                if step >= STEPS - 2:
                    states[STEPS - 1 - step, own] = core
            below, here = here, above

    cells = layers * rows
    steps_at = iota((SUBLANES, STEPS * lanes), 1) // lanes == iota((SUBLANES, STEPS * lanes), 0)
    steps_at = jnp.where(steps_at, 1.0, 0.0).astype(bf16)
    size = place_ref.shape[0] // len(sends)
    for at, send in enumerate(sends):
        part = place_ref[at * size : (at + 1) * size, :]
        found = dot(part[:, :cells], seen[...], (1, 0))
        lane_of = part[:, cells:].astype(f32)
        found = jnp.concatenate([found[:, i * lanes : (i + 1) * lanes] * lane_of for i in range(STEPS)], 1)
        send[...] = dot(steps_at, found.astype(bf16), (1, 1))[:STEPS].astype(bf16)


def store_kernel(states, final_hbm, prior_hbm, sems):
    for copy in fetch(((states.at[0], final_hbm), (states.at[1], prior_hbm)), sems):
        copy.wait()


def spread(at, size, total, bucket):
    wanted = iota((size, 1), 0) + at * size + lax.axis_index("tile") * bucket
    wanted = jnp.where(wanted >= total, wanted - total, wanted)
    return jnp.where(iota((size, total), 1) == wanted, 1.0, 0.0).astype(bf16)


def project_kernel(buckets, area_ref, shapes_ref, *rest):
    *parts, out_ref = rest
    total = area_ref.shape[1]
    size = parts[0].shape[1]
    loads = 0.0
    for at, part in enumerate(parts):
        loads = loads + dot(part[...], spread(at, size, total, total // buckets), (1, 0))
    weighted = (loads * area_ref[...]).astype(bf16)
    out_ref[...] = dot(weighted, shapes_ref[...], (1, 0))


def respond_kernel(buckets, addends, freq_ref, damp_ref, start_ref, shapes_ref, *rest):
    forces_in, rest = rest[:addends], rest[addends:]
    state_ref, *sends, accel = rest
    forces = forces_in[0][...]
    for ref in forces_in[1:]:
        forces = forces + ref[...].astype(f32)
    frequency, damping = freq_ref[...], damp_ref[...]
    drag, stiffness = 2.0 * damping * frequency, frequency * frequency
    displace, velocity = start_ref[0:1, :], start_ref[1:2, :]
    accel[...] = jnp.zeros_like(accel)
    for step in range(STEPS):
        acceleration = forces[step : step + 1, :] - drag * velocity - stiffness * displace
        velocity = velocity + acceleration
        displace = displace + velocity
        accel[step : step + 1, :] = acceleration
    state_ref[0:1, :] = displace
    state_ref[1:2, :] = velocity
    node = dot(accel[...].astype(bf16), shapes_ref[...], (1, 1)).astype(bf16)
    total = node.shape[1]
    size = total // len(sends)
    for at, send in enumerate(sends):
        send[...] = dot(node, spread(at, size, total, total // buckets), (1, 1))[:STEPS].astype(bf16)


def return_kernel(route_ref, *rest):
    *parts, out_ref = rest
    size = parts[0].shape[1]
    surface = 0.0
    for at, part in enumerate(parts):
        surface = surface + dot(part[...], route_ref[at * size : (at + 1) * size, :], (1, 0))
    out_ref[...] = surface.astype(bf16)


def exchange(parts, buckets):
    if len(parts) == buckets:
        return [parts[0]] + [lax.ppermute(parts[-k], "tile", shift(buckets, -k)) for k in range(1, buckets)]
    me = lax.axis_index("tile")
    (whole,) = parts
    steps, total = whole.shape
    stacked = whole.reshape(steps, buckets, total // buckets).transpose(1, 0, 2)
    stacked = lax.all_to_all(jnp.roll(stacked, me, 0), "tile", 0, 0, tiled=True)
    return [jnp.roll(stacked, -me, 0).transpose(1, 0, 2).reshape(steps, total)]


def body(
    pressure,
    previous_pressure,
    courant_square,
    node_area,
    mode_shapes,
    frequency,
    damping_ratio,
    modal_start,
    slot_cell,
    slot_owner,
    surface_count,
):
    buckets, subs, reps = (lax.axis_size(axis) for axis in ("tile", "sub", "rep"))
    layers, rows, lanes = pressure.shape
    slots = slot_cell.shape[-1]
    modes = mode_shapes.shape[1]
    bucket = slots // buckets
    parts = buckets if buckets <= 4 and bucket % 16 == 0 else 1
    total = layers + 2 * STEPS
    wide_rows = rows + 2 * STEPS

    ends = 1 if subs == 2 else 2
    slab = shape_of((FIELDS, layers * STEPS, lanes), bf16)
    fields = jnp.stack([pressure, previous_pressure, courant_square])
    packed = call(functools.partial(pack_sub_kernel, ends), (slab,) * ends, (fields,))
    if subs == 2:
        sub_halo = (lax.ppermute(packed[0], "sub", shift(2, 1)),) * 2
    else:
        sub_halo = both_ways("sub", *packed)

    cells = layers * rows
    route, place = call(
        functools.partial(route_kernel, buckets, lanes, cells),
        (shape_of((slots, slots), bf16), shape_of((slots, cells + lanes), bf16)),
        (packed[0], slot_owner.reshape(1, slots), slot_cell.reshape(1, slots), surface_count.reshape(1, 1)),
    )

    slab = shape_of((FIELDS * STEPS * 3 // 2, rows, lanes), bf16)
    packed = call(pack_tile_kernel, (slab, slab), (fields, *sub_halo, route))
    tile_halo = [lax.ppermute(value, "tile", pairs(buckets, i)) for i, value in enumerate(packed)]
    packed = call(
        pack_rep_kernel,
        shape_of((2 * STEPS, FIELDS * total * wide_rows), bf16),
        (fields, *sub_halo, *tile_halo),
        scratch=[pltpu.VMEM((total * wide_rows, lanes), bf16)],
    )
    if reps == 2:
        rep_halo = (lax.ppermute(packed, "rep", shift(2, 1)),) * 2
    else:
        rep_halo = both_ways("rep", packed, packed)

    wide = pltpu.VMEM((total, wide_rows, 2 * lanes), f32)
    part = shape_of((STEPS, slots // parts), bf16)
    block = shape_of(pressure.shape, f32)
    states, *sends = call(
        window_kernel,
        (shape_of((2, layers, rows, lanes), f32),) + (part,) * parts,
        (fields, *sub_halo, *tile_halo, *rep_halo, place),
        scratch=[wide] * 4 + [pltpu.VMEM((cells, STEPS * lanes), bf16)],
        micros=2.0,
    )
    final_field, prior_field = call(
        store_kernel, (block, block), (states,), out_specs=(HBM, HBM), scratch=[pltpu.SemaphoreType.DMA((2,))]
    )

    forces = call(
        functools.partial(project_kernel, buckets),
        shape_of((STEPS, modes), f32),
        (node_area.reshape(1, slots), mode_shapes, *exchange(sends, buckets)),
    )
    addends = [forces]
    for axis in ("rep", "sub", "tile"):
        count = lax.axis_size(axis)
        forces = functools.reduce(jnp.add, addends)
        if count <= 4:
            sent = forces.astype(bf16) if axis == "tile" else forces
            addends = [forces] + [lax.ppermute(sent, axis, shift(count, k)) for k in range(1, count)]
        else:
            addends = [lax.psum(forces, axis)]

    state, *sends = call(
        functools.partial(respond_kernel, buckets, len(addends)),
        (shape_of((2, modes), f32),) + (part,) * parts,
        (frequency.reshape(1, modes), damping_ratio.reshape(1, modes), modal_start, mode_shapes, *addends),
        scratch=[pltpu.VMEM((SUBLANES, modes), f32)],
    )
    share = modes // (buckets * subs * reps)
    modal_state = lax.dynamic_slice_in_dim(state, lax.axis_index(("tile", "sub", "rep")) * share, share, 1)
    surface = call(return_kernel, shape_of((STEPS, slots), bf16), (route, *exchange(sends, buckets)))
    return (final_field, prior_field, surface.reshape(1, 1, 1, STEPS, slots), modal_state)


def solution(mesh):
    in_specs = (
        P(("groups", "tile"), "sub", "rep"),
        P(("groups", "tile"), "sub", "rep"),
        P(("groups", "tile"), "sub", "rep"),
        P(("groups", "tile", "sub", "rep")),
        P(("groups", "tile", "sub", "rep"), None),
        P("groups"),
        P("groups"),
        P(None, "groups"),
        P(("groups", "tile"), "sub", "rep", None),
        P(("groups", "tile"), "sub", "rep", None, None),
        P(("groups", "sub"), "rep", "tile"),
    )
    out_specs = (
        P(("groups", "tile"), "sub", "rep"),
        P(("groups", "tile"), "sub", "rep"),
        P(("groups", "tile"), "sub", "rep", None, None),
        P(None, ("groups", "tile", "sub", "rep")),
    )
    return jax.shard_map(body, mesh=mesh, in_specs=in_specs, out_specs=out_specs, check_vma=False)
```

```python
import functools

import jax
import jax.numpy as jnp
from jax import lax
from jax.experimental import pallas as pl
from jax.experimental.pallas import tpu as pltpu
from jax.sharding import PartitionSpec as P

STEPS = 4
FIELDS = 3
SUBLANES = 8

nonlinear = 0.03
viscous = 0.02

f32 = jnp.float32
bf16 = jnp.bfloat16
VMEM = pl.BlockSpec(memory_space=pltpu.VMEM)
HBM = pl.BlockSpec(memory_space=pltpu.HBM)


def shift(count, by):
    return [(i, (i + by) % count) for i in range(count)]


def line(count, by):
    return [(i, i + by) for i in range(count) if 0 <= i + by < count]


def iota(shape, dim):
    return lax.broadcasted_iota(jnp.int32, shape, dim)


def dot(a, b, contract):
    return lax.dot_general(a, b, (((contract[0],), (contract[1],)), ((), ())), preferred_element_type=f32)


def call(kernel, out_shape, inputs, scratch=(), specs=None, out_specs=None, micros=1.0, vmem=32):
    return pl.pallas_call(
        kernel,
        out_shape=out_shape,
        in_specs=specs or [VMEM] * len(inputs),
        out_specs=out_specs or jax.tree.map(lambda _: VMEM, out_shape),
        scratch_shapes=list(scratch),
        cost_estimate=pl.CostEstimate(flops=int(micros * 1e9), bytes_accessed=0, transcendentals=0),
        compiler_params=pltpu.CompilerParams(vmem_limit_bytes=vmem * 1024 * 1024),
    )(*inputs)


def shape_of(dims, dtype):
    return jax.ShapeDtypeStruct(dims, dtype)


def fetch(pairs, sems):
    copies = [pltpu.make_async_copy(a, b, sems.at[i]) for i, (a, b) in enumerate(pairs)]
    for copy in copies:
        copy.start()
    return copies


def both_ways(axis, ahead, behind):
    count = lax.axis_size(axis)
    after = lax.ppermute(behind, axis, line(count, -1))
    before = lax.ppermute(ahead, axis, line(count, 1))
    return after, before


def route_kernel(buckets, lanes, rows, after_ref, owner_ref, cell_ref, count_ref, route_ref, place_ref):
    slots = owner_ref.shape[1]
    bucket = slots // buckets
    me = lax.axis_index("tile")
    owner = owner_ref[...]
    live = iota((1, slots), 1) < count_ref[...]
    held = -(-buckets // SUBLANES) * SUBLANES
    member = jnp.where((iota((held, slots), 0) == owner) & live, 1.0, 0.0)
    earlier = jnp.where(iota((slots, slots), 0) < iota((slots, slots), 1), 1.0, 0.0).astype(bf16)
    before = dot(member.astype(bf16), earlier, (1, 0))
    rank = jnp.sum(before * member, axis=0, keepdims=True).astype(jnp.int32)
    away = owner - me
    away = jnp.where(away < 0, away + buckets, away)
    target = jnp.where(live, away * bucket + rank, -1)
    route = jnp.where(iota((slots, slots), 0) == target, 1.0, 0.0).astype(bf16)
    route_ref[...] = route
    cell = cell_ref[...]
    row = jnp.where(iota((rows, slots), 0) == cell // lanes, 1.0, 0.0)
    lane = jnp.where(iota((lanes, slots), 0) == cell % lanes, 1.0, 0.0)
    place_ref[:, :rows] = dot(route, row.astype(bf16), (1, 1)).astype(bf16)
    place_ref[:, rows:] = dot(route, lane.astype(bf16), (1, 1)).astype(bf16)


def pack_sub_kernel(ends, fields, *outs):
    layers, rows, lanes = fields.shape[1:]
    low = iota((SUBLANES, lanes), 0) < STEPS
    for at in range(FIELDS):
        for pair in range(layers // 2):
            tiles = []
            for layer in (2 * pair, 2 * pair + 1):
                last = pltpu.roll(fields[at, layer, rows - SUBLANES :, :], STEPS, 0)
                first = fields[at, layer, :SUBLANES, :]
                tiles.append((last, first))
            picked = [jnp.where(low, a, pltpu.roll(b, STEPS, 0)) for a, b in zip(*tiles)]
            if ends == 1:
                picked = [jnp.where(lax.axis_index("sub") == 0, picked[0], picked[1])]
            for out, value in zip(outs, picked):
                out[at, pair * SUBLANES : (pair + 1) * SUBLANES, :] = value.astype(bf16)


def side_rows(at, base, k, after_ref, before_ref):
    start = base // 2 * SUBLANES + k // 2 * SUBLANES
    if not isinstance(start, int):
        start = pl.multiple_of(start, SUBLANES)
    after = after_ref[at, pl.ds(start, SUBLANES), :].astype(f32)
    before = before_ref[at, pl.ds(start, SUBLANES), :].astype(f32)
    if k % 2 == 0:
        before = pltpu.roll(before, STEPS, 0)
    else:
        after = pltpu.roll(after, STEPS, 0)
    me, count = lax.axis_index("sub"), lax.axis_size("sub")
    low = iota(after.shape, 0) < STEPS
    keep_after = jnp.where(me < count - 1, 1.0, 0.0)
    keep_before = jnp.where(me > 0, 1.0, 0.0)
    return jnp.where(low, after * keep_after, before * keep_before)


def pack_tile_kernel(fields, after_ref, before_ref, *outs):
    layers = fields.shape[1]
    for out, base in zip(outs, (layers - STEPS, 0)):
        for at in range(FIELDS):
            for k in range(STEPS):
                out[at * STEPS + k] = fields[at, base + k].astype(bf16)
            for k in range(0, STEPS, 2):
                beside = [side_rows(at, base, k + i, after_ref, before_ref) for i in range(2)]
                out[FIELDS * STEPS + (at * STEPS + k) // 2] = jnp.concatenate(beside, 0).astype(bf16)


def end_lanes(lanes):
    row = iota((2 * STEPS, lanes), 0)
    wanted = jnp.where(row < STEPS, row, lanes - 2 * STEPS + row)
    return jnp.where(iota((2 * STEPS, lanes), 1) == wanted, 1.0, 0.0).astype(bf16)


def pack_rep_kernel(fields, sub_after, sub_before, tile_before, tile_after, ready_ref, out_ref, wide):
    layers, rows, lanes = fields.shape[1:]
    beside = 2 * STEPS
    total = layers + 2 * STEPS
    picks = end_lanes(lanes)
    for at in range(FIELDS):
        for side, base in ((tile_before, 0), (tile_after, STEPS + layers)):
            start = base * rows
            wide[start : start + STEPS * rows, :] = side[at * STEPS : (at + 1) * STEPS].reshape(STEPS * rows, lanes)
            start = total * rows + base * beside
            packed = FIELDS * STEPS + at * STEPS // 2
            wide[start : start + STEPS * beside, :] = side[packed : packed + STEPS // 2].reshape(STEPS * beside, lanes)
        for k in range(layers):
            wide[(STEPS + k) * rows : (STEPS + k + 1) * rows, :] = fields[at, k].astype(bf16)
        for k in range(0, layers, 2):
            start = total * rows + (STEPS + k) * beside
            pair = [side_rows(at, 0, k + i, sub_after, sub_before) for i in range(2)]
            wide[start : start + 2 * beside, :] = jnp.concatenate(pair, 0).astype(bf16)
        width = wide.shape[0]
        out_ref[:, at * width : (at + 1) * width] = dot(picks, wide[...], (1, 1)).astype(bf16)


def window_kernel(
    fields, sub_after, sub_before, tile_before, tile_after, rep_after, rep_before, place_ref, states, *rest
):
    *sends, now, ago, coef, lapped, seen = rest
    layers, rows, lanes = fields.shape[1:]
    beside = 2 * STEPS
    total = layers + 2 * STEPS
    wide_rows, wide_lanes = rows + beside, 2 * lanes
    tile, tiles = lax.axis_index("tile"), lax.axis_size("tile")
    sub, subs = lax.axis_index("sub"), lax.axis_size("sub")
    rep, reps = lax.axis_index("rep"), lax.axis_size("rep")

    keep_low = jnp.where(tile > 0, 1.0, 0.0)
    keep_high = jnp.where(tile < tiles - 1, 1.0, 0.0)
    picks = end_lanes(lanes)
    width = total * wide_rows
    end = iota((2 * STEPS, width), 0) < STEPS
    keep_after = jnp.where(rep < reps - 1, 1.0, 0.0)
    keep_before = jnp.where(rep > 0, 1.0, 0.0)
    for at, out in enumerate((now, ago, coef)):
        for k in range(layers):
            out[STEPS + k, :rows, :lanes] = fields[at, k]
            out[STEPS + k, rows:, :lanes] = side_rows(at, 0, k, sub_after, sub_before)
        for side, base, keep in ((tile_before, 0, keep_low), (tile_after, STEPS + layers, keep_high)):
            for k in range(STEPS):
                out[base + k, :rows, :lanes] = side[at * STEPS + k].astype(f32) * keep
                pair = side[FIELDS * STEPS + (at * STEPS + k) // 2].astype(f32) * keep
                out[base + k, rows:, :lanes] = pair[k % 2 * beside : (k % 2 + 1) * beside]
        after = rep_after[:, at * width : (at + 1) * width].astype(f32) * keep_after
        before = rep_before[:, at * width : (at + 1) * width].astype(f32) * keep_before
        strip = dot(jnp.where(end, after, before).astype(bf16), picks, (0, 0))
        for k in range(total):
            keep = keep_low if k < STEPS else keep_high if k >= STEPS + layers else 1.0
            out[k, :rows, lanes:] = strip[k * rows : (k + 1) * rows] * keep
            out[k, rows:, lanes:] = strip[total * rows + k * beside : total * rows + (k + 1) * beside] * keep

    row = iota((wide_rows, wide_lanes), 0)
    lane = iota((wide_rows, wide_lanes), 1)
    inside = (row < rows) | ((row < rows + STEPS) & (sub < subs - 1)) | ((row >= rows + STEPS) & (sub > 0))
    inside &= (lane < lanes) | ((lane < lanes + STEPS) & (rep < reps - 1)) | ((lane >= wide_lanes - STEPS) & (rep > 0))
    inside = jnp.where(inside, 1.0, 0.0)
    inside_low, inside_high = inside * keep_low, inside * keep_high

    def laplace(below, here, above):
        summed = below + above
        summed = summed + pltpu.roll(here, 1, 0) + pltpu.roll(here, wide_rows - 1, 0)
        summed = summed + pltpu.roll(here, 1, 1) + pltpu.roll(here, wide_lanes - 1, 1)
        return summed - 6.0 * here

    for k in range(1, total - 1):
        lapped[k] = laplace(ago[k - 1], ago[k], ago[k + 1])
    for step in range(STEPS):
        below = now[step]
        here = now[step + 1]
        for k in range(step + 1, total - step - 1):
            above = now[k + 1]
            before = ago[k]
            lap = laplace(below, here, above)
            change = here - before
            driving = coef[k] * lap + viscous * (lap - lapped[k]) + 2.0 * nonlinear * change * change
            updated = 2.0 * here - before + (1.0 + 2.0 * nonlinear * here) * driving
            mask = inside_low if k < STEPS else inside_high if k >= STEPS + layers else inside
            updated = updated * mask
            now[k] = updated
            ago[k] = here
            lapped[k] = lap
            own = k - STEPS
            if 0 <= own < layers:
                core = updated[:rows, :lanes]
                seen[own * rows : (own + 1) * rows, step * lanes : (step + 1) * lanes] = core.astype(bf16)
                if step >= STEPS - 2:
                    states[STEPS - 1 - step, own] = core
            below, here = here, above

    cells = layers * rows
    steps_at = iota((SUBLANES, STEPS * lanes), 1) // lanes == iota((SUBLANES, STEPS * lanes), 0)
    steps_at = jnp.where(steps_at, 1.0, 0.0).astype(bf16)
    size = place_ref.shape[0] // len(sends)
    for at, send in enumerate(sends):
        part = place_ref[at * size : (at + 1) * size, :]
        found = dot(part[:, :cells], seen[...], (1, 0))
        lane_of = part[:, cells:].astype(f32)
        found = jnp.concatenate([found[:, i * lanes : (i + 1) * lanes] * lane_of for i in range(STEPS)], 1)
        send[...] = dot(steps_at, found.astype(bf16), (1, 1))[:STEPS].astype(bf16)


def store_kernel(states, final_hbm, prior_hbm, sems):
    for copy in fetch(((states.at[0], final_hbm), (states.at[1], prior_hbm)), sems):
        copy.wait()


def spread(at, size, total, bucket):
    wanted = iota((size, 1), 0) + at * size + lax.axis_index("tile") * bucket
    wanted = jnp.where(wanted >= total, wanted - total, wanted)
    return jnp.where(iota((size, total), 1) == wanted, 1.0, 0.0).astype(bf16)


def project_kernel(buckets, area_ref, shapes_ref, *rest):
    *parts, out_ref = rest
    total = area_ref.shape[1]
    size = parts[0].shape[1]
    loads = 0.0
    for at, part in enumerate(parts):
        loads = loads + dot(part[...], spread(at, size, total, total // buckets), (1, 0))
    weighted = (loads * area_ref[...]).astype(bf16)
    out_ref[...] = dot(weighted, shapes_ref[...], (1, 0))


def respond_kernel(buckets, addends, freq_ref, damp_ref, start_ref, shapes_ref, *rest):
    forces_in, rest = rest[:addends], rest[addends:]
    state_ref, *sends, accel = rest
    forces = forces_in[0][...]
    for ref in forces_in[1:]:
        forces = forces + ref[...].astype(f32)
    frequency, damping = freq_ref[...], damp_ref[...]
    drag, stiffness = 2.0 * damping * frequency, frequency * frequency
    displace, velocity = start_ref[0:1, :], start_ref[1:2, :]
    accel[...] = jnp.zeros_like(accel)
    for step in range(STEPS):
        acceleration = forces[step : step + 1, :] - drag * velocity - stiffness * displace
        velocity = velocity + acceleration
        displace = displace + velocity
        accel[step : step + 1, :] = acceleration
    state_ref[0:1, :] = displace
    state_ref[1:2, :] = velocity
    node = dot(accel[...].astype(bf16), shapes_ref[...], (1, 1)).astype(bf16)
    total = node.shape[1]
    size = total // len(sends)
    for at, send in enumerate(sends):
        send[...] = dot(node, spread(at, size, total, total // buckets), (1, 1))[:STEPS].astype(bf16)


def return_kernel(route_ref, *rest):
    *parts, out_ref = rest
    size = parts[0].shape[1]
    surface = 0.0
    for at, part in enumerate(parts):
        surface = surface + dot(part[...], route_ref[at * size : (at + 1) * size, :], (1, 0))
    out_ref[...] = surface.astype(bf16)


def exchange(parts, buckets):
    if len(parts) == buckets:
        return [parts[0]] + [lax.ppermute(parts[-k], "tile", shift(buckets, -k)) for k in range(1, buckets)]
    me = lax.axis_index("tile")
    (whole,) = parts
    steps, total = whole.shape
    stacked = whole.reshape(steps, buckets, total // buckets).transpose(1, 0, 2)
    stacked = lax.all_to_all(jnp.roll(stacked, me, 0), "tile", 0, 0, tiled=True)
    return [jnp.roll(stacked, -me, 0).transpose(1, 0, 2).reshape(steps, total)]


def body(
    pressure,
    previous_pressure,
    courant_square,
    node_area,
    mode_shapes,
    frequency,
    damping_ratio,
    modal_start,
    slot_cell,
    slot_owner,
    surface_count,
):
    buckets, subs, reps = (lax.axis_size(axis) for axis in ("tile", "sub", "rep"))
    layers, rows, lanes = pressure.shape
    slots = slot_cell.shape[-1]
    modes = mode_shapes.shape[1]
    bucket = slots // buckets
    parts = buckets if buckets <= 4 and bucket % 16 == 0 else 1
    total = layers + 2 * STEPS
    wide_rows = rows + 2 * STEPS

    ends = 1 if subs == 2 else 2
    slab = shape_of((FIELDS, layers * STEPS, lanes), bf16)
    fields = jnp.stack([pressure, previous_pressure, courant_square])
    packed = call(functools.partial(pack_sub_kernel, ends), (slab,) * ends, (fields,))
    if subs == 2:
        sub_halo = (lax.ppermute(packed[0], "sub", shift(2, 1)),) * 2
    else:
        sub_halo = both_ways("sub", *packed)

    cells = layers * rows
    slab = shape_of((FIELDS * STEPS * 3 // 2, rows, lanes), bf16)
    packed = call(pack_tile_kernel, (slab, slab), (fields, *sub_halo))
    route, place = call(
        functools.partial(route_kernel, buckets, lanes, cells),
        (shape_of((slots, slots), bf16), shape_of((slots, cells + lanes), bf16)),
        (packed[0], slot_owner.reshape(1, slots), slot_cell.reshape(1, slots), surface_count.reshape(1, 1)),
    )

    tile_halo = [lax.ppermute(value, "tile", shift(buckets, by)) for value, by in zip(packed, (1, -1))]
    packed = call(
        pack_rep_kernel,
        shape_of((2 * STEPS, FIELDS * total * wide_rows), bf16),
        (fields, *sub_halo, *tile_halo, route),
        scratch=[pltpu.VMEM((total * wide_rows, lanes), bf16)],
    )
    if reps == 2:
        rep_halo = (lax.ppermute(packed, "rep", shift(2, 1)),) * 2
    else:
        rep_halo = both_ways("rep", packed, packed)

    wide = pltpu.VMEM((total, wide_rows, 2 * lanes), f32)
    part = shape_of((STEPS, slots // parts), bf16)
    block = shape_of(pressure.shape, f32)
    states, *sends = call(
        window_kernel,
        (shape_of((2, layers, rows, lanes), f32),) + (part,) * parts,
        (fields, *sub_halo, *tile_halo, *rep_halo, place),
        scratch=[wide] * 4 + [pltpu.VMEM((cells, STEPS * lanes), bf16)],
        micros=2.0,
    )
    final_field, prior_field = call(
        store_kernel, (block, block), (states,), out_specs=(HBM, HBM), scratch=[pltpu.SemaphoreType.DMA((2,))]
    )

    forces = call(
        functools.partial(project_kernel, buckets),
        shape_of((STEPS, modes), f32),
        (node_area.reshape(1, slots), mode_shapes, *exchange(sends, buckets)),
    )
    addends = [forces]
    for axis in ("rep", "sub", "tile"):
        count = lax.axis_size(axis)
        forces = functools.reduce(jnp.add, addends)
        if count <= 4:
            sent = forces.astype(bf16) if axis == "tile" else forces
            addends = [forces] + [lax.ppermute(sent, axis, shift(count, k)) for k in range(1, count)]
        else:
            addends = [lax.psum(forces, axis)]

    state, *sends = call(
        functools.partial(respond_kernel, buckets, len(addends)),
        (shape_of((2, modes), f32),) + (part,) * parts,
        (frequency.reshape(1, modes), damping_ratio.reshape(1, modes), modal_start, mode_shapes, *addends),
        scratch=[pltpu.VMEM((SUBLANES, modes), f32)],
    )
    share = modes // (buckets * subs * reps)
    modal_state = lax.dynamic_slice_in_dim(state, lax.axis_index(("tile", "sub", "rep")) * share, share, 1)
    surface = call(return_kernel, shape_of((STEPS, slots), bf16), (route, *exchange(sends, buckets)))
    return (final_field, prior_field, surface.reshape(1, 1, 1, STEPS, slots), modal_state)


def solution(mesh):
    in_specs = (
        P(("groups", "tile"), "sub", "rep"),
        P(("groups", "tile"), "sub", "rep"),
        P(("groups", "tile"), "sub", "rep"),
        P(("groups", "tile", "sub", "rep")),
        P(("groups", "tile", "sub", "rep"), None),
        P("groups"),
        P("groups"),
        P(None, "groups"),
        P(("groups", "tile"), "sub", "rep", None),
        P(("groups", "tile"), "sub", "rep", None, None),
        P(("groups", "sub"), "rep", "tile"),
    )
    out_specs = (
        P(("groups", "tile"), "sub", "rep"),
        P(("groups", "tile"), "sub", "rep"),
        P(("groups", "tile"), "sub", "rep", None, None),
        P(None, ("groups", "tile", "sub", "rep")),
    )
    return jax.shard_map(body, mesh=mesh, in_specs=in_specs, out_specs=out_specs, check_vma=False)
```

```python
import functools

import jax
import jax.numpy as jnp
from jax import lax
from jax.experimental import pallas as pl
from jax.experimental.pallas import tpu as pltpu
from jax.sharding import PartitionSpec as P

STEPS = 4
FIELDS = 3
SUBLANES = 8

nonlinear = 0.03
viscous = 0.02

f32 = jnp.float32
bf16 = jnp.bfloat16
VMEM = pl.BlockSpec(memory_space=pltpu.VMEM)
HBM = pl.BlockSpec(memory_space=pltpu.HBM)


def shift(count, by):
    return [(i, (i + by) % count) for i in range(count)]


def line(count, by):
    return [(i, i + by) for i in range(count) if 0 <= i + by < count]


def swaps(count, by):
    return [(i, i ^ by) for i in range(count)]


def iota(shape, dim):
    return lax.broadcasted_iota(jnp.int32, shape, dim)


def dot(a, b, contract):
    return lax.dot_general(a, b, (((contract[0],), (contract[1],)), ((), ())), preferred_element_type=f32)


def call(kernel, out_shape, inputs, scratch=(), specs=None, out_specs=None, micros=1.0, vmem=32):
    return pl.pallas_call(
        kernel,
        out_shape=out_shape,
        in_specs=specs or [VMEM] * len(inputs),
        out_specs=out_specs or jax.tree.map(lambda _: VMEM, out_shape),
        scratch_shapes=list(scratch),
        cost_estimate=pl.CostEstimate(flops=int(micros * 1e9), bytes_accessed=0, transcendentals=0),
        compiler_params=pltpu.CompilerParams(vmem_limit_bytes=vmem * 1024 * 1024),
    )(*inputs)


def shape_of(dims, dtype):
    return jax.ShapeDtypeStruct(dims, dtype)


def fetch(pairs, sems):
    copies = [pltpu.make_async_copy(a, b, sems.at[i]) for i, (a, b) in enumerate(pairs)]
    for copy in copies:
        copy.start()
    return copies


def both_ways(axis, ahead, behind):
    count = lax.axis_size(axis)
    after = lax.ppermute(behind, axis, line(count, -1))
    before = lax.ppermute(ahead, axis, line(count, 1))
    return after, before


def route_kernel(buckets, lanes, rows, after_ref, owner_ref, cell_ref, count_ref, route_ref, place_ref):
    slots = owner_ref.shape[1]
    bucket = slots // buckets
    me = lax.axis_index("tile")
    owner = owner_ref[...]
    live = iota((1, slots), 1) < count_ref[...]
    held = -(-buckets // SUBLANES) * SUBLANES
    member = jnp.where((iota((held, slots), 0) == owner) & live, 1.0, 0.0)
    earlier = jnp.where(iota((slots, slots), 0) < iota((slots, slots), 1), 1.0, 0.0).astype(bf16)
    before = dot(member.astype(bf16), earlier, (1, 0))
    rank = jnp.sum(before * member, axis=0, keepdims=True).astype(jnp.int32)
    target = jnp.where(live, (owner ^ me) * bucket + rank, -1)
    route = jnp.where(iota((slots, slots), 0) == target, 1.0, 0.0).astype(bf16)
    route_ref[...] = route
    cell = cell_ref[...]
    row = jnp.where(iota((rows, slots), 0) == cell // lanes, 1.0, 0.0)
    lane = jnp.where(iota((lanes, slots), 0) == cell % lanes, 1.0, 0.0)
    place_ref[:, :rows] = dot(route, row.astype(bf16), (1, 1)).astype(bf16)
    place_ref[:, rows:] = dot(route, lane.astype(bf16), (1, 1)).astype(bf16)


def pack_sub_kernel(sides, fields, *outs):
    layers, rows, lanes = fields.shape[1:]
    low = iota((SUBLANES, lanes), 0) < STEPS
    for at in range(FIELDS):
        for pair in range(layers // 2):
            tiles = []
            for layer in (2 * pair, 2 * pair + 1):
                last = pltpu.roll(fields[at, layer, rows - SUBLANES :, :], STEPS, 0)
                first = fields[at, layer, :SUBLANES, :]
                tiles.append((last, first))
            picked = [jnp.where(low, a, pltpu.roll(b, STEPS, 0)) for a, b in zip(*tiles)]
            if sides == 1:
                picked = [jnp.where(lax.axis_index("sub") == 0, picked[0], picked[1])]
            for out, value in zip(outs, picked):
                out[at, pair * SUBLANES : (pair + 1) * SUBLANES, :] = value.astype(bf16)


def side_rows(at, base, k, after_ref, before_ref):
    start = base // 2 * SUBLANES + k // 2 * SUBLANES
    if not isinstance(start, int):
        start = pl.multiple_of(start, SUBLANES)
    after = after_ref[at, pl.ds(start, SUBLANES), :].astype(f32)
    before = before_ref[at, pl.ds(start, SUBLANES), :].astype(f32)
    if k % 2 == 0:
        before = pltpu.roll(before, STEPS, 0)
    else:
        after = pltpu.roll(after, STEPS, 0)
    me, count = lax.axis_index("sub"), lax.axis_size("sub")
    low = iota(after.shape, 0) < STEPS
    keep_after = jnp.where(me < count - 1, 1.0, 0.0)
    keep_before = jnp.where(me > 0, 1.0, 0.0)
    return jnp.where(low, after * keep_after, before * keep_before)


def pack_tile_kernel(fields, after_ref, before_ref, *outs):
    layers = fields.shape[1]
    for out, base in zip(outs, (layers - STEPS, 0)):
        for at in range(FIELDS):
            for k in range(STEPS):
                out[at * STEPS + k] = fields[at, base + k].astype(bf16)
            for k in range(0, STEPS, 2):
                beside = [side_rows(at, base, k + i, after_ref, before_ref) for i in range(2)]
                out[FIELDS * STEPS + (at * STEPS + k) // 2] = jnp.concatenate(beside, 0).astype(bf16)


def pack_rep_kernel(fields, sub_after, sub_before, tile_before, tile_after, ready_ref, out_ref, ends_ref):
    layers, rows, lanes = fields.shape[1:]
    beside = 2 * STEPS
    total = layers + 2 * STEPS
    layer_of = iota((rows + beside, lanes), 1) // beside
    for at in range(FIELDS):
        packed = jnp.zeros((rows + beside, lanes), f32)
        for k in range(total):
            own = k - STEPS
            if 0 <= own < layers:
                here = fields[at, own], side_rows(at, 0, own, sub_after, sub_before)
            else:
                side, depth = (tile_before, k) if k < STEPS else (tile_after, own - layers)
                pair = side[FIELDS * STEPS + (at * STEPS + depth) // 2].astype(f32)
                here = side[at * STEPS + depth].astype(f32), pair[depth % 2 * beside : (depth % 2 + 1) * beside]
            here = jnp.concatenate(here, 0)
            packed = jnp.where(layer_of == k, pltpu.roll(here, (beside * k + STEPS) % lanes, 1), packed)
        out_ref[at] = packed.astype(bf16)
        ends_ref[at] = packed


def across(value):
    return pltpu.roll(value, 1, 0) + pltpu.roll(value, value.shape[0] - 1, 0)


def beside_lanes(value):
    lanes = value.shape[1]
    lane = iota(value.shape, 1)
    left = jnp.where(lane == 0, 0.0, pltpu.roll(value, 1, 1))
    right = jnp.where(lane == lanes - 1, 0.0, pltpu.roll(value, lanes - 1, 1))
    return left + right


def laplace(below, here, above):
    return below + above + across(here) + beside_lanes(here) - 6.0 * here


def row_masks(layers, rows, lanes):
    tile, sub = lax.axis_index("tile"), lax.axis_index("sub")
    keep_low, keep_high = jnp.where(tile > 0, 1.0, 0.0), jnp.where(tile < lax.axis_size("tile") - 1, 1.0, 0.0)
    keep_before, keep_after = jnp.where(sub > 0, 1.0, 0.0), jnp.where(sub < lax.axis_size("sub") - 1, 1.0, 0.0)
    row = iota((rows + 2 * STEPS, lanes), 0)
    inside = jnp.where(row < rows, 1.0, jnp.where(row < rows + STEPS, keep_after, keep_before))
    return inside * keep_low, inside, inside * keep_high


def assemble_kernel(
    fields, sub_after, sub_before, tile_before, tile_after, ready_ref, now, ago, coef, lapped, lapped_ago
):
    layers, rows, lanes = fields.shape[1:]
    beside = 2 * STEPS
    total = layers + 2 * STEPS
    tile = lax.axis_index("tile")
    keep_low, keep_high = jnp.where(tile > 0, 1.0, 0.0), jnp.where(tile < lax.axis_size("tile") - 1, 1.0, 0.0)
    for at, out in enumerate((now, ago, coef)):
        extra = viscous if at == 2 else 0.0
        for k in range(layers):
            out[STEPS + k, :rows] = fields[at, k] + extra
            out[STEPS + k, rows:] = side_rows(at, 0, k, sub_after, sub_before) + extra
        for side, base, keep in ((tile_before, 0, keep_low), (tile_after, STEPS + layers, keep_high)):
            for k in range(STEPS):
                out[base + k, :rows] = side[at * STEPS + k].astype(f32) * keep + extra
                pair = side[FIELDS * STEPS + (at * STEPS + k) // 2].astype(f32) * keep
                out[base + k, rows:] = pair[k % 2 * beside : (k % 2 + 1) * beside] + extra
    for value, out in ((now, lapped), (ago, lapped_ago)):
        for k in range(1, total - 1):
            out[k] = laplace(value[k - 1], value[k], value[k + 1])


def window_kernel(
    now_in, ago_in, coef, lapped_in, lapped_ago_in, ends_ref, rep_after, rep_before, place_ref, states, *rest
):
    *sends, now, ago, lapped, seen = rest
    layers, rows, lanes = states.shape[1:]
    beside = 2 * STEPS
    total, wide_rows = now.shape[:2]
    rep, reps = lax.axis_index("rep"), lax.axis_size("rep")
    keep_left, keep_right = jnp.where(rep > 0, 1.0, 0.0), jnp.where(rep < reps - 1, 1.0, 0.0)
    inside_low, inside, inside_high = row_masks(layers, rows, lanes)

    lane = iota((wide_rows, lanes), 1)
    layer_of = lane // beside
    outer = lane % beside < STEPS
    ending = (lane == 0) | (lane == lanes - 1)
    inside_side = jnp.where(layer_of < STEPS, inside_low, jnp.where(layer_of < STEPS + layers, inside, inside_high))
    inside_side = jnp.where(layer_of < total, inside_side, 0.0)
    inside_left = inside_side * jnp.where(outer, keep_left, 1.0)
    inside_right = inside_side * jnp.where(outer, 1.0, keep_right)
    lefts, rights = [], []
    for at in range(FIELDS):
        extra = viscous if at == 2 else 0.0
        left = jnp.where(outer, rep_before[at].astype(f32), ends_ref[at])
        right = jnp.where(outer, ends_ref[at], rep_after[at].astype(f32))
        lefts.append(left * inside_left + extra)
        rights.append(right * inside_right + extra)
    left_now, left_ago, left_coef = lefts
    right_now, right_ago, right_coef = rights

    def edges(left, right):
        return jnp.where(outer, pltpu.roll(right, lanes - 1, 1), pltpu.roll(left, 1, 1))

    def edge_of(k, edge):
        return jnp.where(ending, pltpu.roll(edge, (lanes - beside * k - STEPS) % lanes, 1), 0.0)

    def laplace_side(side):
        beyond = pltpu.roll(side, beside, 1) + pltpu.roll(side, lanes - beside, 1)
        return beyond + across(side) + pltpu.roll(side, 1, 1) + pltpu.roll(side, lanes - 1, 1) - 6.0 * side

    def advance(here, before, gain, lap, lap_before, mask):
        change = here - before
        driving = gain * lap - lap_before + 2.0 * nonlinear * change * change
        return (here + change + (1.0 + 2.0 * nonlinear * here) * driving) * mask

    edge_ago = edges(left_ago, right_ago)
    left_lapped, right_lapped = viscous * laplace_side(left_ago), viscous * laplace_side(right_ago)

    cells = layers * rows
    slots = place_ref.shape[0]
    lane_of = place_ref[:, cells:].astype(f32)
    loads = jnp.zeros((SUBLANES, slots), f32)
    for step in range(STEPS):
        edge = edges(left_now, right_now)
        source = now_in if step == 0 else now
        below, here = source[step], source[step + 1]
        for k in range(step + 1, total - step - 1):
            above = source[k + 1]
            if step == 0:
                lap, before = lapped_in[k], ago_in[k]
                lap_before = viscous * (lapped_ago_in[k] + edge_of(k, edge_ago))
            else:
                lap, before, lap_before = laplace(below, here, above), ago[k], lapped[k]
            lap = lap + edge_of(k, edge)
            mask = inside_low if k < STEPS else inside_high if k >= STEPS + layers else inside
            updated = advance(here, before, coef[k], lap, lap_before, mask)
            now[k] = updated
            ago[k] = here
            lapped[k] = viscous * lap
            own = k - STEPS
            if 0 <= own < layers:
                core = updated[:rows]
                seen[own * rows : (own + 1) * rows, :] = core.astype(bf16)
                if step >= STEPS - 2:
                    states[STEPS - 1 - step, own] = core
            below, here = here, above
        if step < STEPS - 1:
            lap = laplace_side(left_now)
            updated = advance(left_now, left_ago, left_coef, lap, left_lapped, inside_left)
            left_now, left_ago, left_lapped = updated, left_now, viscous * lap
            lap = laplace_side(right_now)
            updated = advance(right_now, right_ago, right_coef, lap, right_lapped, inside_right)
            right_now, right_ago, right_lapped = updated, right_now, viscous * lap
        found = (dot(place_ref[:, :cells], seen[...], (1, 0)) * lane_of).astype(bf16)
        summed = dot(jnp.ones((SUBLANES, lanes), bf16), found, (1, 1))
        loads = jnp.where(iota((SUBLANES, slots), 0) == step, summed, loads)

    size = slots // len(sends)
    for at, send in enumerate(sends):
        send[...] = loads[:STEPS, at * size : (at + 1) * size].astype(bf16)


def store_kernel(states, final_hbm, prior_hbm, sems):
    for copy in fetch(((states.at[0], final_hbm), (states.at[1], prior_hbm)), sems):
        copy.wait()


def spread(at, size, total, bucket):
    entry = iota((size, 1), 0) + at * size
    part = at if size == bucket else entry // bucket
    wanted = entry + ((part ^ lax.axis_index("tile")) - part) * bucket
    return jnp.where(iota((size, total), 1) == wanted, 1.0, 0.0).astype(bf16)


def project_kernel(order, buckets, area_ref, shapes_ref, *rest):
    *parts, out_ref = rest
    total = area_ref.shape[1]
    size = parts[0].shape[1]
    loads = 0.0
    for at, part in zip(order, parts):
        loads = loads + dot(part[...], spread(at, size, total, total // buckets), (1, 0))
    weighted = (loads * area_ref[...]).astype(bf16)
    out_ref[...] = dot(weighted, shapes_ref[...], (1, 0))


def respond_kernel(buckets, addends, freq_ref, damp_ref, start_ref, shapes_ref, *rest):
    forces_in, rest = rest[:addends], rest[addends:]
    state_ref, *sends, accel = rest
    forces = forces_in[0][...]
    for ref in forces_in[1:]:
        forces = forces + ref[...].astype(f32)
    frequency, damping = freq_ref[...], damp_ref[...]
    drag, stiffness = 2.0 * damping * frequency, frequency * frequency
    displace, velocity = start_ref[0:1, :], start_ref[1:2, :]
    accel[...] = jnp.zeros_like(accel)
    for step in range(STEPS):
        acceleration = forces[step : step + 1, :] - drag * velocity - stiffness * displace
        velocity = velocity + acceleration
        displace = displace + velocity
        accel[step : step + 1, :] = acceleration
    state_ref[0:1, :] = displace
    state_ref[1:2, :] = velocity
    node = dot(accel[...].astype(bf16), shapes_ref[...], (1, 1)).astype(bf16)
    total = node.shape[1]
    size = total // len(sends)
    for at, send in enumerate(sends):
        send[...] = dot(node, spread(at, size, total, total // buckets), (1, 1))[:STEPS].astype(bf16)


def return_kernel(order, route_ref, *rest):
    *parts, out_ref = rest
    size = parts[0].shape[1]
    surface = 0.0
    for at, part in zip(order, parts):
        surface = surface + dot(part[...], route_ref[at * size : (at + 1) * size, :], (1, 0))
    out_ref[...] = surface.astype(bf16)


def exchange(parts, order):
    buckets = lax.axis_size("tile")
    if len(parts) == buckets:
        return [lax.ppermute(parts[k], "tile", swaps(buckets, k)) if k else parts[0] for k in order]
    tiles = jnp.arange(buckets) ^ lax.axis_index("tile")
    (whole,) = parts
    steps, total = whole.shape
    stacked = whole.reshape(steps, buckets, total // buckets).transpose(1, 0, 2)
    stacked = lax.all_to_all(stacked[tiles], "tile", 0, 0, tiled=True)
    return [stacked[tiles].transpose(1, 0, 2).reshape(steps, total)]


def body(
    pressure,
    previous_pressure,
    courant_square,
    node_area,
    mode_shapes,
    frequency,
    damping_ratio,
    modal_start,
    slot_cell,
    slot_owner,
    surface_count,
):
    buckets, subs, reps = (lax.axis_size(axis) for axis in ("tile", "sub", "rep"))
    layers, rows, lanes = pressure.shape
    slots = slot_cell.shape[-1]
    modes = mode_shapes.shape[1]
    bucket = slots // buckets
    parts = buckets if buckets in (2, 4) and bucket % 16 == 0 else 1
    total = layers + 2 * STEPS
    wide_rows = rows + 2 * STEPS

    sides = 1 if subs == 2 else 2
    slab = shape_of((FIELDS, layers * STEPS, lanes), bf16)
    fields = jnp.stack([pressure, previous_pressure, courant_square])
    packed = call(functools.partial(pack_sub_kernel, sides), (slab,) * sides, (fields,))
    if subs == 2:
        sub_halo = (lax.ppermute(packed[0], "sub", shift(2, 1)),) * 2
    else:
        sub_halo = both_ways("sub", *packed)

    cells = layers * rows
    slab = shape_of((FIELDS * STEPS * 3 // 2, rows, lanes), bf16)
    packed = call(pack_tile_kernel, (slab, slab), (fields, *sub_halo))
    route, place = call(
        functools.partial(route_kernel, buckets, lanes, cells),
        (shape_of((slots, slots), bf16), shape_of((slots, cells + lanes), bf16)),
        (packed[0], slot_owner.reshape(1, slots), slot_cell.reshape(1, slots), surface_count.reshape(1, 1)),
    )

    tile_halo = [lax.ppermute(value, "tile", shift(buckets, by)) for value, by in zip(packed, (1, -1))]
    packed, ends = call(
        pack_rep_kernel,
        (shape_of((FIELDS, wide_rows, lanes), bf16), shape_of((FIELDS, wide_rows, lanes), f32)),
        (fields, *sub_halo, *tile_halo, route),
    )
    if reps == 2:
        rep_halo = (lax.ppermute(packed, "rep", shift(2, 1)),) * 2
    else:
        rep_halo = both_ways("rep", packed, packed)

    wide = shape_of((total, wide_rows, lanes), f32)
    assembled = call(assemble_kernel, (wide,) * 5, (fields, *sub_halo, *tile_halo, packed))
    wide = pltpu.VMEM(wide.shape, f32)
    part = shape_of((STEPS, slots // parts), bf16)
    block = shape_of(pressure.shape, f32)
    states, *sends = call(
        window_kernel,
        (shape_of((2, layers, rows, lanes), f32),) + (part,) * parts,
        (*assembled, ends, *rep_halo, place),
        scratch=[wide] * 3 + [pltpu.VMEM((cells, lanes), bf16)],
        micros=2.0,
    )
    final_field, prior_field = call(
        store_kernel, (block, block), (states,), out_specs=(HBM, HBM), scratch=[pltpu.SemaphoreType.DMA((2,))]
    )

    order = [k for k in (0, 2, 3, 1) if k < parts]
    forces = call(
        functools.partial(project_kernel, order, buckets),
        shape_of((STEPS, modes), f32),
        (node_area.reshape(1, slots), mode_shapes, *exchange(sends, order)),
    )
    addends = [forces]
    for axis in ("rep", "sub", "tile"):
        count = lax.axis_size(axis)
        forces = functools.reduce(jnp.add, addends)
        if count in (2, 4):
            sent = forces.astype(bf16) if axis != "rep" else forces
            addends = [forces] + [lax.ppermute(sent, axis, swaps(count, k)) for k in (1, 3, 2) if k < count]
        else:
            addends = [lax.psum(forces, axis)]

    state, *sends = call(
        functools.partial(respond_kernel, buckets, len(addends)),
        (shape_of((2, modes), f32),) + (part,) * parts,
        (frequency.reshape(1, modes), damping_ratio.reshape(1, modes), modal_start, mode_shapes, *addends),
        scratch=[pltpu.VMEM((SUBLANES, modes), f32)],
    )
    share = modes // (buckets * subs * reps)
    modal_state = lax.dynamic_slice_in_dim(state, lax.axis_index(("tile", "sub", "rep")) * share, share, 1)
    order = [k for k in (0, 3, 2, 1) if k < parts]
    surface = call(
        functools.partial(return_kernel, order), shape_of((STEPS, slots), bf16), (route, *exchange(sends, order))
    )
    return (final_field, prior_field, surface.reshape(1, 1, 1, STEPS, slots), modal_state)


def solution(mesh):
    in_specs = (
        P(("groups", "tile"), "sub", "rep"),
        P(("groups", "tile"), "sub", "rep"),
        P(("groups", "tile"), "sub", "rep"),
        P(("groups", "tile", "sub", "rep")),
        P(("groups", "tile", "sub", "rep"), None),
        P("groups"),
        P("groups"),
        P(None, "groups"),
        P(("groups", "tile"), "sub", "rep", None),
        P(("groups", "tile"), "sub", "rep", None, None),
        P(("groups", "sub"), "rep", "tile"),
    )
    out_specs = (
        P(("groups", "tile"), "sub", "rep"),
        P(("groups", "tile"), "sub", "rep"),
        P(("groups", "tile"), "sub", "rep", None, None),
        P(None, ("groups", "tile", "sub", "rep")),
    )
    return jax.shard_map(body, mesh=mesh, in_specs=in_specs, out_specs=out_specs, check_vma=False)
```

```python
import functools

import jax
import jax.numpy as jnp
from jax import lax
from jax.experimental import pallas as pl
from jax.experimental.pallas import tpu as pltpu
from jax.sharding import PartitionSpec as P

STEPS = 4
FIELDS = 3
SUBLANES = 8

nonlinear = 0.03
viscous = 0.02

f32 = jnp.float32
bf16 = jnp.bfloat16
VMEM = pl.BlockSpec(memory_space=pltpu.VMEM)
HBM = pl.BlockSpec(memory_space=pltpu.HBM)


def shift(count, by):
    return [(i, (i + by) % count) for i in range(count)]


def line(count, by):
    return [(i, i + by) for i in range(count) if 0 <= i + by < count]


def swaps(count, by):
    return [(i, i ^ by) for i in range(count)]


def iota(shape, dim):
    return lax.broadcasted_iota(jnp.int32, shape, dim)


def dot(a, b, contract):
    return lax.dot_general(a, b, (((contract[0],), (contract[1],)), ((), ())), preferred_element_type=f32)


def call(kernel, out_shape, inputs, scratch=(), specs=None, out_specs=None, micros=1.0, vmem=32):
    return pl.pallas_call(
        kernel,
        out_shape=out_shape,
        in_specs=specs or [VMEM] * len(inputs),
        out_specs=out_specs or jax.tree.map(lambda _: VMEM, out_shape),
        scratch_shapes=list(scratch),
        cost_estimate=pl.CostEstimate(flops=int(micros * 1e9), bytes_accessed=0, transcendentals=0),
        compiler_params=pltpu.CompilerParams(vmem_limit_bytes=vmem * 1024 * 1024),
    )(*inputs)


def shape_of(dims, dtype):
    return jax.ShapeDtypeStruct(dims, dtype)


def fetch(pairs, sems):
    copies = [pltpu.make_async_copy(a, b, sems.at[i]) for i, (a, b) in enumerate(pairs)]
    for copy in copies:
        copy.start()
    return copies


def both_ways(axis, ahead, behind):
    count = lax.axis_size(axis)
    after = lax.ppermute(behind, axis, line(count, -1))
    before = lax.ppermute(ahead, axis, line(count, 1))
    return after, before


def route_kernel(buckets, lanes, rows, after_ref, owner_ref, cell_ref, count_ref, route_ref, place_ref):
    slots = owner_ref.shape[1]
    bucket = slots // buckets
    me = lax.axis_index("tile")
    owner = owner_ref[...]
    live = iota((1, slots), 1) < count_ref[...]
    held = -(-buckets // SUBLANES) * SUBLANES
    member = jnp.where((iota((held, slots), 0) == owner) & live, 1.0, 0.0)
    earlier = jnp.where(iota((slots, slots), 0) < iota((slots, slots), 1), 1.0, 0.0).astype(bf16)
    before = dot(member.astype(bf16), earlier, (1, 0))
    rank = jnp.sum(before * member, axis=0, keepdims=True).astype(jnp.int32)
    target = jnp.where(live, (owner ^ me) * bucket + rank, -1)
    route = jnp.where(iota((slots, slots), 0) == target, 1.0, 0.0).astype(bf16)
    route_ref[...] = route
    cell = cell_ref[...]
    row = jnp.where(iota((rows, slots), 0) == cell // lanes, 1.0, 0.0)
    lane = jnp.where(iota((lanes, slots), 0) == cell % lanes, 1.0, 0.0)
    place_ref[:rows] = dot(row.astype(bf16), route, (1, 1)).astype(bf16)
    place_ref[rows:] = dot(lane.astype(bf16), route, (1, 1)).astype(bf16)


def pack_tile_kernel(fields, ahead, behind):
    layers = fields.shape[1]
    for out, base, unused in ((ahead, layers - STEPS, 0), (behind, 0, STEPS - 1)):
        kept = [(at, k) for at in range(FIELDS) for k in range(STEPS) if at < 2 or k != unused]
        for entry, (at, k) in enumerate(kept):
            out[entry] = fields[at, base + k].astype(bf16)


def layer_of_block(at, k, fields, tile_before, tile_after):
    layers = fields.shape[1]
    if STEPS <= k < STEPS + layers:
        return fields[at, k - STEPS]
    side, depth, unused = (tile_before, k, 0) if k < STEPS else (tile_after, k - STEPS - layers, STEPS - 1)
    if at == 2 and depth == unused:
        return jnp.zeros(fields.shape[2:], f32)
    return side[at * STEPS + depth - (at == 2 and unused == 0)].astype(f32)


def pack_sub_kernel(sides, fields, tile_before, tile_after, ready_ref, *outs):
    layers, rows, lanes = fields.shape[1:]
    low = iota((SUBLANES, lanes), 0) < STEPS
    for at in range(FIELDS):
        for pair in range(layers // 2 + STEPS):
            tiles = []
            for layer in (2 * pair, 2 * pair + 1):
                here = layer_of_block(at, layer, fields, tile_before, tile_after)
                tiles.append((pltpu.roll(here[rows - SUBLANES :], STEPS, 0), here[:SUBLANES]))
            picked = [jnp.where(low, a, pltpu.roll(b, STEPS, 0)) for a, b in zip(*tiles)]
            if sides == 1:
                picked = [jnp.where(lax.axis_index("sub") == 0, picked[0], picked[1])]
            for out, value in zip(outs, picked):
                out[at, pair * SUBLANES : (pair + 1) * SUBLANES, :] = value.astype(bf16)


def side_rows(at, k, after_ref, before_ref):
    start = k // 2 * SUBLANES
    after = after_ref[at, start : start + SUBLANES, :].astype(f32)
    before = before_ref[at, start : start + SUBLANES, :].astype(f32)
    if k % 2 == 0:
        before = pltpu.roll(before, STEPS, 0)
    else:
        after = pltpu.roll(after, STEPS, 0)
    me, count = lax.axis_index("sub"), lax.axis_size("sub")
    low = iota(after.shape, 0) < STEPS
    keep_after = jnp.where(me < count - 1, 1.0, 0.0)
    keep_before = jnp.where(me > 0, 1.0, 0.0)
    return jnp.where(low, after * keep_after, before * keep_before)


def pack_rep_kernel(fields, tile_before, tile_after, sub_after, sub_before, ready_ref, out_ref, ends_ref):
    layers, rows, lanes = fields.shape[1:]
    beside = 2 * STEPS
    total = layers + 2 * STEPS
    layer_at = iota((rows + beside, lanes), 1) // beside
    for at in range(FIELDS):
        packed = jnp.zeros((rows + beside, lanes), f32)
        for k in range(total):
            here = layer_of_block(at, k, fields, tile_before, tile_after), side_rows(at, k, sub_after, sub_before)
            here = pltpu.roll(jnp.concatenate(here, 0), (beside * k + STEPS) % lanes, 1)
            packed = jnp.where(layer_at == k, here, packed)
        out_ref[at] = packed.astype(bf16)
        ends_ref[at] = packed


def across(value):
    return pltpu.roll(value, 1, 0) + pltpu.roll(value, value.shape[0] - 1, 0)


def beside_lanes(value):
    lanes = value.shape[1]
    lane = iota(value.shape, 1)
    left = jnp.where(lane == 0, 0.0, pltpu.roll(value, 1, 1))
    right = jnp.where(lane == lanes - 1, 0.0, pltpu.roll(value, lanes - 1, 1))
    return left + right


def laplace(below, here, above):
    return below + above + across(here) + beside_lanes(here) - 6.0 * here


def row_masks(layers, rows, lanes):
    tile, sub = lax.axis_index("tile"), lax.axis_index("sub")
    keep_low, keep_high = jnp.where(tile > 0, 1.0, 0.0), jnp.where(tile < lax.axis_size("tile") - 1, 1.0, 0.0)
    keep_before, keep_after = jnp.where(sub > 0, 1.0, 0.0), jnp.where(sub < lax.axis_size("sub") - 1, 1.0, 0.0)
    row = iota((rows + 2 * STEPS, lanes), 0)
    inside = jnp.where(row < rows, 1.0, jnp.where(row < rows + STEPS, keep_after, keep_before))
    return inside * keep_low, inside, inside * keep_high


def assemble_kernel(
    fields, tile_before, tile_after, sub_after, sub_before, ready_ref, now, ago, coef, lapped, lapped_ago
):
    layers, rows, lanes = fields.shape[1:]
    total = layers + 2 * STEPS
    tile = lax.axis_index("tile")
    keep_low, keep_high = jnp.where(tile > 0, 1.0, 0.0), jnp.where(tile < lax.axis_size("tile") - 1, 1.0, 0.0)
    for at, out in enumerate((now, ago, coef)):
        extra = viscous if at == 2 else 0.0
        for k in range(total):
            keep = keep_low if k < STEPS else keep_high if k >= STEPS + layers else 1.0
            out[k, :rows] = layer_of_block(at, k, fields, tile_before, tile_after) * keep + extra
            out[k, rows:] = side_rows(at, k, sub_after, sub_before) * keep + extra
    for value, out in ((now, lapped), (ago, lapped_ago)):
        for k in range(1, total - 1):
            out[k] = laplace(value[k - 1], value[k], value[k + 1])


def window_kernel(
    now_in, ago_in, coef, lapped_in, lapped_ago_in, ends_ref, rep_after, rep_before, place_ref, states, *rest
):
    *sends, now, ago, lapped = rest
    layers, rows, lanes = states.shape[1:]
    beside = 2 * STEPS
    total, wide_rows = now.shape[:2]
    rep, reps = lax.axis_index("rep"), lax.axis_size("rep")
    keep_left, keep_right = jnp.where(rep > 0, 1.0, 0.0), jnp.where(rep < reps - 1, 1.0, 0.0)
    inside_low, inside, inside_high = row_masks(layers, rows, lanes)

    lane = iota((wide_rows, lanes), 1)
    layer_of = lane // beside
    outer = lane % beside < STEPS
    ending = (lane == 0) | (lane == lanes - 1)
    inside_side = jnp.where(layer_of < STEPS, inside_low, jnp.where(layer_of < STEPS + layers, inside, inside_high))
    inside_side = jnp.where(layer_of < total, inside_side, 0.0)
    inside_left = inside_side * jnp.where(outer, keep_left, 1.0)
    inside_right = inside_side * jnp.where(outer, 1.0, keep_right)
    lefts, rights = [], []
    for at in range(FIELDS):
        extra = viscous if at == 2 else 0.0
        left = jnp.where(outer, rep_before[at].astype(f32), ends_ref[at])
        right = jnp.where(outer, ends_ref[at], rep_after[at].astype(f32))
        lefts.append(left * inside_left + extra)
        rights.append(right * inside_right + extra)
    left_now, left_ago, left_coef = lefts
    right_now, right_ago, right_coef = rights

    def edges(left, right):
        return jnp.where(outer, pltpu.roll(right, lanes - 1, 1), pltpu.roll(left, 1, 1))

    def edge_of(k, edge):
        return jnp.where(ending, pltpu.roll(edge, (lanes - beside * k - STEPS) % lanes, 1), 0.0)

    def laplace_side(side):
        beyond = pltpu.roll(side, beside, 1) + pltpu.roll(side, lanes - beside, 1)
        return beyond + across(side) + pltpu.roll(side, 1, 1) + pltpu.roll(side, lanes - 1, 1) - 6.0 * side

    def advance(here, before, gain, lap, lap_before, mask):
        change = here - before
        driving = gain * lap - lap_before + 2.0 * nonlinear * change * change
        return (here + change + (1.0 + 2.0 * nonlinear * here) * driving) * mask

    edge_ago = edges(left_ago, right_ago)
    left_lapped, right_lapped = viscous * laplace_side(left_ago), viscous * laplace_side(right_ago)

    cells = layers * rows
    slots = place_ref.shape[1]
    lane_of = place_ref[cells:]
    loads = jnp.zeros((SUBLANES, slots), f32)
    for step in range(STEPS):
        edge = edges(left_now, right_now)
        found = jnp.zeros((rows, slots), f32)
        source = now_in if step == 0 else now
        below, here = source[step], source[step + 1]
        for k in range(step + 1, total - step - 1):
            above = source[k + 1]
            if step == 0:
                lap, before = lapped_in[k], ago_in[k]
                lap_before = viscous * (lapped_ago_in[k] + edge_of(k, edge_ago))
            else:
                lap, before, lap_before = laplace(below, here, above), ago[k], lapped[k]
            lap = lap + edge_of(k, edge)
            mask = inside_low if k < STEPS else inside_high if k >= STEPS + layers else inside
            updated = advance(here, before, coef[k], lap, lap_before, mask)
            now[k] = updated
            ago[k] = here
            lapped[k] = viscous * lap
            own = k - STEPS
            if 0 <= own < layers:
                core = updated[:rows]
                row_of = place_ref[own * rows : (own + 1) * rows].astype(f32)
                found = found + dot(core.astype(bf16), lane_of, (1, 0)) * row_of
                if step >= STEPS - 2:
                    states[STEPS - 1 - step, own] = core
            below, here = here, above
        if step < STEPS - 1:
            lap = laplace_side(left_now)
            updated = advance(left_now, left_ago, left_coef, lap, left_lapped, inside_left)
            left_now, left_ago, left_lapped = updated, left_now, viscous * lap
            lap = laplace_side(right_now)
            updated = advance(right_now, right_ago, right_coef, lap, right_lapped, inside_right)
            right_now, right_ago, right_lapped = updated, right_now, viscous * lap
        loads = jnp.where(iota((SUBLANES, slots), 0) == step, jnp.sum(found, axis=0, keepdims=True), loads)

    size = slots // len(sends)
    for at, send in enumerate(sends):
        send[...] = loads[:STEPS, at * size : (at + 1) * size].astype(bf16)


def store_kernel(states, final_hbm, prior_hbm, sems):
    for copy in fetch(((states.at[0], final_hbm), (states.at[1], prior_hbm)), sems):
        copy.wait()


def turn_kernel(buckets, ready_ref, shapes_ref, area_ref, turned_ref, flipped_ref, area_out):
    total = shapes_ref.shape[0]
    bucket = total // buckets
    entry = iota((total, 1), 0)
    part = entry // bucket
    wanted = entry + ((part ^ lax.axis_index("tile")) - part) * bucket
    picks = jnp.where(iota((total, total), 1) == wanted, 1.0, 0.0)
    turned = dot(picks.astype(bf16), shapes_ref[...], (1, 0))
    turned_ref[...] = turned.astype(bf16)
    flipped_ref[...] = turned.T.astype(bf16)
    area_out[...] = lax.dot_general(
        area_ref[...], picks, (((1,), (1,)), ((), ())), precision=lax.Precision.HIGHEST, preferred_element_type=f32
    )


def project_kernel(order, area_ref, turned_ref, *rest):
    *parts, out_ref = rest
    size = parts[0].shape[1]
    forces = 0.0
    for at, part in zip(order, parts):
        weighted = (part[...].astype(f32) * area_ref[:, at * size : (at + 1) * size]).astype(bf16)
        forces = forces + dot(weighted, turned_ref[at * size : (at + 1) * size, :], (1, 0))
    out_ref[...] = forces


def respond_kernel(addends, freq_ref, damp_ref, start_ref, flipped_ref, *rest):
    forces_in, rest = rest[:addends], rest[addends:]
    state_ref, *sends, accel = rest
    forces = forces_in[0][...]
    for ref in forces_in[1:]:
        forces = forces + ref[...].astype(f32)
    frequency, damping = freq_ref[...], damp_ref[...]
    drag, stiffness = 2.0 * damping * frequency, frequency * frequency
    displace, velocity = start_ref[0:1, :], start_ref[1:2, :]
    accel[...] = jnp.zeros_like(accel)
    for step in range(STEPS):
        acceleration = forces[step : step + 1, :] - drag * velocity - stiffness * displace
        velocity = velocity + acceleration
        displace = displace + velocity
        accel[step : step + 1, :] = acceleration
    state_ref[0:1, :] = displace
    state_ref[1:2, :] = velocity
    node = dot(accel[...].astype(bf16), flipped_ref[...], (1, 0))
    size = node.shape[1] // len(sends)
    for at, send in enumerate(sends):
        send[...] = node[:STEPS, at * size : (at + 1) * size].astype(bf16)


def return_kernel(order, route_ref, *rest):
    *parts, out_ref = rest
    size = parts[0].shape[1]
    surface = 0.0
    for at, part in zip(order, parts):
        surface = surface + dot(part[...], route_ref[at * size : (at + 1) * size, :], (1, 0))
    out_ref[...] = surface.astype(bf16)


def exchange(parts, order):
    buckets = lax.axis_size("tile")
    if len(parts) == buckets:
        return [lax.ppermute(parts[k], "tile", swaps(buckets, k)) if k else parts[0] for k in order]
    tiles = jnp.arange(buckets) ^ lax.axis_index("tile")
    (whole,) = parts
    steps, total = whole.shape
    stacked = whole.reshape(steps, buckets, total // buckets).transpose(1, 0, 2)
    stacked = lax.all_to_all(stacked[tiles], "tile", 0, 0, tiled=True)
    return [stacked[tiles].transpose(1, 0, 2).reshape(steps, total)]


def body(
    pressure,
    previous_pressure,
    courant_square,
    node_area,
    mode_shapes,
    frequency,
    damping_ratio,
    modal_start,
    slot_cell,
    slot_owner,
    surface_count,
):
    buckets, subs, reps = (lax.axis_size(axis) for axis in ("tile", "sub", "rep"))
    layers, rows, lanes = pressure.shape
    slots = slot_cell.shape[-1]
    modes = mode_shapes.shape[1]
    bucket = slots // buckets
    parts = buckets if buckets in (2, 4) and bucket % 16 == 0 else 1
    total = layers + 2 * STEPS
    wide_rows = rows + 2 * STEPS

    cells = layers * rows
    fields = jnp.stack([pressure, previous_pressure, courant_square])
    slab = shape_of((FIELDS * STEPS - 1, rows, lanes), bf16)
    packed = call(pack_tile_kernel, (slab, slab), (fields,))
    route, place = call(
        functools.partial(route_kernel, buckets, lanes, cells),
        (shape_of((slots, slots), bf16), shape_of((cells + lanes, slots), bf16)),
        (packed[0], slot_owner.reshape(1, slots), slot_cell.reshape(1, slots), surface_count.reshape(1, 1)),
    )
    tile_halo = [lax.ppermute(value, "tile", shift(buckets, by)) for value, by in zip(packed, (1, -1))]

    sides = 1 if subs == 2 else 2
    slab = shape_of((FIELDS, total * STEPS, lanes), bf16)
    packed = call(functools.partial(pack_sub_kernel, sides), (slab,) * sides, (fields, *tile_halo, route))
    if subs == 2:
        sub_halo = (lax.ppermute(packed[0], "sub", shift(2, 1)),) * 2
    else:
        sub_halo = both_ways("sub", *packed)

    turned, flipped, area = call(
        functools.partial(turn_kernel, buckets),
        (shape_of(mode_shapes.shape, bf16), shape_of(mode_shapes.shape[::-1], bf16), shape_of((1, slots), f32)),
        (packed[0], mode_shapes, node_area.reshape(1, slots)),
    )

    packed, ends = call(
        pack_rep_kernel,
        (shape_of((FIELDS, wide_rows, lanes), bf16), shape_of((FIELDS, wide_rows, lanes), f32)),
        (fields, *tile_halo, *sub_halo, area),
    )
    if reps == 2:
        rep_halo = (lax.ppermute(packed, "rep", shift(2, 1)),) * 2
    else:
        rep_halo = both_ways("rep", packed, packed)

    wide = shape_of((total, wide_rows, lanes), f32)
    assembled = call(assemble_kernel, (wide,) * 5, (fields, *tile_halo, *sub_halo, packed))
    wide = pltpu.VMEM(wide.shape, f32)
    part = shape_of((STEPS, slots // parts), bf16)
    block = shape_of(pressure.shape, f32)
    states, *sends = call(
        window_kernel,
        (shape_of((2, layers, rows, lanes), f32),) + (part,) * parts,
        (*assembled, ends, *rep_halo, place),
        scratch=[wide] * 3,
        micros=2.0,
    )
    final_field, prior_field = call(
        store_kernel, (block, block), (states,), out_specs=(HBM, HBM), scratch=[pltpu.SemaphoreType.DMA((2,))]
    )

    order = [k for k in (0, 2, 3, 1) if k < parts]
    forces = call(
        functools.partial(project_kernel, order),
        shape_of((STEPS, modes), f32),
        (area, turned, *exchange(sends, order)),
    )
    addends = [forces]
    for axis in ("rep", "sub", "tile"):
        count = lax.axis_size(axis)
        forces = functools.reduce(jnp.add, addends)
        if count in (2, 4):
            sent = forces.astype(bf16) if axis != "rep" else forces
            addends = [forces] + [lax.ppermute(sent, axis, swaps(count, k)) for k in (1, 3, 2) if k < count]
        else:
            addends = [lax.psum(forces, axis)]

    state, *sends = call(
        functools.partial(respond_kernel, len(addends)),
        (shape_of((2, modes), f32),) + (part,) * parts,
        (frequency.reshape(1, modes), damping_ratio.reshape(1, modes), modal_start, flipped, *addends),
        scratch=[pltpu.VMEM((SUBLANES, modes), f32)],
    )
    share = modes // (buckets * subs * reps)
    modal_state = lax.dynamic_slice_in_dim(state, lax.axis_index(("tile", "sub", "rep")) * share, share, 1)
    order = [k for k in (0, 3, 2, 1) if k < parts]
    surface = call(
        functools.partial(return_kernel, order), shape_of((STEPS, slots), bf16), (route, *exchange(sends, order))
    )
    return (final_field, prior_field, surface.reshape(1, 1, 1, STEPS, slots), modal_state)


def solution(mesh):
    in_specs = (
        P(("groups", "tile"), "sub", "rep"),
        P(("groups", "tile"), "sub", "rep"),
        P(("groups", "tile"), "sub", "rep"),
        P(("groups", "tile", "sub", "rep")),
        P(("groups", "tile", "sub", "rep"), None),
        P("groups"),
        P("groups"),
        P(None, "groups"),
        P(("groups", "tile"), "sub", "rep", None),
        P(("groups", "tile"), "sub", "rep", None, None),
        P(("groups", "sub"), "rep", "tile"),
    )
    out_specs = (
        P(("groups", "tile"), "sub", "rep"),
        P(("groups", "tile"), "sub", "rep"),
        P(("groups", "tile"), "sub", "rep", None, None),
        P(None, ("groups", "tile", "sub", "rep")),
    )
    return jax.shard_map(body, mesh=mesh, in_specs=in_specs, out_specs=out_specs, check_vma=False)
```

```python
import functools

import jax
import jax.numpy as jnp
from jax import lax
from jax.experimental import pallas as pl
from jax.experimental.pallas import tpu as pltpu
from jax.sharding import PartitionSpec as P

STEPS = 4
FIELDS = 3
SUBLANES = 8

nonlinear = 0.03
viscous = 0.02

f32 = jnp.float32
bf16 = jnp.bfloat16
VMEM = pl.BlockSpec(memory_space=pltpu.VMEM)
HBM = pl.BlockSpec(memory_space=pltpu.HBM)


def shift(count, by):
    return [(i, (i + by) % count) for i in range(count)]


def line(count, by):
    return [(i, i + by) for i in range(count) if 0 <= i + by < count]


def swaps(count, by):
    return [(i, i ^ by) for i in range(count)]


def iota(shape, dim):
    return lax.broadcasted_iota(jnp.int32, shape, dim)


def dot(a, b, contract):
    return lax.dot_general(a, b, (((contract[0],), (contract[1],)), ((), ())), preferred_element_type=f32)


def call(kernel, out_shape, inputs, scratch=(), specs=None, out_specs=None, micros=1.0, vmem=32):
    return pl.pallas_call(
        kernel,
        out_shape=out_shape,
        in_specs=specs or [VMEM] * len(inputs),
        out_specs=out_specs or jax.tree.map(lambda _: VMEM, out_shape),
        scratch_shapes=list(scratch),
        cost_estimate=pl.CostEstimate(flops=int(micros * 1e9), bytes_accessed=0, transcendentals=0),
        compiler_params=pltpu.CompilerParams(vmem_limit_bytes=vmem * 1024 * 1024),
    )(*inputs)


def shape_of(dims, dtype):
    return jax.ShapeDtypeStruct(dims, dtype)


def fetch(pairs, sems):
    copies = [pltpu.make_async_copy(a, b, sems.at[i]) for i, (a, b) in enumerate(pairs)]
    for copy in copies:
        copy.start()
    return copies


def both_ways(axis, ahead, behind):
    count = lax.axis_size(axis)
    after = lax.ppermute(behind, axis, line(count, -1))
    before = lax.ppermute(ahead, axis, line(count, 1))
    return after, before


def route_kernel(buckets, lanes, rows, after_ref, owner_ref, cell_ref, count_ref, route_ref, place_ref):
    slots = owner_ref.shape[1]
    bucket = slots // buckets
    me = lax.axis_index("tile")
    owner = owner_ref[...]
    live = iota((1, slots), 1) < count_ref[...]
    held = -(-buckets // SUBLANES) * SUBLANES
    member = jnp.where((iota((held, slots), 0) == owner) & live, 1.0, 0.0)
    earlier = jnp.where(iota((slots, slots), 0) < iota((slots, slots), 1), 1.0, 0.0).astype(bf16)
    before = dot(member.astype(bf16), earlier, (1, 0))
    rank = jnp.sum(before * member, axis=0, keepdims=True).astype(jnp.int32)
    target = jnp.where(live, (owner ^ me) * bucket + rank, -1)
    route = jnp.where(iota((slots, slots), 0) == target, 1.0, 0.0).astype(bf16)
    route_ref[...] = route
    cell = cell_ref[...]
    row = jnp.where(iota((rows, slots), 0) == cell // lanes, 1.0, 0.0)
    lane = jnp.where(iota((lanes, slots), 0) == cell % lanes, 1.0, 0.0)
    place_ref[:rows] = dot(row.astype(bf16), route, (1, 1)).astype(bf16)
    place_ref[rows:] = dot(lane.astype(bf16), route, (1, 1)).astype(bf16)


def pack_tile_kernel(fields, ahead, behind):
    layers = fields.shape[1]
    for out, base, unused in ((ahead, layers - STEPS, 0), (behind, 0, STEPS - 1)):
        kept = [(at, k) for at in range(FIELDS) for k in range(STEPS) if at < 2 or k != unused]
        for entry, (at, k) in enumerate(kept):
            out[entry] = fields[at, base + k].astype(bf16)


def layer_of_block(at, k, fields, tile_before, tile_after):
    layers = fields.shape[1]
    if STEPS <= k < STEPS + layers:
        return fields[at, k - STEPS]
    side, depth, unused = (tile_before, k, 0) if k < STEPS else (tile_after, k - STEPS - layers, STEPS - 1)
    if at == 2 and depth == unused:
        return jnp.zeros(fields.shape[2:], f32)
    return side[at * STEPS + depth - (at == 2 and unused == 0)].astype(f32)


def pack_sub_kernel(sides, fields, tile_before, tile_after, ready_ref, *outs):
    layers, rows, lanes = fields.shape[1:]
    low = iota((SUBLANES, lanes), 0) < STEPS
    for at in range(FIELDS):
        for pair in range(layers // 2 + STEPS):
            tiles = []
            for layer in (2 * pair, 2 * pair + 1):
                here = layer_of_block(at, layer, fields, tile_before, tile_after)
                tiles.append((pltpu.roll(here[rows - SUBLANES :], STEPS, 0), here[:SUBLANES]))
            picked = [jnp.where(low, a, pltpu.roll(b, STEPS, 0)) for a, b in zip(*tiles)]
            if sides == 1:
                picked = [jnp.where(lax.axis_index("sub") == 0, picked[0], picked[1])]
            for out, value in zip(outs, picked):
                out[at, pair * SUBLANES : (pair + 1) * SUBLANES, :] = value.astype(bf16)


def side_rows(at, k, after_ref, before_ref):
    start = k // 2 * SUBLANES
    after = after_ref[at, start : start + SUBLANES, :].astype(f32)
    before = before_ref[at, start : start + SUBLANES, :].astype(f32)
    if k % 2 == 0:
        before = pltpu.roll(before, STEPS, 0)
    else:
        after = pltpu.roll(after, STEPS, 0)
    me, count = lax.axis_index("sub"), lax.axis_size("sub")
    low = iota(after.shape, 0) < STEPS
    keep_after = jnp.where(me < count - 1, 1.0, 0.0)
    keep_before = jnp.where(me > 0, 1.0, 0.0)
    return jnp.where(low, after * keep_after, before * keep_before)


def pack_rep_kernel(fields, tile_before, tile_after, sub_after, sub_before, ready_ref, out_ref, ends_ref):
    layers, rows, lanes = fields.shape[1:]
    beside = 2 * STEPS
    total = layers + 2 * STEPS
    layer_at = iota((rows + beside, lanes), 1) // beside
    for at in range(FIELDS):
        packed = jnp.zeros((rows + beside, lanes), f32)
        for k in range(total):
            here = layer_of_block(at, k, fields, tile_before, tile_after), side_rows(at, k, sub_after, sub_before)
            here = pltpu.roll(jnp.concatenate(here, 0), (beside * k + STEPS) % lanes, 1)
            packed = jnp.where(layer_at == k, here, packed)
        out_ref[at] = packed.astype(bf16)
        ends_ref[at] = packed


def across(value):
    return pltpu.roll(value, 1, 0) + pltpu.roll(value, value.shape[0] - 1, 0)


def beside_lanes(value):
    lanes = value.shape[1]
    lane = iota(value.shape, 1)
    left = jnp.where(lane == 0, 0.0, pltpu.roll(value, 1, 1))
    right = jnp.where(lane == lanes - 1, 0.0, pltpu.roll(value, lanes - 1, 1))
    return left + right


def laplace(below, here, above):
    return below + above + across(here) + beside_lanes(here) - 6.0 * here


def row_masks(layers, rows, lanes):
    tile, sub = lax.axis_index("tile"), lax.axis_index("sub")
    keep_low, keep_high = jnp.where(tile > 0, 1.0, 0.0), jnp.where(tile < lax.axis_size("tile") - 1, 1.0, 0.0)
    keep_before, keep_after = jnp.where(sub > 0, 1.0, 0.0), jnp.where(sub < lax.axis_size("sub") - 1, 1.0, 0.0)
    row = iota((rows + 2 * STEPS, lanes), 0)
    inside = jnp.where(row < rows, 1.0, jnp.where(row < rows + STEPS, keep_after, keep_before))
    return inside * keep_low, inside, inside * keep_high


def assemble_kernel(
    fields, tile_before, tile_after, sub_after, sub_before, ready_ref, now, ago, coef, lapped, lapped_ago
):
    layers, rows, lanes = fields.shape[1:]
    total = layers + 2 * STEPS
    tile = lax.axis_index("tile")
    keep_low, keep_high = jnp.where(tile > 0, 1.0, 0.0), jnp.where(tile < lax.axis_size("tile") - 1, 1.0, 0.0)
    for at, out in enumerate((now, ago, coef)):
        extra = viscous if at == 2 else 0.0
        for k in range(total):
            keep = keep_low if k < STEPS else keep_high if k >= STEPS + layers else 1.0
            out[k, :rows] = layer_of_block(at, k, fields, tile_before, tile_after) * keep + extra
            out[k, rows:] = side_rows(at, k, sub_after, sub_before) * keep + extra
    for value, out in ((now, lapped), (ago, lapped_ago)):
        for k in range(1, total - 1):
            out[k] = laplace(value[k - 1], value[k], value[k + 1])


def window_kernel(
    now_in, ago_in, coef, lapped_in, lapped_ago_in, ends_ref, rep_after, rep_before, place_ref, states, *rest
):
    *sends, now, ago, lapped = rest
    layers, rows, lanes = states.shape[1:]
    beside = 2 * STEPS
    total, wide_rows = now.shape[:2]
    rep, reps = lax.axis_index("rep"), lax.axis_size("rep")
    keep_left, keep_right = jnp.where(rep > 0, 1.0, 0.0), jnp.where(rep < reps - 1, 1.0, 0.0)
    inside_low, inside, inside_high = row_masks(layers, rows, lanes)

    lane = iota((wide_rows, lanes), 1)
    layer_of = lane // beside
    outer = lane % beside < STEPS
    ending = (lane == 0) | (lane == lanes - 1)
    inside_side = jnp.where(layer_of < STEPS, inside_low, jnp.where(layer_of < STEPS + layers, inside, inside_high))
    inside_side = jnp.where(layer_of < total, inside_side, 0.0)
    inside_left = inside_side * jnp.where(outer, keep_left, 1.0)
    inside_right = inside_side * jnp.where(outer, 1.0, keep_right)
    lefts, rights = [], []
    for at in range(FIELDS):
        extra = viscous if at == 2 else 0.0
        left = jnp.where(outer, rep_before[at].astype(f32), ends_ref[at])
        right = jnp.where(outer, ends_ref[at], rep_after[at].astype(f32))
        lefts.append(left * inside_left + extra)
        rights.append(right * inside_right + extra)
    left_now, left_ago, left_coef = lefts
    right_now, right_ago, right_coef = rights

    def edges(left, right):
        return jnp.where(outer, pltpu.roll(right, lanes - 1, 1), pltpu.roll(left, 1, 1))

    def edge_of(k, edge):
        return jnp.where(ending, pltpu.roll(edge, (lanes - beside * k - STEPS) % lanes, 1), 0.0)

    def laplace_side(side):
        beyond = pltpu.roll(side, beside, 1) + pltpu.roll(side, lanes - beside, 1)
        return beyond + across(side) + pltpu.roll(side, 1, 1) + pltpu.roll(side, lanes - 1, 1) - 6.0 * side

    def advance(here, before, gain, lap, lap_before, mask):
        change = here - before
        driving = gain * lap - lap_before + 2.0 * nonlinear * change * change
        return (here + change + (1.0 + 2.0 * nonlinear * here) * driving) * mask

    edge_ago = edges(left_ago, right_ago)
    left_lapped, right_lapped = viscous * laplace_side(left_ago), viscous * laplace_side(right_ago)

    cells = layers * rows
    slots = place_ref.shape[1]
    lane_of = place_ref[cells:]
    loads = jnp.zeros((SUBLANES, slots), f32)
    for step in range(STEPS):
        edge = edges(left_now, right_now)
        found = jnp.zeros((rows, slots), f32)
        source = now_in if step == 0 else now
        below, here = source[step], source[step + 1]
        for k in range(step + 1, total - step - 1):
            above = source[k + 1]
            if step == 0:
                lap, before = lapped_in[k], ago_in[k]
                lap_before = viscous * (lapped_ago_in[k] + edge_of(k, edge_ago))
            else:
                lap, before, lap_before = laplace(below, here, above), ago[k], lapped[k]
            lap = lap + edge_of(k, edge)
            mask = inside_low if k < STEPS else inside_high if k >= STEPS + layers else inside
            updated = advance(here, before, coef[k], lap, lap_before, mask)
            now[k] = updated
            ago[k] = here
            lapped[k] = viscous * lap
            own = k - STEPS
            if 0 <= own < layers:
                core = updated[:rows]
                row_of = place_ref[own * rows : (own + 1) * rows].astype(f32)
                found = found + dot(core.astype(bf16), lane_of, (1, 0)) * row_of
                if step >= STEPS - 2:
                    states[STEPS - 1 - step, own] = core
            below, here = here, above
        if step < STEPS - 1:
            lap = laplace_side(left_now)
            updated = advance(left_now, left_ago, left_coef, lap, left_lapped, inside_left)
            left_now, left_ago, left_lapped = updated, left_now, viscous * lap
            lap = laplace_side(right_now)
            updated = advance(right_now, right_ago, right_coef, lap, right_lapped, inside_right)
            right_now, right_ago, right_lapped = updated, right_now, viscous * lap
        loads = jnp.where(iota((SUBLANES, slots), 0) == step, jnp.sum(found, axis=0, keepdims=True), loads)

    size = slots // len(sends)
    for at, send in enumerate(sends):
        send[...] = loads[:STEPS, at * size : (at + 1) * size].astype(bf16)


def store_kernel(states, final_hbm, prior_hbm, sems):
    for copy in fetch(((states.at[0], final_hbm), (states.at[1], prior_hbm)), sems):
        copy.wait()


def turn_kernel(buckets, ready_ref, shapes_ref, area_ref, turned_ref, flipped_ref, area_out):
    total = shapes_ref.shape[0]
    bucket = total // buckets
    entry = iota((total, 1), 0)
    part = entry // bucket
    wanted = entry + ((part ^ lax.axis_index("tile")) - part) * bucket
    picks = jnp.where(iota((total, total), 1) == wanted, 1.0, 0.0)
    turned = dot(picks.astype(bf16), shapes_ref[...], (1, 0))
    turned_ref[...] = turned.astype(bf16)
    flipped_ref[...] = turned.T.astype(bf16)
    area_out[...] = lax.dot_general(
        area_ref[...], picks, (((1,), (1,)), ((), ())), precision=lax.Precision.HIGHEST, preferred_element_type=f32
    )


def project_kernel(order, area_ref, turned_ref, *rest):
    *parts, out_ref = rest
    size = parts[0].shape[1]
    forces = 0.0
    for at, part in zip(order, parts):
        weighted = (part[...].astype(f32) * area_ref[:, at * size : (at + 1) * size]).astype(bf16)
        forces = forces + dot(weighted, turned_ref[at * size : (at + 1) * size, :], (1, 0))
    out_ref[...] = forces


def respond_kernel(addends, freq_ref, damp_ref, start_ref, flipped_ref, *rest):
    forces_in, rest = rest[:addends], rest[addends:]
    state_ref, *sends, accel = rest
    forces = forces_in[0][...]
    for ref in forces_in[1:]:
        forces = forces + ref[...].astype(f32)
    frequency, damping = freq_ref[...], damp_ref[...]
    drag, stiffness = 2.0 * damping * frequency, frequency * frequency
    displace, velocity = start_ref[0:1, :], start_ref[1:2, :]
    accel[...] = jnp.zeros_like(accel)
    for step in range(STEPS):
        acceleration = forces[step : step + 1, :] - drag * velocity - stiffness * displace
        velocity = velocity + acceleration
        displace = displace + velocity
        accel[step : step + 1, :] = acceleration
    state_ref[0:1, :] = displace
    state_ref[1:2, :] = velocity
    node = dot(accel[...].astype(bf16), flipped_ref[...], (1, 0))
    size = node.shape[1] // len(sends)
    for at, send in enumerate(sends):
        send[...] = node[:STEPS, at * size : (at + 1) * size].astype(bf16)


def return_kernel(order, route_ref, *rest):
    *parts, out_ref = rest
    size = parts[0].shape[1]
    surface = 0.0
    for at, part in zip(order, parts):
        surface = surface + dot(part[...], route_ref[at * size : (at + 1) * size, :], (1, 0))
    out_ref[...] = surface.astype(bf16)


def crossed_swap(value, axis, by):
    count = lax.axis_size(axis)
    places = [(2 * i + r, 2 * (i ^ by) + 1 - r) for i in range(count) for r in range(2)]
    return lax.ppermute(value, (axis, "rep"), places)


def exchange(parts, order, crossed):
    buckets = lax.axis_size("tile")
    if crossed:
        return [crossed_swap(parts[k], "tile", k) if k else lax.ppermute(parts[0], "rep", swaps(2, 1)) for k in order]
    if len(parts) == buckets:
        return [lax.ppermute(parts[k], "tile", swaps(buckets, k)) if k else parts[0] for k in order]
    tiles = jnp.arange(buckets) ^ lax.axis_index("tile")
    (whole,) = parts
    steps, total = whole.shape
    stacked = whole.reshape(steps, buckets, total // buckets).transpose(1, 0, 2)
    stacked = lax.all_to_all(stacked[tiles], "tile", 0, 0, tiled=True)
    return [stacked[tiles].transpose(1, 0, 2).reshape(steps, total)]


def body(
    pressure,
    previous_pressure,
    courant_square,
    node_area,
    mode_shapes,
    frequency,
    damping_ratio,
    modal_start,
    slot_cell,
    slot_owner,
    surface_count,
):
    buckets, subs, reps = (lax.axis_size(axis) for axis in ("tile", "sub", "rep"))
    layers, rows, lanes = pressure.shape
    slots = slot_cell.shape[-1]
    modes = mode_shapes.shape[1]
    bucket = slots // buckets
    parts = buckets if buckets in (2, 4) and bucket % 16 == 0 else 1
    total = layers + 2 * STEPS
    wide_rows = rows + 2 * STEPS
    crossed = parts > 1 and reps == 2
    if crossed:
        mode_shapes, node_area = (lax.ppermute(value, "rep", swaps(2, 1)) for value in (mode_shapes, node_area))

    cells = layers * rows
    fields = jnp.stack([pressure, previous_pressure, courant_square])
    slab = shape_of((FIELDS * STEPS - 1, rows, lanes), bf16)
    packed = call(pack_tile_kernel, (slab, slab), (fields,))
    route, place = call(
        functools.partial(route_kernel, buckets, lanes, cells),
        (shape_of((slots, slots), bf16), shape_of((cells + lanes, slots), bf16)),
        (packed[0], slot_owner.reshape(1, slots), slot_cell.reshape(1, slots), surface_count.reshape(1, 1)),
    )
    tile_halo = [lax.ppermute(value, "tile", shift(buckets, by)) for value, by in zip(packed, (1, -1))]

    sides = 1 if subs == 2 else 2
    slab = shape_of((FIELDS, total * STEPS, lanes), bf16)
    packed = call(functools.partial(pack_sub_kernel, sides), (slab,) * sides, (fields, *tile_halo, route))
    if subs == 2:
        sub_halo = (lax.ppermute(packed[0], "sub", shift(2, 1)),) * 2
    else:
        sub_halo = both_ways("sub", *packed)

    turned, flipped, area = call(
        functools.partial(turn_kernel, buckets),
        (shape_of(mode_shapes.shape, bf16), shape_of(mode_shapes.shape[::-1], bf16), shape_of((1, slots), f32)),
        (packed[0], mode_shapes, node_area.reshape(1, slots)),
    )

    packed, ends = call(
        pack_rep_kernel,
        (shape_of((FIELDS, wide_rows, lanes), bf16), shape_of((FIELDS, wide_rows, lanes), f32)),
        (fields, *tile_halo, *sub_halo, area),
    )
    if reps == 2:
        rep_halo = (lax.ppermute(packed, "rep", shift(2, 1)),) * 2
    else:
        rep_halo = both_ways("rep", packed, packed)

    wide = shape_of((total, wide_rows, lanes), f32)
    assembled = call(assemble_kernel, (wide,) * 5, (fields, *tile_halo, *sub_halo, packed))
    wide = pltpu.VMEM(wide.shape, f32)
    part = shape_of((STEPS, slots // parts), bf16)
    block = shape_of(pressure.shape, f32)
    states, *sends = call(
        window_kernel,
        (shape_of((2, layers, rows, lanes), f32),) + (part,) * parts,
        (*assembled, ends, *rep_halo, place),
        scratch=[wide] * 3,
        micros=2.0,
    )
    final_field, prior_field = call(
        store_kernel, (block, block), (states,), out_specs=(HBM, HBM), scratch=[pltpu.SemaphoreType.DMA((2,))]
    )

    order = [k for k in (2, 3, 1, 0) if k < parts]
    forces = call(
        functools.partial(project_kernel, order),
        shape_of((STEPS, modes), f32),
        (area, turned, *exchange(sends, order, crossed)),
    )
    addends = [forces]
    for axis in ("rep", "sub", "tile"):
        count = lax.axis_size(axis)
        forces = functools.reduce(jnp.add, addends)
        if count in (2, 4):
            sent = forces.astype(bf16) if axis != "rep" else forces
            if axis != "rep" and reps == 2:
                addends = [forces] + [crossed_swap(sent, axis, k) for k in (1, 3, 2) if k < count]
            else:
                addends = [forces] + [lax.ppermute(sent, axis, swaps(count, k)) for k in (1, 3, 2) if k < count]
        else:
            addends = [lax.psum(forces, axis)]

    state, *sends = call(
        functools.partial(respond_kernel, len(addends)),
        (shape_of((2, modes), f32),) + (part,) * parts,
        (frequency.reshape(1, modes), damping_ratio.reshape(1, modes), modal_start, flipped, *addends),
        scratch=[pltpu.VMEM((SUBLANES, modes), f32)],
    )
    share = modes // (buckets * subs * reps)
    modal_state = lax.dynamic_slice_in_dim(state, lax.axis_index(("tile", "sub", "rep")) * share, share, 1)
    order = [k for k in (3, 2, 1, 0) if k < parts]
    surface = call(
        functools.partial(return_kernel, order), shape_of((STEPS, slots), bf16), (route, *exchange(sends, order, crossed))
    )
    return (final_field, prior_field, surface.reshape(1, 1, 1, STEPS, slots), modal_state)


def solution(mesh):
    in_specs = (
        P(("groups", "tile"), "sub", "rep"),
        P(("groups", "tile"), "sub", "rep"),
        P(("groups", "tile"), "sub", "rep"),
        P(("groups", "tile", "sub", "rep")),
        P(("groups", "tile", "sub", "rep"), None),
        P("groups"),
        P("groups"),
        P(None, "groups"),
        P(("groups", "tile"), "sub", "rep", None),
        P(("groups", "tile"), "sub", "rep", None, None),
        P(("groups", "sub"), "rep", "tile"),
    )
    out_specs = (
        P(("groups", "tile"), "sub", "rep"),
        P(("groups", "tile"), "sub", "rep"),
        P(("groups", "tile"), "sub", "rep", None, None),
        P(None, ("groups", "tile", "sub", "rep")),
    )
    return jax.shard_map(body, mesh=mesh, in_specs=in_specs, out_specs=out_specs, check_vma=False)
```

```python
import functools

import jax
import jax.numpy as jnp
from jax import lax
from jax.experimental import pallas as pl
from jax.experimental.pallas import tpu as pltpu
from jax.sharding import PartitionSpec as P

STEPS = 4
FIELDS = 3
SUBLANES = 8

nonlinear = 0.03
viscous = 0.02

f32 = jnp.float32
bf16 = jnp.bfloat16
VMEM = pl.BlockSpec(memory_space=pltpu.VMEM)
HBM = pl.BlockSpec(memory_space=pltpu.HBM)


def shift(count, by):
    return [(i, (i + by) % count) for i in range(count)]


def line(count, by):
    return [(i, i + by) for i in range(count) if 0 <= i + by < count]


def swaps(count, by):
    return [(i, i ^ by) for i in range(count)]


def iota(shape, dim):
    return lax.broadcasted_iota(jnp.int32, shape, dim)


def dot(a, b, contract):
    return lax.dot_general(a, b, (((contract[0],), (contract[1],)), ((), ())), preferred_element_type=f32)


def call(kernel, out_shape, inputs, scratch=(), specs=None, out_specs=None, micros=1.0, vmem=32):
    return pl.pallas_call(
        kernel,
        out_shape=out_shape,
        in_specs=specs or [VMEM] * len(inputs),
        out_specs=out_specs or jax.tree.map(lambda _: VMEM, out_shape),
        scratch_shapes=list(scratch),
        cost_estimate=pl.CostEstimate(flops=int(micros * 1e9), bytes_accessed=0, transcendentals=0),
        compiler_params=pltpu.CompilerParams(vmem_limit_bytes=vmem * 1024 * 1024),
    )(*inputs)


def shape_of(dims, dtype):
    return jax.ShapeDtypeStruct(dims, dtype)


def fetch(pairs, sems):
    copies = [pltpu.make_async_copy(a, b, sems.at[i]) for i, (a, b) in enumerate(pairs)]
    for copy in copies:
        copy.start()
    return copies


def send(value, axis, places, crossed):
    if not crossed:
        return lax.ppermute(value, axis, places)
    return lax.ppermute(value, (axis, "rep"), [(2 * i + r, 2 * j + 1 - r) for i, j in places for r in range(2)])


def both_ways(axis, ahead, behind, crossed=False):
    count = lax.axis_size(axis)
    after = send(behind, axis, line(count, -1), crossed)
    before = send(ahead, axis, line(count, 1), crossed)
    return after, before


def route_kernel(buckets, lanes, rows, after_ref, owner_ref, cell_ref, count_ref, route_ref, place_ref):
    slots = owner_ref.shape[1]
    bucket = slots // buckets
    me = lax.axis_index("tile")
    owner = owner_ref[...]
    live = iota((1, slots), 1) < count_ref[...]
    held = -(-buckets // SUBLANES) * SUBLANES
    member = jnp.where((iota((held, slots), 0) == owner) & live, 1.0, 0.0)
    earlier = jnp.where(iota((slots, slots), 0) < iota((slots, slots), 1), 1.0, 0.0).astype(bf16)
    before = dot(member.astype(bf16), earlier, (1, 0))
    rank = jnp.sum(before * member, axis=0, keepdims=True).astype(jnp.int32)
    target = jnp.where(live, (owner ^ me) * bucket + rank, -1)
    route = jnp.where(iota((slots, slots), 0) == target, 1.0, 0.0).astype(bf16)
    route_ref[...] = route
    cell = cell_ref[...]
    row = jnp.where(iota((rows, slots), 0) == cell // lanes, 1.0, 0.0)
    lane = jnp.where(iota((lanes, slots), 0) == cell % lanes, 1.0, 0.0)
    place_ref[:rows] = dot(row.astype(bf16), route, (1, 1)).astype(bf16)
    place_ref[rows:] = dot(lane.astype(bf16), route, (1, 1)).astype(bf16)


def end_rows(layers, outs):
    rows, lanes = layers[0].shape
    low = iota((SUBLANES, lanes), 0) < STEPS
    last = [pltpu.roll(layer[rows - SUBLANES :], STEPS, 0) for layer in layers]
    picked = [jnp.where(low, a, pltpu.roll(b, STEPS, 0)) for a, b in (last, [layer[:SUBLANES] for layer in layers])]
    if outs == 1:
        picked = [jnp.where(lax.axis_index("sub") == 0, *picked)]
    return picked


def pack_tile_kernel(fields, ahead, behind, *ends):
    layers = fields.shape[1]
    for out, base, unused in ((ahead, layers - STEPS, 0), (behind, 0, STEPS - 1)):
        kept = [(at, k) for at in range(FIELDS) for k in range(STEPS) if at < 2 or k != unused]
        for entry, (at, k) in enumerate(kept):
            out[entry] = fields[at, base + k].astype(bf16)
    for at in range(FIELDS):
        for pair in range(layers // 2):
            picked = end_rows([fields[at, 2 * pair], fields[at, 2 * pair + 1]], len(ends))
            for out, value in zip(ends, picked):
                out[at, pair * SUBLANES : (pair + 1) * SUBLANES, :] = value.astype(bf16)


def layer_beside(at, k, layers, tile_before, tile_after):
    side, depth, unused = (tile_before, k, 0) if k < STEPS else (tile_after, k - STEPS - layers, STEPS - 1)
    if at == 2 and depth == unused:
        return jnp.zeros(side.shape[1:], f32)
    return side[at * STEPS + depth - (at == 2 and unused == 0)].astype(f32)


def layer_of_block(at, k, fields, tile_before, tile_after):
    layers = fields.shape[1]
    if STEPS <= k < STEPS + layers:
        return fields[at, k - STEPS]
    return layer_beside(at, k, layers, tile_before, tile_after)


def pack_sub_kernel(sides, tile_before, tile_after, ready_ref, *rest):
    ends, outs = rest[:sides], rest[sides:]
    held = ends[0].shape[1]
    layers = held // STEPS
    for at in range(FIELDS):
        for out, own in zip(outs, ends):
            out[at, STEPS * STEPS : STEPS * STEPS + held, :] = own[at]
        for first in (*range(0, STEPS, 2), *range(STEPS + layers, 2 * STEPS + layers, 2)):
            beside = [layer_beside(at, k, layers, tile_before, tile_after) for k in (first, first + 1)]
            for out, value in zip(outs, end_rows(beside, sides)):
                out[at, first * STEPS : first * STEPS + SUBLANES, :] = value.astype(bf16)


def side_rows(at, k, after_ref, before_ref):
    start = k // 2 * SUBLANES
    after = after_ref[at, start : start + SUBLANES, :].astype(f32)
    before = before_ref[at, start : start + SUBLANES, :].astype(f32)
    if k % 2 == 0:
        before = pltpu.roll(before, STEPS, 0)
    else:
        after = pltpu.roll(after, STEPS, 0)
    me, count = lax.axis_index("sub"), lax.axis_size("sub")
    low = iota(after.shape, 0) < STEPS
    keep_after = jnp.where(me < count - 1, 1.0, 0.0)
    keep_before = jnp.where(me > 0, 1.0, 0.0)
    return jnp.where(low, after * keep_after, before * keep_before)


def pack_rep_kernel(fields, tile_before, tile_after, sub_after, sub_before, ready_ref, out_ref, ends_ref):
    layers, rows, lanes = fields.shape[1:]
    beside = 2 * STEPS
    total = layers + 2 * STEPS
    layer_at = iota((rows + beside, lanes), 1) // beside
    for at in range(FIELDS):
        packed = jnp.zeros((rows + beside, lanes), f32)
        for k in range(total):
            here = layer_of_block(at, k, fields, tile_before, tile_after), side_rows(at, k, sub_after, sub_before)
            here = pltpu.roll(jnp.concatenate(here, 0), (beside * k + STEPS) % lanes, 1)
            packed = jnp.where(layer_at == k, here, packed)
        out_ref[at] = packed.astype(bf16)
        ends_ref[at] = packed


def across(value):
    return pltpu.roll(value, 1, 0) + pltpu.roll(value, value.shape[0] - 1, 0)


def beside_lanes(value):
    lanes = value.shape[1]
    lane = iota(value.shape, 1)
    left = jnp.where(lane == 0, 0.0, pltpu.roll(value, 1, 1))
    right = jnp.where(lane == lanes - 1, 0.0, pltpu.roll(value, lanes - 1, 1))
    return left + right


def laplace(below, here, above):
    return below + above + across(here) + beside_lanes(here) - 6.0 * here


def row_masks(layers, rows, lanes):
    tile, sub = lax.axis_index("tile"), lax.axis_index("sub")
    keep_low, keep_high = jnp.where(tile > 0, 1.0, 0.0), jnp.where(tile < lax.axis_size("tile") - 1, 1.0, 0.0)
    keep_before, keep_after = jnp.where(sub > 0, 1.0, 0.0), jnp.where(sub < lax.axis_size("sub") - 1, 1.0, 0.0)
    row = iota((rows + 2 * STEPS, lanes), 0)
    inside = jnp.where(row < rows, 1.0, jnp.where(row < rows + STEPS, keep_after, keep_before))
    return inside * keep_low, inside, inside * keep_high


def assemble_kernel(
    fields, tile_before, tile_after, sub_after, sub_before, ready_ref, now, ago, coef, lapped, lapped_ago
):
    layers, rows, lanes = fields.shape[1:]
    total = layers + 2 * STEPS
    tile = lax.axis_index("tile")
    keep_low, keep_high = jnp.where(tile > 0, 1.0, 0.0), jnp.where(tile < lax.axis_size("tile") - 1, 1.0, 0.0)
    for at, out in enumerate((now, ago, coef)):
        extra = viscous if at == 2 else 0.0
        for k in range(total):
            keep = keep_low if k < STEPS else keep_high if k >= STEPS + layers else 1.0
            out[k, :rows] = layer_of_block(at, k, fields, tile_before, tile_after) * keep + extra
            out[k, rows:] = side_rows(at, k, sub_after, sub_before) * keep + extra
    for value, out in ((now, lapped), (ago, lapped_ago)):
        for k in range(1, total - 1):
            out[k] = laplace(value[k - 1], value[k], value[k + 1])


def window_kernel(
    now_in, ago_in, coef, lapped_in, lapped_ago_in, ends_ref, rep_after, rep_before, place_ref, states, *rest
):
    *sends, now, ago, lapped = rest
    layers, rows, lanes = states.shape[1:]
    beside = 2 * STEPS
    total, wide_rows = now.shape[:2]
    rep, reps = lax.axis_index("rep"), lax.axis_size("rep")
    keep_left, keep_right = jnp.where(rep > 0, 1.0, 0.0), jnp.where(rep < reps - 1, 1.0, 0.0)
    inside_low, inside, inside_high = row_masks(layers, rows, lanes)

    lane = iota((wide_rows, lanes), 1)
    layer_of = lane // beside
    outer = lane % beside < STEPS
    ending = (lane == 0) | (lane == lanes - 1)
    inside_side = jnp.where(layer_of < STEPS, inside_low, jnp.where(layer_of < STEPS + layers, inside, inside_high))
    inside_side = jnp.where(layer_of < total, inside_side, 0.0)
    inside_left = inside_side * jnp.where(outer, keep_left, 1.0)
    inside_right = inside_side * jnp.where(outer, 1.0, keep_right)
    lefts, rights = [], []
    for at in range(FIELDS):
        extra = viscous if at == 2 else 0.0
        left = jnp.where(outer, rep_before[at].astype(f32), ends_ref[at])
        right = jnp.where(outer, ends_ref[at], rep_after[at].astype(f32))
        lefts.append(left * inside_left + extra)
        rights.append(right * inside_right + extra)
    left_now, left_ago, left_coef = lefts
    right_now, right_ago, right_coef = rights

    def edges(left, right):
        return jnp.where(outer, pltpu.roll(right, lanes - 1, 1), pltpu.roll(left, 1, 1))

    def edge_of(k, edge):
        return jnp.where(ending, pltpu.roll(edge, (lanes - beside * k - STEPS) % lanes, 1), 0.0)

    def laplace_side(side):
        beyond = pltpu.roll(side, beside, 1) + pltpu.roll(side, lanes - beside, 1)
        return beyond + across(side) + pltpu.roll(side, 1, 1) + pltpu.roll(side, lanes - 1, 1) - 6.0 * side

    def advance(here, before, gain, lap, lap_before, mask):
        change = here - before
        driving = gain * lap - lap_before + 2.0 * nonlinear * change * change
        return (here + change + (1.0 + 2.0 * nonlinear * here) * driving) * mask

    edge_ago = edges(left_ago, right_ago)
    left_lapped, right_lapped = viscous * laplace_side(left_ago), viscous * laplace_side(right_ago)

    cells = layers * rows
    slots = place_ref.shape[1]
    lane_of = place_ref[cells:]
    loads = jnp.zeros((SUBLANES, slots), f32)
    for step in range(STEPS):
        edge = edges(left_now, right_now)
        found = jnp.zeros((rows, slots), f32)
        source = now_in if step == 0 else now
        below, here = source[step], source[step + 1]
        for k in range(step + 1, total - step - 1):
            above = source[k + 1]
            if step == 0:
                lap, before = lapped_in[k], ago_in[k]
                lap_before = viscous * (lapped_ago_in[k] + edge_of(k, edge_ago))
            else:
                lap, before, lap_before = laplace(below, here, above), ago[k], lapped[k]
            lap = lap + edge_of(k, edge)
            mask = inside_low if k < STEPS else inside_high if k >= STEPS + layers else inside
            updated = advance(here, before, coef[k], lap, lap_before, mask)
            now[k] = updated
            ago[k] = here
            lapped[k] = viscous * lap
            own = k - STEPS
            if 0 <= own < layers:
                core = updated[:rows]
                row_of = place_ref[own * rows : (own + 1) * rows].astype(f32)
                found = found + dot(core.astype(bf16), lane_of, (1, 0)) * row_of
                if step >= STEPS - 2:
                    states[STEPS - 1 - step, own] = core
            below, here = here, above
        if step < STEPS - 1:
            lap = laplace_side(left_now)
            updated = advance(left_now, left_ago, left_coef, lap, left_lapped, inside_left)
            left_now, left_ago, left_lapped = updated, left_now, viscous * lap
            lap = laplace_side(right_now)
            updated = advance(right_now, right_ago, right_coef, lap, right_lapped, inside_right)
            right_now, right_ago, right_lapped = updated, right_now, viscous * lap
        loads = jnp.where(iota((SUBLANES, slots), 0) == step, jnp.sum(found, axis=0, keepdims=True), loads)

    size = slots // len(sends)
    for at, send in enumerate(sends):
        send[...] = loads[:STEPS, at * size : (at + 1) * size].astype(bf16)


def store_kernel(states, final_hbm, prior_hbm, sems):
    for copy in fetch(((states.at[0], final_hbm), (states.at[1], prior_hbm)), sems):
        copy.wait()


def turn_kernel(buckets, ready_ref, shapes_ref, area_ref, turned_ref, flipped_ref, area_out):
    total = shapes_ref.shape[0]
    bucket = total // buckets
    entry = iota((total, 1), 0)
    part = entry // bucket
    wanted = entry + ((part ^ lax.axis_index("tile")) - part) * bucket
    picks = jnp.where(iota((total, total), 1) == wanted, 1.0, 0.0)
    turned = dot(picks.astype(bf16), shapes_ref[...], (1, 0))
    turned_ref[...] = turned.astype(bf16)
    flipped_ref[...] = turned.T.astype(bf16)
    area_out[...] = lax.dot_general(
        area_ref[...], picks, (((1,), (1,)), ((), ())), precision=lax.Precision.HIGHEST, preferred_element_type=f32
    )


def project_kernel(order, area_ref, turned_ref, *rest):
    *parts, out_ref = rest
    size = parts[0].shape[1]
    forces = 0.0
    for at, part in zip(order, parts):
        weighted = (part[...].astype(f32) * area_ref[:, at * size : (at + 1) * size]).astype(bf16)
        forces = forces + dot(weighted, turned_ref[at * size : (at + 1) * size, :], (1, 0))
    out_ref[...] = forces


def respond_kernel(addends, freq_ref, damp_ref, start_ref, flipped_ref, *rest):
    forces_in, rest = rest[:addends], rest[addends:]
    state_ref, *sends, accel = rest
    forces = forces_in[0][...]
    for ref in forces_in[1:]:
        forces = forces + ref[...].astype(f32)
    frequency, damping = freq_ref[...], damp_ref[...]
    drag, stiffness = 2.0 * damping * frequency, frequency * frequency
    displace, velocity = start_ref[0:1, :], start_ref[1:2, :]
    accel[...] = jnp.zeros_like(accel)
    for step in range(STEPS):
        acceleration = forces[step : step + 1, :] - drag * velocity - stiffness * displace
        velocity = velocity + acceleration
        displace = displace + velocity
        accel[step : step + 1, :] = acceleration
    state_ref[0:1, :] = displace
    state_ref[1:2, :] = velocity
    node = dot(accel[...].astype(bf16), flipped_ref[...], (1, 0))
    size = node.shape[1] // len(sends)
    for at, send in enumerate(sends):
        send[...] = node[:STEPS, at * size : (at + 1) * size].astype(bf16)


def return_kernel(order, route_ref, *rest):
    *parts, out_ref = rest
    size = parts[0].shape[1]
    surface = 0.0
    for at, part in zip(order, parts):
        surface = surface + dot(part[...], route_ref[at * size : (at + 1) * size, :], (1, 0))
    out_ref[...] = surface.astype(bf16)


def exchange(parts, order, crossed):
    buckets = lax.axis_size("tile")
    if len(parts) == buckets:
        own = lax.ppermute(parts[0], "rep", swaps(2, 1)) if crossed else parts[0]
        return [send(parts[k], "tile", swaps(buckets, k), crossed) if k else own for k in order]
    tiles = jnp.arange(buckets) ^ lax.axis_index("tile")
    (whole,) = parts
    steps, total = whole.shape
    stacked = whole.reshape(steps, buckets, total // buckets).transpose(1, 0, 2)
    stacked = lax.all_to_all(stacked[tiles], "tile", 0, 0, tiled=True)
    return [stacked[tiles].transpose(1, 0, 2).reshape(steps, total)]


def body(
    pressure,
    previous_pressure,
    courant_square,
    node_area,
    mode_shapes,
    frequency,
    damping_ratio,
    modal_start,
    slot_cell,
    slot_owner,
    surface_count,
):
    buckets, subs, reps = (lax.axis_size(axis) for axis in ("tile", "sub", "rep"))
    layers, rows, lanes = pressure.shape
    slots = slot_cell.shape[-1]
    modes = mode_shapes.shape[1]
    bucket = slots // buckets
    parts = buckets if buckets in (2, 4) and bucket % 16 == 0 else 1
    total = layers + 2 * STEPS
    wide_rows = rows + 2 * STEPS
    crossed = parts > 1 and reps == 2
    if crossed:
        mode_shapes, node_area = (lax.ppermute(value, "rep", swaps(2, 1)) for value in (mode_shapes, node_area))

    cells = layers * rows
    fields = jnp.stack([pressure, previous_pressure, courant_square])
    sides = 1 if subs == 2 else 2
    slab = shape_of((FIELDS * STEPS - 1, rows, lanes), bf16)
    held = shape_of((FIELDS, layers * STEPS, lanes), bf16)
    ahead, behind, *ends = call(pack_tile_kernel, (slab, slab) + (held,) * sides, (fields,))
    route, place = call(
        functools.partial(route_kernel, buckets, lanes, cells),
        (shape_of((slots, slots), bf16), shape_of((cells + lanes, slots), bf16)),
        (ahead, slot_owner.reshape(1, slots), slot_cell.reshape(1, slots), surface_count.reshape(1, 1)),
    )
    two = reps == 2
    tile_halo = [send(value, "tile", shift(buckets, by), two) for value, by in ((ahead, 1), (behind, -1))]
    if two:
        ends = [lax.ppermute(value, "rep", swaps(2, 1)) for value in ends]
    slab = shape_of((FIELDS, total * STEPS, lanes), bf16)
    packed = call(functools.partial(pack_sub_kernel, sides), (slab,) * sides, (*tile_halo, route, *ends))
    if sides == 1:
        sub_halo = (send(packed[0], "sub", swaps(2, 1), two),) * 2
    else:
        sub_halo = both_ways("sub", *packed, two)
    if two:
        tile_halo = [lax.ppermute(value, "rep", swaps(2, 1)) for value in tile_halo]

    turned, flipped, area = call(
        functools.partial(turn_kernel, buckets),
        (shape_of(mode_shapes.shape, bf16), shape_of(mode_shapes.shape[::-1], bf16), shape_of((1, slots), f32)),
        (packed[0], mode_shapes, node_area.reshape(1, slots)),
    )

    packed, ends = call(
        pack_rep_kernel,
        (shape_of((FIELDS, wide_rows, lanes), bf16), shape_of((FIELDS, wide_rows, lanes), f32)),
        (fields, *tile_halo, *sub_halo, area),
    )
    if reps == 2:
        rep_halo = (lax.ppermute(packed, "rep", shift(2, 1)),) * 2
    else:
        rep_halo = both_ways("rep", packed, packed)

    wide = shape_of((total, wide_rows, lanes), f32)
    assembled = call(assemble_kernel, (wide,) * 5, (fields, *tile_halo, *sub_halo, packed))
    wide = pltpu.VMEM(wide.shape, f32)
    part = shape_of((STEPS, slots // parts), bf16)
    block = shape_of(pressure.shape, f32)
    states, *sends = call(
        window_kernel,
        (shape_of((2, layers, rows, lanes), f32),) + (part,) * parts,
        (*assembled, ends, *rep_halo, place),
        scratch=[wide] * 3,
        micros=2.0,
    )
    final_field, prior_field = call(
        store_kernel, (block, block), (states,), out_specs=(HBM, HBM), scratch=[pltpu.SemaphoreType.DMA((2,))]
    )

    order = [k for k in (0, 2, 3, 1) if k < parts]
    forces = call(
        functools.partial(project_kernel, order),
        shape_of((STEPS, modes), f32),
        (area, turned, *exchange(sends, order, crossed)),
    )
    addends = [forces]
    for axis in ("rep", "sub", "tile"):
        count = lax.axis_size(axis)
        forces = functools.reduce(jnp.add, addends)
        if count in (2, 4):
            sent = forces.astype(bf16) if axis != "rep" else forces
            places = [swaps(count, k) for k in (2, 3, 1) if k < count]
            addends = [forces] + [send(sent, axis, swap, reps == 2 and axis != "rep") for swap in places]
        else:
            addends = [lax.psum(forces, axis)]

    state, *sends = call(
        functools.partial(respond_kernel, len(addends)),
        (shape_of((2, modes), f32),) + (part,) * parts,
        (frequency.reshape(1, modes), damping_ratio.reshape(1, modes), modal_start, flipped, *addends),
        scratch=[pltpu.VMEM((SUBLANES, modes), f32)],
    )
    share = modes // (buckets * subs * reps)
    modal_state = lax.dynamic_slice_in_dim(state, lax.axis_index(("tile", "sub", "rep")) * share, share, 1)
    order = [k for k in (3, 2, 1, 0) if k < parts]
    surface = call(
        functools.partial(return_kernel, order), shape_of((STEPS, slots), bf16), (route, *exchange(sends, order, crossed))
    )
    return (final_field, prior_field, surface.reshape(1, 1, 1, STEPS, slots), modal_state)


def solution(mesh):
    in_specs = (
        P(("groups", "tile"), "sub", "rep"),
        P(("groups", "tile"), "sub", "rep"),
        P(("groups", "tile"), "sub", "rep"),
        P(("groups", "tile", "sub", "rep")),
        P(("groups", "tile", "sub", "rep"), None),
        P("groups"),
        P("groups"),
        P(None, "groups"),
        P(("groups", "tile"), "sub", "rep", None),
        P(("groups", "tile"), "sub", "rep", None, None),
        P(("groups", "sub"), "rep", "tile"),
    )
    out_specs = (
        P(("groups", "tile"), "sub", "rep"),
        P(("groups", "tile"), "sub", "rep"),
        P(("groups", "tile"), "sub", "rep", None, None),
        P(None, ("groups", "tile", "sub", "rep")),
    )
    return jax.shard_map(body, mesh=mesh, in_specs=in_specs, out_specs=out_specs, check_vma=False)
```

```python
import functools

import jax
import jax.numpy as jnp
from jax import lax
from jax.experimental import pallas as pl
from jax.experimental.pallas import tpu as pltpu
from jax.sharding import PartitionSpec as P

STEPS = 4
FIELDS = 3
SUBLANES = 8

nonlinear = 0.03
viscous = 0.02

f32 = jnp.float32
bf16 = jnp.bfloat16
VMEM = pl.BlockSpec(memory_space=pltpu.VMEM)
HBM = pl.BlockSpec(memory_space=pltpu.HBM)


def shift(count, by):
    return [(i, (i + by) % count) for i in range(count)]


def line(count, by):
    return [(i, i + by) for i in range(count) if 0 <= i + by < count]


def swaps(count, by):
    return [(i, i ^ by) for i in range(count)]


def iota(shape, dim):
    return lax.broadcasted_iota(jnp.int32, shape, dim)


def dot(a, b, contract):
    return lax.dot_general(a, b, (((contract[0],), (contract[1],)), ((), ())), preferred_element_type=f32)


def call(kernel, out_shape, inputs, scratch=(), specs=None, out_specs=None, micros=1.0, vmem=32):
    return pl.pallas_call(
        kernel,
        out_shape=out_shape,
        in_specs=specs or [VMEM] * len(inputs),
        out_specs=out_specs or jax.tree.map(lambda _: VMEM, out_shape),
        scratch_shapes=list(scratch),
        cost_estimate=pl.CostEstimate(flops=int(micros * 1e9), bytes_accessed=0, transcendentals=0),
        compiler_params=pltpu.CompilerParams(vmem_limit_bytes=vmem * 1024 * 1024),
    )(*inputs)


def shape_of(dims, dtype):
    return jax.ShapeDtypeStruct(dims, dtype)


def fetch(pairs, sems):
    copies = [pltpu.make_async_copy(a, b, sems.at[i]) for i, (a, b) in enumerate(pairs)]
    for copy in copies:
        copy.start()
    return copies


def send(value, axis, places, crossed):
    if not crossed:
        return lax.ppermute(value, axis, places)
    return lax.ppermute(value, (axis, "rep"), [(2 * i + r, 2 * j + 1 - r) for i, j in places for r in range(2)])


def both_ways(axis, ahead, behind, crossed=False):
    count = lax.axis_size(axis)
    after = send(behind, axis, line(count, -1), crossed)
    before = send(ahead, axis, line(count, 1), crossed)
    return after, before


def route_kernel(buckets, lanes, rows, after_ref, owner_ref, cell_ref, count_ref, route_ref, place_ref):
    slots = owner_ref.shape[1]
    bucket = slots // buckets
    me = lax.axis_index("tile")
    owner = owner_ref[...]
    live = iota((1, slots), 1) < count_ref[...]
    held = -(-buckets // SUBLANES) * SUBLANES
    member = jnp.where((iota((held, slots), 0) == owner) & live, 1.0, 0.0)
    earlier = jnp.where(iota((slots, slots), 0) < iota((slots, slots), 1), 1.0, 0.0).astype(bf16)
    before = dot(member.astype(bf16), earlier, (1, 0))
    rank = jnp.sum(before * member, axis=0, keepdims=True).astype(jnp.int32)
    target = jnp.where(live, (owner ^ me) * bucket + rank, -1)
    route = jnp.where(iota((slots, slots), 0) == target, 1.0, 0.0).astype(bf16)
    route_ref[...] = route
    cell = cell_ref[...]
    row = jnp.where(iota((rows, slots), 0) == cell // lanes, 1.0, 0.0)
    lane = jnp.where(iota((lanes, slots), 0) == cell % lanes, 1.0, 0.0)
    place_ref[:rows] = dot(row.astype(bf16), route, (1, 1)).astype(bf16)
    place_ref[rows:] = dot(lane.astype(bf16), route, (1, 1)).astype(bf16)


def end_rows(layers, outs):
    rows, lanes = layers[0].shape
    low = iota((SUBLANES, lanes), 0) < STEPS
    last = [pltpu.roll(layer[rows - SUBLANES :], STEPS, 0) for layer in layers]
    picked = [jnp.where(low, a, pltpu.roll(b, STEPS, 0)) for a, b in (last, [layer[:SUBLANES] for layer in layers])]
    if outs == 1:
        picked = [jnp.where(lax.axis_index("sub") == 0, *picked)]
    return picked


def pack_tile_kernel(fields, ahead, behind, *ends):
    layers = fields.shape[1]
    for out, base, unused in ((ahead, layers - STEPS, 0), (behind, 0, STEPS - 1)):
        kept = [(at, k) for at in range(FIELDS) for k in range(STEPS) if at < 2 or k != unused]
        for entry, (at, k) in enumerate(kept):
            out[entry] = fields[at, base + k].astype(bf16)
    for at in range(FIELDS):
        for pair in range(layers // 2):
            picked = end_rows([fields[at, 2 * pair], fields[at, 2 * pair + 1]], len(ends))
            for out, value in zip(ends, picked):
                out[at, pair * SUBLANES : (pair + 1) * SUBLANES, :] = value.astype(bf16)


def layer_beside(at, k, layers, tile_before, tile_after):
    side, depth, unused = (tile_before, k, 0) if k < STEPS else (tile_after, k - STEPS - layers, STEPS - 1)
    if at == 2 and depth == unused:
        return jnp.zeros(side.shape[1:], f32)
    return side[at * STEPS + depth - (at == 2 and unused == 0)].astype(f32)


def layer_of_block(at, k, fields, tile_before, tile_after):
    layers = fields.shape[1]
    if STEPS <= k < STEPS + layers:
        return fields[at, k - STEPS]
    return layer_beside(at, k, layers, tile_before, tile_after)


NEAR, NEXT = 4, 6


def beside_tile(nearest, outs):
    rows, lanes = nearest[0].shape
    row = iota((SUBLANES, lanes), 0)
    picked = []
    for pieces, rolls in (([a[rows - SUBLANES :] for a in nearest], (4, 6, 0)), ([a[:SUBLANES] for a in nearest], (0, 4, 6))):
        a, b, c = (pltpu.roll(piece, by, 0) if by else piece for piece, by in zip(pieces, rolls))
        picked.append(jnp.where(row < NEAR, a, jnp.where(row < NEXT, b, c)))
    if outs == 1:
        picked = [jnp.where(lax.axis_index("sub") == 0, *picked)]
    return picked


def pack_sub_kernel(sides, tile_before, tile_after, ready_ref, *rest):
    ends, outs = rest[:sides], rest[sides:]
    held = ends[0].shape[1]
    layers = held // STEPS
    for at in range(FIELDS):
        before = [layer_beside(at, STEPS - 1 - k, layers, tile_before, tile_after) for k in range(STEPS - 1)]
        after = [layer_beside(at, STEPS + layers + k, layers, tile_before, tile_after) for k in range(STEPS - 1)]
        for out, own, a, b in zip(outs, ends, beside_tile(before, sides), beside_tile(after, sides)):
            out[at, :held, :] = own[at]
            out[at, held:, :] = jnp.concatenate([a, b], 0).astype(bf16)


def side_rows(at, k, layers, after_ref, before_ref):
    own = k - STEPS
    if 0 <= own < layers:
        start, rolls = own // 2 * SUBLANES, ((0, 4), (4, 0))[own % 2]
    else:
        depth = -own if own < 0 else own - layers + 1
        if depth == STEPS:
            return jnp.zeros((SUBLANES, after_ref.shape[2]), f32)
        start, rolls = layers * STEPS + (own > 0) * SUBLANES, ((0, 4), (4, 2), (2, 0))[depth - 1]
    after = after_ref[at, start : start + SUBLANES, :].astype(f32)
    before = before_ref[at, start : start + SUBLANES, :].astype(f32)
    after, before = (pltpu.roll(value, by, 0) if by else value for value, by in zip((after, before), rolls))
    me, count = lax.axis_index("sub"), lax.axis_size("sub")
    low = iota(after.shape, 0) < STEPS
    keep_after = jnp.where(me < count - 1, 1.0, 0.0)
    keep_before = jnp.where(me > 0, 1.0, 0.0)
    return jnp.where(low, after * keep_after, before * keep_before)


def pack_rep_kernel(fields, tile_before, tile_after, sub_after, sub_before, ready_ref, out_ref, ends_ref):
    layers, rows, lanes = fields.shape[1:]
    beside = 2 * STEPS
    total = layers + 2 * STEPS
    layer_at = iota((rows + beside, lanes), 1) // beside
    for at in range(FIELDS):
        packed = jnp.zeros((rows + beside, lanes), f32)
        for k in range(total):
            here = layer_of_block(at, k, fields, tile_before, tile_after), side_rows(at, k, layers, sub_after, sub_before)
            here = pltpu.roll(jnp.concatenate(here, 0), (beside * k + STEPS) % lanes, 1)
            packed = jnp.where(layer_at == k, here, packed)
        out_ref[at] = packed.astype(bf16)
        ends_ref[at] = packed


def across(value):
    return pltpu.roll(value, 1, 0) + pltpu.roll(value, value.shape[0] - 1, 0)


def beside_lanes(value):
    lanes = value.shape[1]
    lane = iota(value.shape, 1)
    left = jnp.where(lane == 0, 0.0, pltpu.roll(value, 1, 1))
    right = jnp.where(lane == lanes - 1, 0.0, pltpu.roll(value, lanes - 1, 1))
    return left + right


def laplace(below, here, above):
    return below + above + across(here) + beside_lanes(here) - 6.0 * here


def row_masks(layers, rows, lanes):
    tile, sub = lax.axis_index("tile"), lax.axis_index("sub")
    keep_low, keep_high = jnp.where(tile > 0, 1.0, 0.0), jnp.where(tile < lax.axis_size("tile") - 1, 1.0, 0.0)
    keep_before, keep_after = jnp.where(sub > 0, 1.0, 0.0), jnp.where(sub < lax.axis_size("sub") - 1, 1.0, 0.0)
    row = iota((rows + 2 * STEPS, lanes), 0)
    inside = jnp.where(row < rows, 1.0, jnp.where(row < rows + STEPS, keep_after, keep_before))
    return inside * keep_low, inside, inside * keep_high


def assemble_kernel(
    fields, tile_before, tile_after, sub_after, sub_before, ready_ref, now, ago, coef, lapped, lapped_ago
):
    layers, rows, lanes = fields.shape[1:]
    total = layers + 2 * STEPS
    tile = lax.axis_index("tile")
    keep_low, keep_high = jnp.where(tile > 0, 1.0, 0.0), jnp.where(tile < lax.axis_size("tile") - 1, 1.0, 0.0)
    for at, out in enumerate((now, ago, coef)):
        extra = viscous if at == 2 else 0.0
        for k in range(total):
            keep = keep_low if k < STEPS else keep_high if k >= STEPS + layers else 1.0
            out[k, :rows] = layer_of_block(at, k, fields, tile_before, tile_after) * keep + extra
            out[k, rows:] = side_rows(at, k, layers, sub_after, sub_before) * keep + extra
    for value, out in ((now, lapped), (ago, lapped_ago)):
        for k in range(1, total - 1):
            out[k] = laplace(value[k - 1], value[k], value[k + 1])


def window_kernel(
    now_in, ago_in, coef, lapped_in, lapped_ago_in, ends_ref, rep_after, rep_before, place_ref, states, *rest
):
    *sends, now, ago, lapped = rest
    layers, rows, lanes = states.shape[1:]
    beside = 2 * STEPS
    total, wide_rows = now.shape[:2]
    rep, reps = lax.axis_index("rep"), lax.axis_size("rep")
    keep_left, keep_right = jnp.where(rep > 0, 1.0, 0.0), jnp.where(rep < reps - 1, 1.0, 0.0)
    inside_low, inside, inside_high = row_masks(layers, rows, lanes)

    lane = iota((wide_rows, lanes), 1)
    layer_of = lane // beside
    outer = lane % beside < STEPS
    ending = (lane == 0) | (lane == lanes - 1)
    inside_side = jnp.where(layer_of < STEPS, inside_low, jnp.where(layer_of < STEPS + layers, inside, inside_high))
    inside_side = jnp.where(layer_of < total, inside_side, 0.0)
    inside_left = inside_side * jnp.where(outer, keep_left, 1.0)
    inside_right = inside_side * jnp.where(outer, 1.0, keep_right)
    lefts, rights = [], []
    for at in range(FIELDS):
        extra = viscous if at == 2 else 0.0
        left = jnp.where(outer, rep_before[at].astype(f32), ends_ref[at])
        right = jnp.where(outer, ends_ref[at], rep_after[at].astype(f32))
        lefts.append(left * inside_left + extra)
        rights.append(right * inside_right + extra)
    left_now, left_ago, left_coef = lefts
    right_now, right_ago, right_coef = rights

    def edges(left, right):
        return jnp.where(outer, pltpu.roll(right, lanes - 1, 1), pltpu.roll(left, 1, 1))

    def edge_of(k, edge):
        return jnp.where(ending, pltpu.roll(edge, (lanes - beside * k - STEPS) % lanes, 1), 0.0)

    def laplace_side(side):
        beyond = pltpu.roll(side, beside, 1) + pltpu.roll(side, lanes - beside, 1)
        return beyond + across(side) + pltpu.roll(side, 1, 1) + pltpu.roll(side, lanes - 1, 1) - 6.0 * side

    def advance(here, before, gain, lap, lap_before, mask):
        change = here - before
        driving = gain * lap - lap_before + 2.0 * nonlinear * change * change
        return (here + change + (1.0 + 2.0 * nonlinear * here) * driving) * mask

    edge_ago = edges(left_ago, right_ago)
    left_lapped, right_lapped = viscous * laplace_side(left_ago), viscous * laplace_side(right_ago)

    cells = layers * rows
    slots = place_ref.shape[1]
    lane_of = place_ref[cells:]
    loads = jnp.zeros((SUBLANES, slots), f32)
    for step in range(STEPS):
        edge = edges(left_now, right_now)
        found = jnp.zeros((rows, slots), f32)
        source = now_in if step == 0 else now
        below, here = source[step], source[step + 1]
        for k in range(step + 1, total - step - 1):
            above = source[k + 1]
            if step == 0:
                lap, before = lapped_in[k], ago_in[k]
                lap_before = viscous * (lapped_ago_in[k] + edge_of(k, edge_ago))
            else:
                lap, before, lap_before = laplace(below, here, above), ago[k], lapped[k]
            lap = lap + edge_of(k, edge)
            mask = inside_low if k < STEPS else inside_high if k >= STEPS + layers else inside
            updated = advance(here, before, coef[k], lap, lap_before, mask)
            now[k] = updated
            ago[k] = here
            lapped[k] = viscous * lap
            own = k - STEPS
            if 0 <= own < layers:
                core = updated[:rows]
                row_of = place_ref[own * rows : (own + 1) * rows].astype(f32)
                found = found + dot(core.astype(bf16), lane_of, (1, 0)) * row_of
                if step >= STEPS - 2:
                    states[STEPS - 1 - step, own] = core
            below, here = here, above
        if step < STEPS - 1:
            lap = laplace_side(left_now)
            updated = advance(left_now, left_ago, left_coef, lap, left_lapped, inside_left)
            left_now, left_ago, left_lapped = updated, left_now, viscous * lap
            lap = laplace_side(right_now)
            updated = advance(right_now, right_ago, right_coef, lap, right_lapped, inside_right)
            right_now, right_ago, right_lapped = updated, right_now, viscous * lap
        loads = jnp.where(iota((SUBLANES, slots), 0) == step, jnp.sum(found, axis=0, keepdims=True), loads)

    size = slots // len(sends)
    for at, send in enumerate(sends):
        send[...] = loads[:STEPS, at * size : (at + 1) * size].astype(bf16)


def store_kernel(states, final_hbm, prior_hbm, sems):
    for copy in fetch(((states.at[0], final_hbm), (states.at[1], prior_hbm)), sems):
        copy.wait()


def turn_kernel(buckets, ready_ref, shapes_ref, area_ref, turned_ref, flipped_ref, area_out):
    total = shapes_ref.shape[0]
    bucket = total // buckets
    me = lax.axis_index("tile")
    if bucket % 16 == 0:
        for k in range(buckets):
            first = pl.multiple_of((me ^ k) * bucket, 16)
            turned_ref[k * bucket : (k + 1) * bucket, :] = shapes_ref[pl.ds(first, bucket), :]
            area = jnp.zeros((1, bucket), f32)
            for part in range(buckets):
                area = jnp.where((me ^ k) == part, area_ref[:, part * bucket : (part + 1) * bucket], area)
            area_out[:, k * bucket : (k + 1) * bucket] = area
    else:
        entry = iota((total, 1), 0)
        part = entry // bucket
        wanted = entry + ((part ^ me) - part) * bucket
        picks = jnp.where(iota((total, total), 1) == wanted, 1.0, 0.0)
        turned_ref[...] = dot(picks.astype(bf16), shapes_ref[...], (1, 0)).astype(bf16)
        area_out[...] = lax.dot_general(
            area_ref[...], picks, (((1,), (1,)), ((), ())), precision=lax.Precision.HIGHEST, preferred_element_type=f32
        )
    flipped_ref[...] = turned_ref[...].astype(f32).T.astype(bf16)


def project_kernel(order, area_ref, turned_ref, *rest):
    *parts, out_ref = rest
    size = parts[0].shape[1]
    forces = 0.0
    for at, part in zip(order, parts):
        weighted = (part[...].astype(f32) * area_ref[:, at * size : (at + 1) * size]).astype(bf16)
        forces = forces + dot(weighted, turned_ref[at * size : (at + 1) * size, :], (1, 0))
    out_ref[...] = forces


def respond_kernel(addends, freq_ref, damp_ref, start_ref, flipped_ref, *rest):
    forces_in, rest = rest[:addends], rest[addends:]
    state_ref, *sends, accel = rest
    forces = forces_in[0][...]
    for ref in forces_in[1:]:
        forces = forces + ref[...].astype(f32)
    frequency, damping = freq_ref[...], damp_ref[...]
    drag, stiffness = 2.0 * damping * frequency, frequency * frequency
    displace, velocity = start_ref[0:1, :], start_ref[1:2, :]
    accel[...] = jnp.zeros_like(accel)
    for step in range(STEPS):
        acceleration = forces[step : step + 1, :] - drag * velocity - stiffness * displace
        velocity = velocity + acceleration
        displace = displace + velocity
        accel[step : step + 1, :] = acceleration
    state_ref[0:1, :] = displace
    state_ref[1:2, :] = velocity
    node = dot(accel[...].astype(bf16), flipped_ref[...], (1, 0))
    size = node.shape[1] // len(sends)
    for at, send in enumerate(sends):
        send[...] = node[:STEPS, at * size : (at + 1) * size].astype(bf16)


def return_kernel(order, route_ref, *rest):
    *parts, out_ref = rest
    size = parts[0].shape[1]
    surface = 0.0
    for at, part in zip(order, parts):
        surface = surface + dot(part[...], route_ref[at * size : (at + 1) * size, :], (1, 0))
    out_ref[...] = surface.astype(bf16)


def exchange(parts, order, crossed):
    buckets = lax.axis_size("tile")
    if len(parts) == buckets:
        own = lax.ppermute(parts[0], "rep", swaps(2, 1)) if crossed else parts[0]
        return [send(parts[k], "tile", swaps(buckets, k), crossed) if k else own for k in order]
    tiles = jnp.arange(buckets) ^ lax.axis_index("tile")
    (whole,) = parts
    steps, total = whole.shape
    stacked = whole.reshape(steps, buckets, total // buckets).transpose(1, 0, 2)
    stacked = lax.all_to_all(stacked[tiles], "tile", 0, 0, tiled=True)
    return [stacked[tiles].transpose(1, 0, 2).reshape(steps, total)]


def body(
    pressure,
    previous_pressure,
    courant_square,
    node_area,
    mode_shapes,
    frequency,
    damping_ratio,
    modal_start,
    slot_cell,
    slot_owner,
    surface_count,
):
    buckets, subs, reps = (lax.axis_size(axis) for axis in ("tile", "sub", "rep"))
    layers, rows, lanes = pressure.shape
    slots = slot_cell.shape[-1]
    modes = mode_shapes.shape[1]
    bucket = slots // buckets
    parts = buckets if buckets in (2, 4) and bucket % 16 == 0 else 1
    total = layers + 2 * STEPS
    wide_rows = rows + 2 * STEPS
    crossed = parts > 1 and reps == 2
    if crossed:
        mode_shapes, node_area = (lax.ppermute(value, "rep", swaps(2, 1)) for value in (mode_shapes, node_area))

    cells = layers * rows
    fields = jnp.stack([pressure, previous_pressure, courant_square])
    sides = 1 if subs == 2 else 2
    slab = shape_of((FIELDS * STEPS - 1, rows, lanes), bf16)
    held = shape_of((FIELDS, layers * STEPS, lanes), bf16)
    ahead, behind, *ends = call(pack_tile_kernel, (slab, slab) + (held,) * sides, (fields,))
    route, place = call(
        functools.partial(route_kernel, buckets, lanes, cells),
        (shape_of((slots, slots), bf16), shape_of((cells + lanes, slots), bf16)),
        (ahead, slot_owner.reshape(1, slots), slot_cell.reshape(1, slots), surface_count.reshape(1, 1)),
    )
    two = reps == 2
    tile_halo = [send(value, "tile", shift(buckets, by), two) for value, by in ((ahead, 1), (behind, -1))]
    if two:
        ends = [lax.ppermute(value, "rep", swaps(2, 1)) for value in ends]
    slab = shape_of((FIELDS, layers * STEPS + 2 * SUBLANES, lanes), bf16)
    packed = call(functools.partial(pack_sub_kernel, sides), (slab,) * sides, (*tile_halo, route, *ends))
    if sides == 1:
        sub_halo = (send(packed[0], "sub", swaps(2, 1), two),) * 2
    else:
        sub_halo = both_ways("sub", *packed, two)
    if two:
        tile_halo = [lax.ppermute(value, "rep", swaps(2, 1)) for value in tile_halo]

    turned, flipped, area = call(
        functools.partial(turn_kernel, buckets),
        (shape_of(mode_shapes.shape, bf16), shape_of(mode_shapes.shape[::-1], bf16), shape_of((1, slots), f32)),
        (packed[0], mode_shapes, node_area.reshape(1, slots)),
    )

    packed, ends = call(
        pack_rep_kernel,
        (shape_of((FIELDS, wide_rows, lanes), bf16), shape_of((FIELDS, wide_rows, lanes), f32)),
        (fields, *tile_halo, *sub_halo, area),
    )
    if reps == 2:
        rep_halo = (lax.ppermute(packed, "rep", shift(2, 1)),) * 2
    else:
        rep_halo = both_ways("rep", packed, packed)

    wide = shape_of((total, wide_rows, lanes), f32)
    assembled = call(assemble_kernel, (wide,) * 5, (fields, *tile_halo, *sub_halo, packed))
    wide = pltpu.VMEM(wide.shape, f32)
    part = shape_of((STEPS, slots // parts), bf16)
    block = shape_of(pressure.shape, f32)
    states, *sends = call(
        window_kernel,
        (shape_of((2, layers, rows, lanes), f32),) + (part,) * parts,
        (*assembled, ends, *rep_halo, place),
        scratch=[wide] * 3,
        micros=2.0,
    )
    final_field, prior_field = call(
        store_kernel, (block, block), (states,), out_specs=(HBM, HBM), scratch=[pltpu.SemaphoreType.DMA((2,))]
    )

    order = [k for k in (0, 2, 3, 1) if k < parts]
    forces = call(
        functools.partial(project_kernel, order),
        shape_of((STEPS, modes), f32),
        (area, turned, *exchange(sends, order, crossed)),
    )
    addends = [forces]
    for axis in ("rep", "sub", "tile"):
        count = lax.axis_size(axis)
        forces = functools.reduce(jnp.add, addends)
        if count in (2, 4):
            sent = forces.astype(bf16) if axis != "rep" else forces
            places = [swaps(count, k) for k in (2, 3, 1) if k < count]
            addends = [forces] + [send(sent, axis, swap, reps == 2 and axis != "rep") for swap in places]
        else:
            addends = [lax.psum(forces, axis)]

    state, *sends = call(
        functools.partial(respond_kernel, len(addends)),
        (shape_of((2, modes), f32),) + (part,) * parts,
        (frequency.reshape(1, modes), damping_ratio.reshape(1, modes), modal_start, flipped, *addends),
        scratch=[pltpu.VMEM((SUBLANES, modes), f32)],
    )
    share = modes // (buckets * subs * reps)
    modal_state = lax.dynamic_slice_in_dim(state, lax.axis_index(("tile", "sub", "rep")) * share, share, 1)
    order = [k for k in (3, 2, 1, 0) if k < parts]
    surface = call(
        functools.partial(return_kernel, order), shape_of((STEPS, slots), bf16), (route, *exchange(sends, order, crossed))
    )
    return (final_field, prior_field, surface.reshape(1, 1, 1, STEPS, slots), modal_state)


def solution(mesh):
    in_specs = (
        P(("groups", "tile"), "sub", "rep"),
        P(("groups", "tile"), "sub", "rep"),
        P(("groups", "tile"), "sub", "rep"),
        P(("groups", "tile", "sub", "rep")),
        P(("groups", "tile", "sub", "rep"), None),
        P("groups"),
        P("groups"),
        P(None, "groups"),
        P(("groups", "tile"), "sub", "rep", None),
        P(("groups", "tile"), "sub", "rep", None, None),
        P(("groups", "sub"), "rep", "tile"),
    )
    out_specs = (
        P(("groups", "tile"), "sub", "rep"),
        P(("groups", "tile"), "sub", "rep"),
        P(("groups", "tile"), "sub", "rep", None, None),
        P(None, ("groups", "tile", "sub", "rep")),
    )
    return jax.shard_map(body, mesh=mesh, in_specs=in_specs, out_specs=out_specs, check_vma=False)
```

```python
import functools

import jax
import jax.numpy as jnp
from jax import lax
from jax.experimental import pallas as pl
from jax.experimental.pallas import tpu as pltpu
from jax.sharding import PartitionSpec as P

STEPS = 4
FIELDS = 3
SUBLANES = 8

nonlinear = 0.03
viscous = 0.02

f32 = jnp.float32
bf16 = jnp.bfloat16
VMEM = pl.BlockSpec(memory_space=pltpu.VMEM)
HBM = pl.BlockSpec(memory_space=pltpu.HBM)


def shift(count, by):
    return [(i, (i + by) % count) for i in range(count)]


def line(count, by):
    return [(i, i + by) for i in range(count) if 0 <= i + by < count]


def swaps(count, by):
    return [(i, i ^ by) for i in range(count)]


def iota(shape, dim):
    return lax.broadcasted_iota(jnp.int32, shape, dim)


def dot(a, b, contract):
    return lax.dot_general(a, b, (((contract[0],), (contract[1],)), ((), ())), preferred_element_type=f32)


def call(kernel, out_shape, inputs, scratch=(), specs=None, out_specs=None, micros=1.0, vmem=32):
    return pl.pallas_call(
        kernel,
        out_shape=out_shape,
        in_specs=specs or [VMEM] * len(inputs),
        out_specs=out_specs or jax.tree.map(lambda _: VMEM, out_shape),
        scratch_shapes=list(scratch),
        cost_estimate=pl.CostEstimate(flops=int(micros * 1e9), bytes_accessed=0, transcendentals=0),
        compiler_params=pltpu.CompilerParams(vmem_limit_bytes=vmem * 1024 * 1024),
    )(*inputs)


def shape_of(dims, dtype):
    return jax.ShapeDtypeStruct(dims, dtype)


def fetch(pairs, sems):
    copies = [pltpu.make_async_copy(a, b, sems.at[i]) for i, (a, b) in enumerate(pairs)]
    for copy in copies:
        copy.start()
    return copies


def send(value, axis, places, crossed):
    if not crossed:
        return lax.ppermute(value, axis, places)
    return lax.ppermute(value, (axis, "rep"), [(2 * i + r, 2 * j + 1 - r) for i, j in places for r in range(2)])


def both_ways(axis, ahead, behind, crossed=False):
    count = lax.axis_size(axis)
    after = send(behind, axis, line(count, -1), crossed)
    before = send(ahead, axis, line(count, 1), crossed)
    return after, before


def route_kernel(buckets, lanes, rows, after_ref, owner_ref, cell_ref, count_ref, route_ref, place_ref):
    slots = owner_ref.shape[1]
    bucket = slots // buckets
    me = lax.axis_index("tile")
    owner = owner_ref[...]
    live = iota((1, slots), 1) < count_ref[...]
    held = -(-buckets // SUBLANES) * SUBLANES
    member = jnp.where((iota((held, slots), 0) == owner) & live, 1.0, 0.0)
    earlier = jnp.where(iota((slots, slots), 0) < iota((slots, slots), 1), 1.0, 0.0).astype(bf16)
    before = dot(member.astype(bf16), earlier, (1, 0))
    rank = jnp.sum(before * member, axis=0, keepdims=True).astype(jnp.int32)
    target = jnp.where(live, (owner ^ me) * bucket + rank, -1)
    route = jnp.where(iota((slots, slots), 0) == target, 1.0, 0.0).astype(bf16)
    route_ref[...] = route
    cell = cell_ref[...]
    row = jnp.where(iota((rows, slots), 0) == cell // lanes, 1.0, 0.0)
    lane = jnp.where(iota((lanes, slots), 0) == cell % lanes, 1.0, 0.0)
    place_ref[:rows] = dot(row.astype(bf16), route, (1, 1)).astype(bf16)
    place_ref[rows:] = dot(lane.astype(bf16), route, (1, 1)).astype(bf16)


def end_rows(layers, outs):
    rows, lanes = layers[0].shape
    low = iota((SUBLANES, lanes), 0) < STEPS
    last = [pltpu.roll(layer[rows - SUBLANES :], STEPS, 0) for layer in layers]
    picked = [jnp.where(low, a, pltpu.roll(b, STEPS, 0)) for a, b in (last, [layer[:SUBLANES] for layer in layers])]
    if outs == 1:
        picked = [jnp.where(lax.axis_index("sub") == 0, *picked)]
    return picked


def pack_tile_kernel(fields, ahead, behind, *ends):
    layers = fields.shape[1]
    for out, base, unused in ((ahead, layers - STEPS, 0), (behind, 0, STEPS - 1)):
        kept = [(at, k) for at in range(FIELDS) for k in range(STEPS) if at < 2 or k != unused]
        for entry, (at, k) in enumerate(kept):
            out[entry] = fields[at, base + k].astype(bf16)
    for at in range(FIELDS):
        for first in range(0, layers, STEPS):
            halves = [end_rows([fields[at, k], fields[at, k + 1]], len(ends)) for k in (first, first + 2)]
            for out, *value in zip(ends, *halves):
                out[at, first * STEPS : (first + STEPS) * STEPS, :] = jnp.concatenate(value, 0).astype(bf16)


def layer_beside(at, k, layers, tile_before, tile_after):
    side, depth, unused = (tile_before, k, 0) if k < STEPS else (tile_after, k - STEPS - layers, STEPS - 1)
    if at == 2 and depth == unused:
        return jnp.zeros(side.shape[1:], f32)
    return side[at * STEPS + depth - (at == 2 and unused == 0)].astype(f32)


def layer_of_block(at, k, fields, tile_before, tile_after):
    layers = fields.shape[1]
    if STEPS <= k < STEPS + layers:
        return fields[at, k - STEPS]
    return layer_beside(at, k, layers, tile_before, tile_after)


NEAR, NEXT = 4, 6


def beside_tile(nearest, outs):
    rows, lanes = nearest[0].shape
    row = iota((SUBLANES, lanes), 0)
    picked = []
    for pieces, rolls in (([a[rows - SUBLANES :] for a in nearest], (4, 6, 0)), ([a[:SUBLANES] for a in nearest], (0, 4, 6))):
        a, b, c = (pltpu.roll(piece, by, 0) if by else piece for piece, by in zip(pieces, rolls))
        picked.append(jnp.where(row < NEAR, a, jnp.where(row < NEXT, b, c)))
    if outs == 1:
        picked = [jnp.where(lax.axis_index("sub") == 0, *picked)]
    return picked


def pack_sub_kernel(sides, tile_before, tile_after, ready_ref, *rest):
    ends, outs = rest[:sides], rest[sides:]
    held = ends[0].shape[1]
    layers = held // STEPS
    for at in range(FIELDS):
        before = [layer_beside(at, STEPS - 1 - k, layers, tile_before, tile_after) for k in range(STEPS - 1)]
        after = [layer_beside(at, STEPS + layers + k, layers, tile_before, tile_after) for k in range(STEPS - 1)]
        for out, own, a, b in zip(outs, ends, beside_tile(before, sides), beside_tile(after, sides)):
            out[at, :held, :] = own[at]
            out[at, held:, :] = jnp.concatenate([a, b], 0).astype(bf16)


def side_rows(at, k, layers, after_ref, before_ref):
    own = k - STEPS
    if 0 <= own < layers:
        start, rolls = own // 2 * SUBLANES, ((0, 4), (4, 0))[own % 2]
    else:
        depth = -own if own < 0 else own - layers + 1
        if depth == STEPS:
            return jnp.zeros((SUBLANES, after_ref.shape[2]), f32)
        start, rolls = layers * STEPS + (own > 0) * SUBLANES, ((0, 4), (4, 2), (2, 0))[depth - 1]
    tile, half = start // (2 * SUBLANES) * 2 * SUBLANES, start % (2 * SUBLANES)
    after, before = (ref[at, tile : tile + 2 * SUBLANES, :].astype(f32)[half : half + SUBLANES] for ref in (after_ref, before_ref))
    after, before = (pltpu.roll(value, by, 0) if by else value for value, by in zip((after, before), rolls))
    me, count = lax.axis_index("sub"), lax.axis_size("sub")
    low = iota(after.shape, 0) < STEPS
    keep_after = jnp.where(me < count - 1, 1.0, 0.0)
    keep_before = jnp.where(me > 0, 1.0, 0.0)
    return jnp.where(low, after * keep_after, before * keep_before)


def pack_rep_kernel(fields, tile_before, tile_after, sub_after, sub_before, ready_ref, ends_ref):
    layers, rows, lanes = fields.shape[1:]
    beside = 2 * STEPS
    total = layers + 2 * STEPS
    layer_at = iota((rows + beside, lanes), 1) // beside
    for at in range(FIELDS):
        packed = jnp.zeros((rows + beside, lanes), f32)
        for k in range(total):
            here = layer_of_block(at, k, fields, tile_before, tile_after), side_rows(at, k, layers, sub_after, sub_before)
            here = pltpu.roll(jnp.concatenate(here, 0), (beside * k + STEPS) % lanes, 1)
            packed = jnp.where(layer_at == k, here, packed)
        ends_ref[at] = packed


def across(value):
    return pltpu.roll(value, 1, 0) + pltpu.roll(value, value.shape[0] - 1, 0)


def beside_lanes(value):
    lanes = value.shape[1]
    lane = iota(value.shape, 1)
    left = jnp.where(lane == 0, 0.0, pltpu.roll(value, 1, 1))
    right = jnp.where(lane == lanes - 1, 0.0, pltpu.roll(value, lanes - 1, 1))
    return left + right


def laplace(below, here, above):
    return below + above + across(here) + beside_lanes(here) - 6.0 * here


def row_masks(layers, rows, lanes):
    tile, sub = lax.axis_index("tile"), lax.axis_index("sub")
    keep_low, keep_high = jnp.where(tile > 0, 1.0, 0.0), jnp.where(tile < lax.axis_size("tile") - 1, 1.0, 0.0)
    keep_before, keep_after = jnp.where(sub > 0, 1.0, 0.0), jnp.where(sub < lax.axis_size("sub") - 1, 1.0, 0.0)
    row = iota((rows + 2 * STEPS, lanes), 0)
    inside = jnp.where(row < rows, 1.0, jnp.where(row < rows + STEPS, keep_after, keep_before))
    return inside * keep_low, inside, inside * keep_high


def assemble_kernel(
    fields, tile_before, tile_after, sub_after, sub_before, ready_ref, now, ago, coef, lapped, lapped_ago
):
    layers, rows, lanes = fields.shape[1:]
    total = layers + 2 * STEPS
    tile = lax.axis_index("tile")
    keep_low, keep_high = jnp.where(tile > 0, 1.0, 0.0), jnp.where(tile < lax.axis_size("tile") - 1, 1.0, 0.0)
    for at, out in enumerate((now, ago, coef)):
        extra = viscous if at == 2 else 0.0
        for k in range(total):
            keep = keep_low if k < STEPS else keep_high if k >= STEPS + layers else 1.0
            out[k, :rows] = layer_of_block(at, k, fields, tile_before, tile_after) * keep + extra
            out[k, rows:] = side_rows(at, k, layers, sub_after, sub_before) * keep + extra
    for value, out in ((now, lapped), (ago, lapped_ago)):
        for k in range(1, total - 1):
            out[k] = laplace(value[k - 1], value[k], value[k + 1])


def window_kernel(
    now_in, ago_in, coef, lapped_in, lapped_ago_in, ends_ref, rep_after, rep_before, place_ref, states, *rest
):
    *sends, now, ago, lapped = rest
    layers, rows, lanes = states.shape[1:]
    beside = 2 * STEPS
    total, wide_rows = now.shape[:2]
    rep, reps = lax.axis_index("rep"), lax.axis_size("rep")
    keep_left, keep_right = jnp.where(rep > 0, 1.0, 0.0), jnp.where(rep < reps - 1, 1.0, 0.0)
    inside_low, inside, inside_high = row_masks(layers, rows, lanes)

    lane = iota((wide_rows, lanes), 1)
    layer_of = lane // beside
    outer = lane % beside < STEPS
    ending = (lane == 0) | (lane == lanes - 1)
    inside_side = jnp.where(layer_of < STEPS, inside_low, jnp.where(layer_of < STEPS + layers, inside, inside_high))
    inside_side = jnp.where(layer_of < total, inside_side, 0.0)
    inside_left = inside_side * jnp.where(outer, keep_left, 1.0)
    inside_right = inside_side * jnp.where(outer, 1.0, keep_right)
    lefts, rights = [], []
    for at in range(FIELDS):
        extra = viscous if at == 2 else 0.0
        left = jnp.where(outer, rep_before[at], ends_ref[at])
        right = jnp.where(outer, ends_ref[at], rep_after[at])
        lefts.append(left * inside_left + extra)
        rights.append(right * inside_right + extra)
    left_now, left_ago, left_coef = lefts
    right_now, right_ago, right_coef = rights

    def edges(left, right):
        return jnp.where(outer, pltpu.roll(right, lanes - 1, 1), pltpu.roll(left, 1, 1))

    def edge_of(k, edge):
        return jnp.where(ending, pltpu.roll(edge, (lanes - beside * k - STEPS) % lanes, 1), 0.0)

    def laplace_side(side):
        beyond = pltpu.roll(side, beside, 1) + pltpu.roll(side, lanes - beside, 1)
        return beyond + across(side) + pltpu.roll(side, 1, 1) + pltpu.roll(side, lanes - 1, 1) - 6.0 * side

    def advance(here, before, gain, lap, lap_before, mask):
        change = here - before
        driving = gain * lap - lap_before + 2.0 * nonlinear * change * change
        return (here + change + (1.0 + 2.0 * nonlinear * here) * driving) * mask

    edge_ago = edges(left_ago, right_ago)
    left_lapped, right_lapped = viscous * laplace_side(left_ago), viscous * laplace_side(right_ago)

    cells = layers * rows
    slots = place_ref.shape[1]
    lane_of = place_ref[cells:]
    loads = jnp.zeros((SUBLANES, slots), f32)
    for step in range(STEPS):
        edge = edges(left_now, right_now)
        found = jnp.zeros((rows, slots), f32)
        source = now_in if step == 0 else now
        below, here = source[step], source[step + 1]
        for k in range(step + 1, total - step - 1):
            above = source[k + 1]
            if step == 0:
                lap, before = lapped_in[k], ago_in[k]
                lap_before = viscous * (lapped_ago_in[k] + edge_of(k, edge_ago))
            else:
                lap, before, lap_before = laplace(below, here, above), ago[k], lapped[k]
            lap = lap + edge_of(k, edge)
            mask = inside_low if k < STEPS else inside_high if k >= STEPS + layers else inside
            updated = advance(here, before, coef[k], lap, lap_before, mask)
            now[k] = updated
            ago[k] = here
            lapped[k] = viscous * lap
            own = k - STEPS
            if 0 <= own < layers:
                core = updated[:rows]
                row_of = place_ref[own * rows : (own + 1) * rows].astype(f32)
                found = found + dot(core.astype(bf16), lane_of, (1, 0)) * row_of
                if step >= STEPS - 2:
                    states[STEPS - 1 - step, own] = core
            below, here = here, above
        if step < STEPS - 1:
            lap = laplace_side(left_now)
            updated = advance(left_now, left_ago, left_coef, lap, left_lapped, inside_left)
            left_now, left_ago, left_lapped = updated, left_now, viscous * lap
            lap = laplace_side(right_now)
            updated = advance(right_now, right_ago, right_coef, lap, right_lapped, inside_right)
            right_now, right_ago, right_lapped = updated, right_now, viscous * lap
        loads = jnp.where(iota((SUBLANES, slots), 0) == step, jnp.sum(found, axis=0, keepdims=True), loads)

    size = slots // len(sends)
    for at, send in enumerate(sends):
        send[...] = loads[:STEPS, at * size : (at + 1) * size].astype(bf16)


def store_kernel(states, final_hbm, prior_hbm, sems):
    for copy in fetch(((states.at[0], final_hbm), (states.at[1], prior_hbm)), sems):
        copy.wait()


def turn_kernel(buckets, ready_ref, shapes_ref, area_ref, turned_ref, flipped_ref, area_out):
    total = shapes_ref.shape[0]
    bucket = total // buckets
    me = lax.axis_index("tile")
    if bucket % 16 == 0:
        for k in range(buckets):
            first = pl.multiple_of((me ^ k) * bucket, 16)
            turned_ref[k * bucket : (k + 1) * bucket, :] = shapes_ref[pl.ds(first, bucket), :]
            area = jnp.zeros((1, bucket), f32)
            for part in range(buckets):
                area = jnp.where((me ^ k) == part, area_ref[:, part * bucket : (part + 1) * bucket], area)
            area_out[:, k * bucket : (k + 1) * bucket] = area
    else:
        entry = iota((total, 1), 0)
        part = entry // bucket
        wanted = entry + ((part ^ me) - part) * bucket
        picks = jnp.where(iota((total, total), 1) == wanted, 1.0, 0.0)
        turned_ref[...] = dot(picks.astype(bf16), shapes_ref[...], (1, 0)).astype(bf16)
        area_out[...] = lax.dot_general(
            area_ref[...], picks, (((1,), (1,)), ((), ())), precision=lax.Precision.HIGHEST, preferred_element_type=f32
        )
    flipped_ref[...] = turned_ref[...].astype(f32).T.astype(bf16)


def project_kernel(order, area_ref, turned_ref, *rest):
    *parts, out_ref = rest
    size = parts[0].shape[1]
    forces = 0.0
    for at, part in zip(order, parts):
        weighted = (part[...].astype(f32) * area_ref[:, at * size : (at + 1) * size]).astype(bf16)
        forces = forces + dot(weighted, turned_ref[at * size : (at + 1) * size, :], (1, 0))
    out_ref[...] = forces


def respond_kernel(addends, freq_ref, damp_ref, start_ref, flipped_ref, *rest):
    forces_in, rest = rest[:addends], rest[addends:]
    state_ref, *sends, accel = rest
    forces = forces_in[0][...]
    for ref in forces_in[1:]:
        forces = forces + ref[...].astype(f32)
    frequency, damping = freq_ref[...], damp_ref[...]
    drag, stiffness = 2.0 * damping * frequency, frequency * frequency
    displace, velocity = start_ref[0:1, :], start_ref[1:2, :]
    accel[...] = jnp.zeros_like(accel)
    for step in range(STEPS):
        acceleration = forces[step : step + 1, :] - drag * velocity - stiffness * displace
        velocity = velocity + acceleration
        displace = displace + velocity
        accel[step : step + 1, :] = acceleration
    state_ref[0:1, :] = displace
    state_ref[1:2, :] = velocity
    node = dot(accel[...].astype(bf16), flipped_ref[...], (1, 0))
    size = node.shape[1] // len(sends)
    for at, send in enumerate(sends):
        send[...] = node[:STEPS, at * size : (at + 1) * size].astype(bf16)


def return_kernel(order, route_ref, *rest):
    *parts, out_ref = rest
    size = parts[0].shape[1]
    surface = 0.0
    for at, part in zip(order, parts):
        surface = surface + dot(part[...], route_ref[at * size : (at + 1) * size, :], (1, 0))
    out_ref[...] = surface.astype(bf16)


def exchange(parts, order, crossed):
    buckets = lax.axis_size("tile")
    if len(parts) == buckets:
        own = lax.ppermute(parts[0], "rep", swaps(2, 1)) if crossed else parts[0]
        return [send(parts[k], "tile", swaps(buckets, k), crossed) if k else own for k in order]
    tiles = jnp.arange(buckets) ^ lax.axis_index("tile")
    (whole,) = parts
    steps, total = whole.shape
    stacked = whole.reshape(steps, buckets, total // buckets).transpose(1, 0, 2)
    stacked = lax.all_to_all(stacked[tiles], "tile", 0, 0, tiled=True)
    return [stacked[tiles].transpose(1, 0, 2).reshape(steps, total)]


def body(
    pressure,
    previous_pressure,
    courant_square,
    node_area,
    mode_shapes,
    frequency,
    damping_ratio,
    modal_start,
    slot_cell,
    slot_owner,
    surface_count,
):
    buckets, subs, reps = (lax.axis_size(axis) for axis in ("tile", "sub", "rep"))
    layers, rows, lanes = pressure.shape
    slots = slot_cell.shape[-1]
    modes = mode_shapes.shape[1]
    bucket = slots // buckets
    parts = buckets if buckets in (2, 4) and bucket % 16 == 0 else 1
    total = layers + 2 * STEPS
    wide_rows = rows + 2 * STEPS
    crossed = parts > 1 and reps == 2
    if crossed:
        mode_shapes, node_area = (lax.ppermute(value, "rep", swaps(2, 1)) for value in (mode_shapes, node_area))

    cells = layers * rows
    fields = jnp.stack([pressure, previous_pressure, courant_square])
    sides = 1 if subs == 2 else 2
    slab = shape_of((FIELDS * STEPS - 1, rows, lanes), bf16)
    held = shape_of((FIELDS, layers * STEPS, lanes), bf16)
    ahead, behind, *ends = call(pack_tile_kernel, (slab, slab) + (held,) * sides, (fields,))
    route, place = call(
        functools.partial(route_kernel, buckets, lanes, cells),
        (shape_of((slots, slots), bf16), shape_of((cells + lanes, slots), bf16)),
        (ahead, slot_owner.reshape(1, slots), slot_cell.reshape(1, slots), surface_count.reshape(1, 1)),
    )
    two = reps == 2
    tile_halo = [send(value, "tile", shift(buckets, by), two) for value, by in ((ahead, 1), (behind, -1))]
    if two:
        ends = [lax.ppermute(value, "rep", swaps(2, 1)) for value in ends]
    slab = shape_of((FIELDS, layers * STEPS + 2 * SUBLANES, lanes), bf16)
    packed = call(functools.partial(pack_sub_kernel, sides), (slab,) * sides, (*tile_halo, route, *ends))
    if sides == 1:
        sub_halo = (send(packed[0], "sub", swaps(2, 1), two),) * 2
    else:
        sub_halo = both_ways("sub", *packed, two)
    if two:
        tile_halo = [lax.ppermute(value, "rep", swaps(2, 1)) for value in tile_halo]

    turned, flipped, area = call(
        functools.partial(turn_kernel, buckets),
        (shape_of(mode_shapes.shape, bf16), shape_of(mode_shapes.shape[::-1], bf16), shape_of((1, slots), f32)),
        (packed[0], mode_shapes, node_area.reshape(1, slots)),
    )

    ends = call(
        pack_rep_kernel,
        shape_of((FIELDS, wide_rows, lanes), f32),
        (fields, *tile_halo, *sub_halo, area),
    )
    if reps == 2:
        rep_halo = (lax.ppermute(ends, "rep", swaps(2, 1)),) * 2
    else:
        rep_halo = both_ways("rep", ends, ends)

    wide = shape_of((total, wide_rows, lanes), f32)
    assembled = call(assemble_kernel, (wide,) * 5, (fields, *tile_halo, *sub_halo, ends))
    wide = pltpu.VMEM(wide.shape, f32)
    part = shape_of((STEPS, slots // parts), bf16)
    block = shape_of(pressure.shape, f32)
    states, *sends = call(
        window_kernel,
        (shape_of((2, layers, rows, lanes), f32),) + (part,) * parts,
        (*assembled, ends, *rep_halo, place),
        scratch=[wide] * 3,
        micros=2.0,
    )
    final_field, prior_field = call(
        store_kernel, (block, block), (states,), out_specs=(HBM, HBM), scratch=[pltpu.SemaphoreType.DMA((2,))]
    )

    order = [k for k in (0, 2, 3, 1) if k < parts]
    forces = call(
        functools.partial(project_kernel, order),
        shape_of((STEPS, modes), f32),
        (area, turned, *exchange(sends, order, crossed)),
    )
    addends = [forces]
    for axis in ("rep", "sub", "tile"):
        count = lax.axis_size(axis)
        forces = functools.reduce(jnp.add, addends)
        if count in (2, 4):
            sent = forces.astype(bf16) if axis != "rep" else forces
            places = [swaps(count, k) for k in (2, 3, 1) if k < count]
            addends = [forces] + [send(sent, axis, swap, reps == 2 and axis != "rep") for swap in places]
        else:
            addends = [lax.psum(forces, axis)]

    state, *sends = call(
        functools.partial(respond_kernel, len(addends)),
        (shape_of((2, modes), f32),) + (part,) * parts,
        (frequency.reshape(1, modes), damping_ratio.reshape(1, modes), modal_start, flipped, *addends),
        scratch=[pltpu.VMEM((SUBLANES, modes), f32)],
    )
    share = modes // (buckets * subs * reps)
    modal_state = lax.dynamic_slice_in_dim(state, lax.axis_index(("tile", "sub", "rep")) * share, share, 1)
    order = [k for k in (3, 2, 1, 0) if k < parts]
    surface = call(
        functools.partial(return_kernel, order), shape_of((STEPS, slots), bf16), (route, *exchange(sends, order, crossed))
    )
    return (final_field, prior_field, surface.reshape(1, 1, 1, STEPS, slots), modal_state)


def solution(mesh):
    in_specs = (
        P(("groups", "tile"), "sub", "rep"),
        P(("groups", "tile"), "sub", "rep"),
        P(("groups", "tile"), "sub", "rep"),
        P(("groups", "tile", "sub", "rep")),
        P(("groups", "tile", "sub", "rep"), None),
        P("groups"),
        P("groups"),
        P(None, "groups"),
        P(("groups", "tile"), "sub", "rep", None),
        P(("groups", "tile"), "sub", "rep", None, None),
        P(("groups", "sub"), "rep", "tile"),
    )
    out_specs = (
        P(("groups", "tile"), "sub", "rep"),
        P(("groups", "tile"), "sub", "rep"),
        P(("groups", "tile"), "sub", "rep", None, None),
        P(None, ("groups", "tile", "sub", "rep")),
    )
    return jax.shard_map(body, mesh=mesh, in_specs=in_specs, out_specs=out_specs, check_vma=False)
```

```python
import functools

import jax
import jax.numpy as jnp
from jax import lax
from jax.experimental import pallas as pl
from jax.experimental.pallas import tpu as pltpu
from jax.sharding import PartitionSpec as P

STEPS = 4
FIELDS = 3
SUBLANES = 8

nonlinear = 0.03
viscous = 0.02

f32 = jnp.float32
bf16 = jnp.bfloat16
VMEM = pl.BlockSpec(memory_space=pltpu.VMEM)
HBM = pl.BlockSpec(memory_space=pltpu.HBM)


def shift(count, by):
    return [(i, (i + by) % count) for i in range(count)]


def line(count, by):
    return [(i, i + by) for i in range(count) if 0 <= i + by < count]


def swaps(count, by):
    return [(i, i ^ by) for i in range(count)]


def iota(shape, dim):
    return lax.broadcasted_iota(jnp.int32, shape, dim)


def dot(a, b, contract):
    return lax.dot_general(a, b, (((contract[0],), (contract[1],)), ((), ())), preferred_element_type=f32)


def call(kernel, out_shape, inputs, scratch=(), specs=None, out_specs=None, micros=1.0, vmem=32):
    return pl.pallas_call(
        kernel,
        out_shape=out_shape,
        in_specs=specs or [VMEM] * len(inputs),
        out_specs=out_specs or jax.tree.map(lambda _: VMEM, out_shape),
        scratch_shapes=list(scratch),
        cost_estimate=pl.CostEstimate(flops=int(micros * 1e9), bytes_accessed=0, transcendentals=0),
        compiler_params=pltpu.CompilerParams(vmem_limit_bytes=vmem * 1024 * 1024),
    )(*inputs)


def shape_of(dims, dtype):
    return jax.ShapeDtypeStruct(dims, dtype)


def fetch(pairs, sems):
    copies = [pltpu.make_async_copy(a, b, sems.at[i]) for i, (a, b) in enumerate(pairs)]
    for copy in copies:
        copy.start()
    return copies


def send(value, axis, places, crossed):
    if not crossed:
        return lax.ppermute(value, axis, places)
    return lax.ppermute(value, (axis, "rep"), [(2 * i + r, 2 * j + 1 - r) for i, j in places for r in range(2)])


def both_ways(axis, ahead, behind, crossed=False):
    count = lax.axis_size(axis)
    after = send(behind, axis, line(count, -1), crossed)
    before = send(ahead, axis, line(count, 1), crossed)
    return after, before


def route_kernel(buckets, lanes, rows, after_ref, owner_ref, cell_ref, count_ref, route_ref, place_ref):
    slots = owner_ref.shape[1]
    bucket = slots // buckets
    me = lax.axis_index("tile")
    owner = owner_ref[...]
    live = iota((1, slots), 1) < count_ref[...]
    held = -(-buckets // SUBLANES) * SUBLANES
    member = jnp.where((iota((held, slots), 0) == owner) & live, 1.0, 0.0)
    earlier = jnp.where(iota((slots, slots), 0) < iota((slots, slots), 1), 1.0, 0.0).astype(bf16)
    before = dot(member.astype(bf16), earlier, (1, 0))
    rank = jnp.sum(before * member, axis=0, keepdims=True).astype(jnp.int32)
    target = jnp.where(live, (owner ^ me) * bucket + rank, -1)
    route = jnp.where(iota((slots, slots), 0) == target, 1.0, 0.0).astype(bf16)
    route_ref[...] = route
    cell = cell_ref[...]
    row = jnp.where(iota((rows, slots), 0) == cell // lanes, 1.0, 0.0)
    lane = jnp.where(iota((lanes, slots), 0) == cell % lanes, 1.0, 0.0)
    place_ref[:rows] = dot(row.astype(bf16), route, (1, 1)).astype(bf16)
    place_ref[rows:] = dot(lane.astype(bf16), route, (1, 1)).astype(bf16)


def end_rows(layers, outs):
    rows, lanes = layers[0].shape
    low = iota((SUBLANES, lanes), 0) < STEPS
    last = [pltpu.roll(layer[rows - SUBLANES :], STEPS, 0) for layer in layers]
    picked = [jnp.where(low, a, pltpu.roll(b, STEPS, 0)) for a, b in (last, [layer[:SUBLANES] for layer in layers])]
    if outs == 1:
        picked = [jnp.where(lax.axis_index("sub") == 0, *picked)]
    return picked


def pack_tile_kernel(fields, ahead, behind, *ends):
    layers = fields.shape[1]
    for out, base, unused in ((ahead, layers - STEPS, 0), (behind, 0, STEPS - 1)):
        kept = [(at, k) for at in range(FIELDS) for k in range(STEPS) if at < 2 or k != unused]
        for entry, (at, k) in enumerate(kept):
            out[entry] = fields[at, base + k].astype(bf16)
    for at in range(FIELDS):
        for first in range(0, layers, STEPS):
            halves = [end_rows([fields[at, k], fields[at, k + 1]], len(ends)) for k in (first, first + 2)]
            for out, *value in zip(ends, *halves):
                out[at, first * STEPS : (first + STEPS) * STEPS, :] = jnp.concatenate(value, 0).astype(bf16)


def layer_beside(at, k, layers, tile_before, tile_after):
    side, depth, unused = (tile_before, k, 0) if k < STEPS else (tile_after, k - STEPS - layers, STEPS - 1)
    if at == 2 and depth == unused:
        return jnp.zeros(side.shape[1:], f32)
    return side[at * STEPS + depth - (at == 2 and unused == 0)].astype(f32)


def layer_of_block(at, k, fields, tile_before, tile_after):
    layers = fields.shape[1]
    if STEPS <= k < STEPS + layers:
        return fields[at, k - STEPS]
    return layer_beside(at, k, layers, tile_before, tile_after)


NEAR, NEXT = 4, 6


def beside_tile(nearest, outs):
    rows, lanes = nearest[0].shape
    row = iota((SUBLANES, lanes), 0)
    picked = []
    for pieces, rolls in (([a[rows - SUBLANES :] for a in nearest], (4, 6, 0)), ([a[:SUBLANES] for a in nearest], (0, 4, 6))):
        a, b, c = (pltpu.roll(piece, by, 0) if by else piece for piece, by in zip(pieces, rolls))
        picked.append(jnp.where(row < NEAR, a, jnp.where(row < NEXT, b, c)))
    if outs == 1:
        picked = [jnp.where(lax.axis_index("sub") == 0, *picked)]
    return picked


def pack_sub_kernel(sides, tile_before, tile_after, ready_ref, *rest):
    ends, outs = rest[:sides], rest[sides:]
    held = ends[0].shape[1]
    layers = held // STEPS
    for at in range(FIELDS):
        before = [layer_beside(at, STEPS - 1 - k, layers, tile_before, tile_after) for k in range(STEPS - 1)]
        after = [layer_beside(at, STEPS + layers + k, layers, tile_before, tile_after) for k in range(STEPS - 1)]
        for out, own, a, b in zip(outs, ends, beside_tile(before, sides), beside_tile(after, sides)):
            out[at, :held, :] = own[at]
            out[at, held:, :] = jnp.concatenate([a, b], 0).astype(bf16)


def side_rows(at, k, layers, after_ref, before_ref):
    own = k - STEPS
    if 0 <= own < layers:
        start, rolls = own // 2 * SUBLANES, ((0, 4), (4, 0))[own % 2]
    else:
        depth = -own if own < 0 else own - layers + 1
        if depth == STEPS:
            return jnp.zeros((SUBLANES, after_ref.shape[2]), f32)
        start, rolls = layers * STEPS + (own > 0) * SUBLANES, ((0, 4), (4, 2), (2, 0))[depth - 1]
    tile, half = start // (2 * SUBLANES) * 2 * SUBLANES, start % (2 * SUBLANES)
    after, before = (ref[at, tile : tile + 2 * SUBLANES, :].astype(f32)[half : half + SUBLANES] for ref in (after_ref, before_ref))
    after, before = (pltpu.roll(value, by, 0) if by else value for value, by in zip((after, before), rolls))
    me, count = lax.axis_index("sub"), lax.axis_size("sub")
    low = iota(after.shape, 0) < STEPS
    keep_after = jnp.where(me < count - 1, 1.0, 0.0)
    keep_before = jnp.where(me > 0, 1.0, 0.0)
    return jnp.where(low, after * keep_after, before * keep_before)


def pack_rep_kernel(fields, tile_before, tile_after, sub_after, sub_before, ready_ref, ends_ref):
    layers, rows, lanes = fields.shape[1:]
    beside = 2 * STEPS
    total = layers + 2 * STEPS
    layer_at = iota((rows + beside, lanes), 1) // beside
    for at in range(FIELDS):
        packed = jnp.zeros((rows + beside, lanes), f32)
        for k in range(total):
            here = layer_of_block(at, k, fields, tile_before, tile_after), side_rows(at, k, layers, sub_after, sub_before)
            here = pltpu.roll(jnp.concatenate(here, 0), (beside * k + STEPS) % lanes, 1)
            packed = jnp.where(layer_at == k, here, packed)
        ends_ref[at] = packed


def across(value):
    return pltpu.roll(value, 1, 0) + pltpu.roll(value, value.shape[0] - 1, 0)


def beside_lanes(value):
    lanes = value.shape[1]
    lane = iota(value.shape, 1)
    left = jnp.where(lane == 0, 0.0, pltpu.roll(value, 1, 1))
    right = jnp.where(lane == lanes - 1, 0.0, pltpu.roll(value, lanes - 1, 1))
    return left + right


def laplace(below, here, above):
    return below + above + across(here) + beside_lanes(here) - 6.0 * here


def row_masks(layers, rows, lanes):
    tile, sub = lax.axis_index("tile"), lax.axis_index("sub")
    keep_low, keep_high = jnp.where(tile > 0, 1.0, 0.0), jnp.where(tile < lax.axis_size("tile") - 1, 1.0, 0.0)
    keep_before, keep_after = jnp.where(sub > 0, 1.0, 0.0), jnp.where(sub < lax.axis_size("sub") - 1, 1.0, 0.0)
    row = iota((rows + 2 * STEPS, lanes), 0)
    inside = jnp.where(row < rows, 1.0, jnp.where(row < rows + STEPS, keep_after, keep_before))
    return inside * keep_low, inside, inside * keep_high


def assemble_kernel(
    fields, tile_before, tile_after, sub_after, sub_before, ready_ref, now, ago, coef, lapped, lapped_ago
):
    layers, rows, lanes = fields.shape[1:]
    total = layers + 2 * STEPS
    tile = lax.axis_index("tile")
    keep_low, keep_high = jnp.where(tile > 0, 1.0, 0.0), jnp.where(tile < lax.axis_size("tile") - 1, 1.0, 0.0)
    for at, out in enumerate((now, ago, coef)):
        extra = viscous if at == 2 else 0.0
        for k in range(total):
            keep = keep_low if k < STEPS else keep_high if k >= STEPS + layers else 1.0
            out[k, :rows] = layer_of_block(at, k, fields, tile_before, tile_after) * keep + extra
            out[k, rows:] = side_rows(at, k, layers, sub_after, sub_before) * keep + extra
    for value, out in ((now, lapped), (ago, lapped_ago)):
        for k in range(1, total - 1):
            out[k] = laplace(value[k - 1], value[k], value[k + 1])


def window_kernel(
    now_in, ago_in, coef, lapped_in, lapped_ago_in, ends_ref, rep_after, rep_before, place_ref, states, *rest
):
    *sends, now, ago, lapped = rest
    layers, rows, lanes = states.shape[1:]
    beside = 2 * STEPS
    total, wide_rows = now.shape[:2]
    rep, reps = lax.axis_index("rep"), lax.axis_size("rep")
    keep_left, keep_right = jnp.where(rep > 0, 1.0, 0.0), jnp.where(rep < reps - 1, 1.0, 0.0)
    inside_low, inside, inside_high = row_masks(layers, rows, lanes)

    lane = iota((wide_rows, lanes), 1)
    layer_of = lane // beside
    outer = lane % beside < STEPS
    ending = (lane == 0) | (lane == lanes - 1)
    inside_side = jnp.where(layer_of < STEPS, inside_low, jnp.where(layer_of < STEPS + layers, inside, inside_high))
    inside_side = jnp.where(layer_of < total, inside_side, 0.0)
    inside_left = inside_side * jnp.where(outer, keep_left, 1.0)
    inside_right = inside_side * jnp.where(outer, 1.0, keep_right)
    lefts, rights = [], []
    for at in range(FIELDS):
        extra = viscous if at == 2 else 0.0
        left = jnp.where(outer, rep_before[at], ends_ref[at])
        right = jnp.where(outer, ends_ref[at], rep_after[at])
        lefts.append(left * inside_left + extra)
        rights.append(right * inside_right + extra)
    left_now, left_ago, left_coef = lefts
    right_now, right_ago, right_coef = rights

    def edges(left, right):
        return jnp.where(outer, pltpu.roll(right, lanes - 1, 1), pltpu.roll(left, 1, 1))

    def edge_of(k, edge):
        return jnp.where(ending, pltpu.roll(edge, (lanes - beside * k - STEPS) % lanes, 1), 0.0)

    def laplace_side(side):
        beyond = pltpu.roll(side, beside, 1) + pltpu.roll(side, lanes - beside, 1)
        return beyond + across(side) + pltpu.roll(side, 1, 1) + pltpu.roll(side, lanes - 1, 1) - 6.0 * side

    def advance(here, before, gain, lap, lap_before, mask):
        change = here - before
        driving = gain * lap - lap_before + 2.0 * nonlinear * change * change
        return (here + change + (1.0 + 2.0 * nonlinear * here) * driving) * mask

    edge_ago = edges(left_ago, right_ago)
    left_lapped, right_lapped = viscous * laplace_side(left_ago), viscous * laplace_side(right_ago)

    cells = layers * rows
    slots = place_ref.shape[1]
    lane_of = place_ref[cells:]
    loads = jnp.zeros((SUBLANES, slots), f32)
    for step in range(STEPS):
        edge = edges(left_now, right_now)
        found = jnp.zeros((rows, slots), f32)
        source = now_in if step == 0 else now
        below, here = source[step], source[step + 1]
        for k in range(step + 1, total - step - 1):
            above = source[k + 1]
            if step == 0:
                lap, before = lapped_in[k], ago_in[k]
                lap_before = viscous * (lapped_ago_in[k] + edge_of(k, edge_ago))
            else:
                lap, before, lap_before = laplace(below, here, above), ago[k], lapped[k]
            lap = lap + edge_of(k, edge)
            mask = inside_low if k < STEPS else inside_high if k >= STEPS + layers else inside
            updated = advance(here, before, coef[k], lap, lap_before, mask)
            if step < STEPS - 1:
                now[k] = updated
                ago[k] = here
                lapped[k] = viscous * lap
            own = k - STEPS
            if 0 <= own < layers:
                core = updated[:rows]
                row_of = place_ref[own * rows : (own + 1) * rows].astype(f32)
                found = found + dot(core.astype(bf16), lane_of, (1, 0)) * row_of
                if step >= STEPS - 2:
                    states[STEPS - 1 - step, own] = core
            below, here = here, above
        if step < STEPS - 1:
            lap = laplace_side(left_now)
            updated = advance(left_now, left_ago, left_coef, lap, left_lapped, inside_left)
            left_now, left_ago, left_lapped = updated, left_now, viscous * lap
            lap = laplace_side(right_now)
            updated = advance(right_now, right_ago, right_coef, lap, right_lapped, inside_right)
            right_now, right_ago, right_lapped = updated, right_now, viscous * lap
        loads = jnp.where(iota((SUBLANES, slots), 0) == step, jnp.sum(found, axis=0, keepdims=True), loads)

    size = slots // len(sends)
    for at, send in enumerate(sends):
        send[...] = loads[:STEPS, at * size : (at + 1) * size].astype(bf16)


def store_kernel(states, final_hbm, prior_hbm, sems):
    for copy in fetch(((states.at[0], final_hbm), (states.at[1], prior_hbm)), sems):
        copy.wait()


def turn_kernel(buckets, ready_ref, shapes_ref, area_ref, turned_ref, flipped_ref, area_out):
    total = shapes_ref.shape[0]
    bucket = total // buckets
    me = lax.axis_index("tile")
    if bucket % 16 == 0:
        for k in range(buckets):
            first = pl.multiple_of((me ^ k) * bucket, 16)
            turned_ref[k * bucket : (k + 1) * bucket, :] = shapes_ref[pl.ds(first, bucket), :]
            area = jnp.zeros((1, bucket), f32)
            for part in range(buckets):
                area = jnp.where((me ^ k) == part, area_ref[:, part * bucket : (part + 1) * bucket], area)
            area_out[:, k * bucket : (k + 1) * bucket] = area
    else:
        entry = iota((total, 1), 0)
        part = entry // bucket
        wanted = entry + ((part ^ me) - part) * bucket
        picks = jnp.where(iota((total, total), 1) == wanted, 1.0, 0.0)
        turned_ref[...] = dot(picks.astype(bf16), shapes_ref[...], (1, 0)).astype(bf16)
        area_out[...] = lax.dot_general(
            area_ref[...], picks, (((1,), (1,)), ((), ())), precision=lax.Precision.HIGHEST, preferred_element_type=f32
        )
    flipped_ref[...] = turned_ref[...].astype(f32).T.astype(bf16)


def project_kernel(order, area_ref, turned_ref, *rest):
    *parts, out_ref = rest
    size = parts[0].shape[1]
    forces = 0.0
    for at, part in zip(order, parts):
        weighted = (part[...].astype(f32) * area_ref[:, at * size : (at + 1) * size]).astype(bf16)
        forces = forces + dot(weighted, turned_ref[at * size : (at + 1) * size, :], (1, 0))
    out_ref[...] = forces


def respond_kernel(addends, freq_ref, damp_ref, start_ref, flipped_ref, *rest):
    forces_in, rest = rest[:addends], rest[addends:]
    state_ref, *sends, accel = rest
    forces = forces_in[0][...]
    for ref in forces_in[1:]:
        forces = forces + ref[...].astype(f32)
    frequency, damping = freq_ref[...], damp_ref[...]
    drag, stiffness = 2.0 * damping * frequency, frequency * frequency
    displace, velocity = start_ref[0:1, :], start_ref[1:2, :]
    accel[...] = jnp.zeros_like(accel)
    for step in range(STEPS):
        acceleration = forces[step : step + 1, :] - drag * velocity - stiffness * displace
        velocity = velocity + acceleration
        displace = displace + velocity
        accel[step : step + 1, :] = acceleration
    state_ref[0:1, :] = displace
    state_ref[1:2, :] = velocity
    node = dot(accel[...].astype(bf16), flipped_ref[...], (1, 0))
    size = node.shape[1] // len(sends)
    for at, send in enumerate(sends):
        send[...] = node[:STEPS, at * size : (at + 1) * size].astype(bf16)


def return_kernel(order, route_ref, *rest):
    *parts, out_ref = rest
    size = parts[0].shape[1]
    surface = 0.0
    for at, part in zip(order, parts):
        surface = surface + dot(part[...], route_ref[at * size : (at + 1) * size, :], (1, 0))
    out_ref[...] = surface.astype(bf16)


def exchange(parts, order, crossed):
    buckets = lax.axis_size("tile")
    if len(parts) == buckets:
        own = lax.ppermute(parts[0], "rep", swaps(2, 1)) if crossed else parts[0]
        return [send(parts[k], "tile", swaps(buckets, k), crossed) if k else own for k in order]
    tiles = jnp.arange(buckets) ^ lax.axis_index("tile")
    (whole,) = parts
    steps, total = whole.shape
    stacked = whole.reshape(steps, buckets, total // buckets).transpose(1, 0, 2)
    stacked = lax.all_to_all(stacked[tiles], "tile", 0, 0, tiled=True)
    return [stacked[tiles].transpose(1, 0, 2).reshape(steps, total)]


def body(
    pressure,
    previous_pressure,
    courant_square,
    node_area,
    mode_shapes,
    frequency,
    damping_ratio,
    modal_start,
    slot_cell,
    slot_owner,
    surface_count,
):
    buckets, subs, reps = (lax.axis_size(axis) for axis in ("tile", "sub", "rep"))
    layers, rows, lanes = pressure.shape
    slots = slot_cell.shape[-1]
    modes = mode_shapes.shape[1]
    bucket = slots // buckets
    parts = buckets if buckets in (2, 4) and bucket % 16 == 0 else 1
    total = layers + 2 * STEPS
    wide_rows = rows + 2 * STEPS
    crossed = parts > 1 and reps == 2
    if crossed:
        mode_shapes, node_area = (lax.ppermute(value, "rep", swaps(2, 1)) for value in (mode_shapes, node_area))

    cells = layers * rows
    fields = jnp.stack([pressure, previous_pressure, courant_square])
    sides = 1 if subs == 2 else 2
    slab = shape_of((FIELDS * STEPS - 1, rows, lanes), bf16)
    held = shape_of((FIELDS, layers * STEPS, lanes), bf16)
    ahead, behind, *ends = call(pack_tile_kernel, (slab, slab) + (held,) * sides, (fields,))
    route, place = call(
        functools.partial(route_kernel, buckets, lanes, cells),
        (shape_of((slots, slots), bf16), shape_of((cells + lanes, slots), bf16)),
        (ahead, slot_owner.reshape(1, slots), slot_cell.reshape(1, slots), surface_count.reshape(1, 1)),
    )
    two = reps == 2
    tile_halo = [send(value, "tile", shift(buckets, by), two) for value, by in ((ahead, 1), (behind, -1))]
    if two:
        ends = [lax.ppermute(value, "rep", swaps(2, 1)) for value in ends]
    slab = shape_of((FIELDS, layers * STEPS + 2 * SUBLANES, lanes), bf16)
    packed = call(functools.partial(pack_sub_kernel, sides), (slab,) * sides, (*tile_halo, route, *ends))
    if sides == 1:
        sub_halo = (send(packed[0], "sub", swaps(2, 1), two),) * 2
    else:
        sub_halo = both_ways("sub", *packed, two)
    if two:
        tile_halo = [lax.ppermute(value, "rep", swaps(2, 1)) for value in tile_halo]

    turned, flipped, area = call(
        functools.partial(turn_kernel, buckets),
        (shape_of(mode_shapes.shape, bf16), shape_of(mode_shapes.shape[::-1], bf16), shape_of((1, slots), f32)),
        (packed[0], mode_shapes, node_area.reshape(1, slots)),
    )

    ends = call(
        pack_rep_kernel,
        shape_of((FIELDS, wide_rows, lanes), f32),
        (fields, *tile_halo, *sub_halo, area),
    )
    if reps == 2:
        rep_halo = (lax.ppermute(ends, "rep", swaps(2, 1)),) * 2
    else:
        rep_halo = both_ways("rep", ends, ends)

    wide = shape_of((total, wide_rows, lanes), f32)
    assembled = call(assemble_kernel, (wide,) * 5, (fields, *tile_halo, *sub_halo, ends))
    wide = pltpu.VMEM(wide.shape, f32)
    part = shape_of((STEPS, slots // parts), bf16)
    block = shape_of(pressure.shape, f32)
    states, *sends = call(
        window_kernel,
        (shape_of((2, layers, rows, lanes), f32),) + (part,) * parts,
        (*assembled, ends, *rep_halo, place),
        scratch=[wide] * 3,
        micros=2.0,
    )
    final_field, prior_field = call(
        store_kernel, (block, block), (states,), out_specs=(HBM, HBM), scratch=[pltpu.SemaphoreType.DMA((2,))]
    )

    order = [k for k in (0, 2, 3, 1) if k < parts]
    forces = call(
        functools.partial(project_kernel, order),
        shape_of((STEPS, modes), f32),
        (area, turned, *exchange(sends, order, crossed)),
    )
    addends = [forces]
    for axis in ("rep", "sub", "tile"):
        count = lax.axis_size(axis)
        forces = functools.reduce(jnp.add, addends)
        if count in (2, 4):
            sent = forces.astype(bf16) if axis != "rep" else forces
            places = [swaps(count, k) for k in (2, 3, 1) if k < count]
            addends = [forces] + [send(sent, axis, swap, reps == 2 and axis != "rep") for swap in places]
        else:
            addends = [lax.psum(forces, axis)]

    state, *sends = call(
        functools.partial(respond_kernel, len(addends)),
        (shape_of((2, modes), f32),) + (part,) * parts,
        (frequency.reshape(1, modes), damping_ratio.reshape(1, modes), modal_start, flipped, *addends),
        scratch=[pltpu.VMEM((SUBLANES, modes), f32)],
    )
    share = modes // (buckets * subs * reps)
    modal_state = lax.dynamic_slice_in_dim(state, lax.axis_index(("tile", "sub", "rep")) * share, share, 1)
    order = [k for k in (2, 3, 1, 0) if k < parts]
    surface = call(
        functools.partial(return_kernel, order), shape_of((STEPS, slots), bf16), (route, *exchange(sends, order, crossed))
    )
    return (final_field, prior_field, surface.reshape(1, 1, 1, STEPS, slots), modal_state)


def solution(mesh):
    in_specs = (
        P(("groups", "tile"), "sub", "rep"),
        P(("groups", "tile"), "sub", "rep"),
        P(("groups", "tile"), "sub", "rep"),
        P(("groups", "tile", "sub", "rep")),
        P(("groups", "tile", "sub", "rep"), None),
        P("groups"),
        P("groups"),
        P(None, "groups"),
        P(("groups", "tile"), "sub", "rep", None),
        P(("groups", "tile"), "sub", "rep", None, None),
        P(("groups", "sub"), "rep", "tile"),
    )
    out_specs = (
        P(("groups", "tile"), "sub", "rep"),
        P(("groups", "tile"), "sub", "rep"),
        P(("groups", "tile"), "sub", "rep", None, None),
        P(None, ("groups", "tile", "sub", "rep")),
    )
    return jax.shard_map(body, mesh=mesh, in_specs=in_specs, out_specs=out_specs, check_vma=False)
```

```python
import functools

import jax
import jax.numpy as jnp
from jax import lax
from jax.experimental import pallas as pl
from jax.experimental.pallas import tpu as pltpu
from jax.sharding import PartitionSpec as P

STEPS = 4
FIELDS = 3
SUBLANES = 8

nonlinear = 0.03
viscous = 0.02

f32 = jnp.float32
bf16 = jnp.bfloat16
VMEM = pl.BlockSpec(memory_space=pltpu.VMEM)
HBM = pl.BlockSpec(memory_space=pltpu.HBM)


def shift(count, by):
    return [(i, (i + by) % count) for i in range(count)]


def line(count, by):
    return [(i, i + by) for i in range(count) if 0 <= i + by < count]


def swaps(count, by):
    return [(i, i ^ by) for i in range(count)]


def iota(shape, dim):
    return lax.broadcasted_iota(jnp.int32, shape, dim)


def dot(a, b, contract):
    return lax.dot_general(a, b, (((contract[0],), (contract[1],)), ((), ())), preferred_element_type=f32)


def call(kernel, out_shape, inputs, scratch=(), specs=None, out_specs=None, micros=1.0, vmem=32):
    return pl.pallas_call(
        kernel,
        out_shape=out_shape,
        in_specs=specs or [VMEM] * len(inputs),
        out_specs=out_specs or jax.tree.map(lambda _: VMEM, out_shape),
        scratch_shapes=list(scratch),
        cost_estimate=pl.CostEstimate(flops=int(micros * 1e9), bytes_accessed=0, transcendentals=0),
        compiler_params=pltpu.CompilerParams(vmem_limit_bytes=vmem * 1024 * 1024),
    )(*inputs)


def shape_of(dims, dtype):
    return jax.ShapeDtypeStruct(dims, dtype)


def fetch(pairs, sems):
    copies = [pltpu.make_async_copy(a, b, sems.at[i]) for i, (a, b) in enumerate(pairs)]
    for copy in copies:
        copy.start()
    return copies


def send(value, axis, places, crossed):
    if not crossed:
        return lax.ppermute(value, axis, places)
    return lax.ppermute(value, (axis, "rep"), [(2 * i + r, 2 * j + 1 - r) for i, j in places for r in range(2)])


def both_ways(axis, ahead, behind, crossed=False):
    count = lax.axis_size(axis)
    after = send(behind, axis, line(count, -1), crossed)
    before = send(ahead, axis, line(count, 1), crossed)
    return after, before


def route_kernel(buckets, lanes, rows, after_ref, owner_ref, cell_ref, count_ref, route_ref, place_ref):
    slots = owner_ref.shape[1]
    bucket = slots // buckets
    me = lax.axis_index("tile")
    owner = owner_ref[...]
    live = iota((1, slots), 1) < count_ref[...]
    held = -(-buckets // SUBLANES) * SUBLANES
    member = jnp.where((iota((held, slots), 0) == owner) & live, 1.0, 0.0)
    earlier = jnp.where(iota((slots, slots), 0) < iota((slots, slots), 1), 1.0, 0.0).astype(bf16)
    before = dot(member.astype(bf16), earlier, (1, 0))
    rank = jnp.sum(before * member, axis=0, keepdims=True).astype(jnp.int32)
    target = jnp.where(live, (owner ^ me) * bucket + rank, -1)
    route = jnp.where(iota((slots, slots), 0) == target, 1.0, 0.0).astype(bf16)
    route_ref[...] = route
    cell = cell_ref[...]
    row = jnp.where(iota((rows, slots), 0) == cell // lanes, 1.0, 0.0)
    lane = jnp.where(iota((lanes, slots), 0) == cell % lanes, 1.0, 0.0)
    place_ref[:rows] = dot(row.astype(bf16), route, (1, 1)).astype(bf16)
    place_ref[rows:] = dot(lane.astype(bf16), route, (1, 1)).astype(bf16)


def end_rows(layers, outs):
    rows, lanes = layers[0].shape
    low = iota((SUBLANES, lanes), 0) < STEPS
    last = [pltpu.roll(layer[rows - SUBLANES :], STEPS, 0) for layer in layers]
    picked = [jnp.where(low, a, pltpu.roll(b, STEPS, 0)) for a, b in (last, [layer[:SUBLANES] for layer in layers])]
    if outs == 1:
        picked = [jnp.where(lax.axis_index("sub") == 0, *picked)]
    return picked


def pack_tile_kernel(fields, ahead, behind, *ends):
    layers = fields.shape[1]
    for out, base, unused in ((ahead, layers - STEPS, 0), (behind, 0, STEPS - 1)):
        kept = [(at, k) for at in range(FIELDS) for k in range(STEPS) if at < 2 or k != unused]
        for entry, (at, k) in enumerate(kept):
            out[entry] = fields[at, base + k].astype(bf16)
    for at in range(FIELDS):
        for first in range(0, layers, STEPS):
            halves = [end_rows([fields[at, k], fields[at, k + 1]], len(ends)) for k in (first, first + 2)]
            for out, *value in zip(ends, *halves):
                out[at, first * STEPS : (first + STEPS) * STEPS, :] = jnp.concatenate(value, 0).astype(bf16)


def layer_beside(at, k, layers, tile_before, tile_after):
    side, depth, unused = (tile_before, k, 0) if k < STEPS else (tile_after, k - STEPS - layers, STEPS - 1)
    if at == 2 and depth == unused:
        return jnp.zeros(side.shape[1:], f32)
    return side[at * STEPS + depth - (at == 2 and unused == 0)].astype(f32)


def layer_of_block(at, k, fields, tile_before, tile_after):
    layers = fields.shape[1]
    if STEPS <= k < STEPS + layers:
        return fields[at, k - STEPS]
    return layer_beside(at, k, layers, tile_before, tile_after)


NEAR, NEXT = 4, 6


def beside_tile(nearest, outs):
    rows, lanes = nearest[0].shape
    row = iota((SUBLANES, lanes), 0)
    picked = []
    for pieces, rolls in (([a[rows - SUBLANES :] for a in nearest], (4, 6, 0)), ([a[:SUBLANES] for a in nearest], (0, 4, 6))):
        a, b, c = (pltpu.roll(piece, by, 0) if by else piece for piece, by in zip(pieces, rolls))
        picked.append(jnp.where(row < NEAR, a, jnp.where(row < NEXT, b, c)))
    if outs == 1:
        picked = [jnp.where(lax.axis_index("sub") == 0, *picked)]
    return picked


def pack_sub_kernel(sides, tile_before, tile_after, ready_ref, *rest):
    ends, outs = rest[:sides], rest[sides:]
    held = ends[0].shape[1]
    layers = held // STEPS
    for at in range(FIELDS):
        before = [layer_beside(at, STEPS - 1 - k, layers, tile_before, tile_after) for k in range(STEPS - 1)]
        after = [layer_beside(at, STEPS + layers + k, layers, tile_before, tile_after) for k in range(STEPS - 1)]
        for out, own, a, b in zip(outs, ends, beside_tile(before, sides), beside_tile(after, sides)):
            out[at, :held, :] = own[at]
            out[at, held:, :] = jnp.concatenate([a, b], 0).astype(bf16)


def side_rows(at, k, layers, after_ref, before_ref):
    own = k - STEPS
    if 0 <= own < layers:
        start, rolls = own // 2 * SUBLANES, ((0, 4), (4, 0))[own % 2]
    else:
        depth = -own if own < 0 else own - layers + 1
        if depth == STEPS:
            return jnp.zeros((SUBLANES, after_ref.shape[2]), f32)
        start, rolls = layers * STEPS + (own > 0) * SUBLANES, ((0, 4), (4, 2), (2, 0))[depth - 1]
    tile, half = start // (2 * SUBLANES) * 2 * SUBLANES, start % (2 * SUBLANES)
    after, before = (ref[at, tile : tile + 2 * SUBLANES, :].astype(f32)[half : half + SUBLANES] for ref in (after_ref, before_ref))
    after, before = (pltpu.roll(value, by, 0) if by else value for value, by in zip((after, before), rolls))
    me, count = lax.axis_index("sub"), lax.axis_size("sub")
    low = iota(after.shape, 0) < STEPS
    keep_after = jnp.where(me < count - 1, 1.0, 0.0)
    keep_before = jnp.where(me > 0, 1.0, 0.0)
    return jnp.where(low, after * keep_after, before * keep_before)


def pack_rep_kernel(fields, tile_before, tile_after, sub_after, sub_before, ready_ref, ends_ref):
    layers, rows, lanes = fields.shape[1:]
    beside = 2 * STEPS
    total = layers + 2 * STEPS
    layer_at = iota((rows + beside, lanes), 1) // beside
    for at in range(FIELDS):
        packed = jnp.zeros((rows + beside, lanes), f32)
        for k in range(total):
            here = layer_of_block(at, k, fields, tile_before, tile_after), side_rows(at, k, layers, sub_after, sub_before)
            here = pltpu.roll(jnp.concatenate(here, 0), (beside * k + STEPS) % lanes, 1)
            packed = jnp.where(layer_at == k, here, packed)
        ends_ref[at] = packed


def across(value):
    return pltpu.roll(value, 1, 0) + pltpu.roll(value, value.shape[0] - 1, 0)


def beside_lanes(value):
    lanes = value.shape[1]
    lane = iota(value.shape, 1)
    left = jnp.where(lane == 0, 0.0, pltpu.roll(value, 1, 1))
    right = jnp.where(lane == lanes - 1, 0.0, pltpu.roll(value, lanes - 1, 1))
    return left + right


def laplace(below, here, above):
    return below + above + across(here) + beside_lanes(here) - 6.0 * here


def row_masks(layers, rows, lanes):
    tile, sub = lax.axis_index("tile"), lax.axis_index("sub")
    keep_low, keep_high = jnp.where(tile > 0, 1.0, 0.0), jnp.where(tile < lax.axis_size("tile") - 1, 1.0, 0.0)
    keep_before, keep_after = jnp.where(sub > 0, 1.0, 0.0), jnp.where(sub < lax.axis_size("sub") - 1, 1.0, 0.0)
    row = iota((rows + 2 * STEPS, lanes), 0)
    inside = jnp.where(row < rows, 1.0, jnp.where(row < rows + STEPS, keep_after, keep_before))
    return inside * keep_low, inside, inside * keep_high


def assemble_kernel(
    fields, tile_before, tile_after, sub_after, sub_before, ready_ref, now, ago, coef, lapped, lapped_ago
):
    layers, rows, lanes = fields.shape[1:]
    total = layers + 2 * STEPS
    tile = lax.axis_index("tile")
    keep_low, keep_high = jnp.where(tile > 0, 1.0, 0.0), jnp.where(tile < lax.axis_size("tile") - 1, 1.0, 0.0)
    for at, out in enumerate((now, ago, coef)):
        extra = viscous if at == 2 else 0.0
        for k in range(total):
            keep = keep_low if k < STEPS else keep_high if k >= STEPS + layers else 1.0
            out[k, :rows] = layer_of_block(at, k, fields, tile_before, tile_after) * keep + extra
            out[k, rows:] = side_rows(at, k, layers, sub_after, sub_before) * keep + extra
    for value, out in ((now, lapped), (ago, lapped_ago)):
        for k in range(1, total - 1):
            out[k] = laplace(value[k - 1], value[k], value[k + 1])


def window_kernel(
    now_in, ago_in, coef, lapped_in, lapped_ago_in, ends_ref, rep_after, rep_before, place_ref, states, *rest
):
    *sends, now, ago, lapped = rest
    layers, rows, lanes = states.shape[1:]
    beside = 2 * STEPS
    total, wide_rows = now.shape[:2]
    rep, reps = lax.axis_index("rep"), lax.axis_size("rep")
    keep_left, keep_right = jnp.where(rep > 0, 1.0, 0.0), jnp.where(rep < reps - 1, 1.0, 0.0)
    inside_low, inside, inside_high = row_masks(layers, rows, lanes)

    lane = iota((wide_rows, lanes), 1)
    layer_of = lane // beside
    outer = lane % beside < STEPS
    ending = (lane == 0) | (lane == lanes - 1)
    inside_side = jnp.where(layer_of < STEPS, inside_low, jnp.where(layer_of < STEPS + layers, inside, inside_high))
    inside_side = jnp.where(layer_of < total, inside_side, 0.0)
    inside_left = inside_side * jnp.where(outer, keep_left, 1.0)
    inside_right = inside_side * jnp.where(outer, 1.0, keep_right)
    lefts, rights = [], []
    for at in range(FIELDS):
        extra = viscous if at == 2 else 0.0
        left = jnp.where(outer, rep_before[at], ends_ref[at])
        right = jnp.where(outer, ends_ref[at], rep_after[at])
        lefts.append(left * inside_left + extra)
        rights.append(right * inside_right + extra)
    left_now, left_ago, left_coef = lefts
    right_now, right_ago, right_coef = rights

    def edges(left, right):
        return jnp.where(outer, pltpu.roll(right, lanes - 1, 1), pltpu.roll(left, 1, 1))

    def edge_of(k, edge):
        return jnp.where(ending, pltpu.roll(edge, (lanes - beside * k - STEPS) % lanes, 1), 0.0)

    def laplace_side(side):
        beyond = pltpu.roll(side, beside, 1) + pltpu.roll(side, lanes - beside, 1)
        return beyond + across(side) + pltpu.roll(side, 1, 1) + pltpu.roll(side, lanes - 1, 1) - 6.0 * side

    def advance(here, before, gain, lap, lap_before, mask):
        change = here - before
        driving = gain * lap - lap_before + 2.0 * nonlinear * change * change
        return (here + change + (1.0 + 2.0 * nonlinear * here) * driving) * mask

    edge_ago = edges(left_ago, right_ago)
    left_lapped, right_lapped = viscous * laplace_side(left_ago), viscous * laplace_side(right_ago)

    cells = layers * rows
    slots = place_ref.shape[1]
    lane_of = place_ref[cells:]
    loads = jnp.zeros((SUBLANES, slots), f32)
    for step in range(STEPS):
        edge = edges(left_now, right_now)
        found = jnp.zeros((rows, slots), f32)
        source = now_in if step == 0 else now
        below, here = source[step], source[step + 1]
        for k in range(step + 1, total - step - 1):
            above = source[k + 1]
            if step == 0:
                lap, before = lapped_in[k], ago_in[k]
                lap_before = viscous * (lapped_ago_in[k] + edge_of(k, edge_ago))
            else:
                lap, before, lap_before = laplace(below, here, above), ago[k], lapped[k]
            lap = lap + edge_of(k, edge)
            mask = inside_low if k < STEPS else inside_high if k >= STEPS + layers else inside
            updated = advance(here, before, coef[k], lap, lap_before, mask)
            if step < STEPS - 1:
                now[k] = updated
                ago[k] = here
                lapped[k] = viscous * lap
            own = k - STEPS
            if 0 <= own < layers:
                core = updated[:rows]
                row_of = place_ref[own * rows : (own + 1) * rows].astype(f32)
                found = found + dot(core.astype(bf16), lane_of, (1, 0)) * row_of
                if step >= STEPS - 2:
                    states[STEPS - 1 - step, own] = core
            below, here = here, above
        if step < STEPS - 1:
            lap = laplace_side(left_now)
            updated = advance(left_now, left_ago, left_coef, lap, left_lapped, inside_left)
            left_now, left_ago, left_lapped = updated, left_now, viscous * lap
            lap = laplace_side(right_now)
            updated = advance(right_now, right_ago, right_coef, lap, right_lapped, inside_right)
            right_now, right_ago, right_lapped = updated, right_now, viscous * lap
        loads = jnp.where(iota((SUBLANES, slots), 0) == step, jnp.sum(found, axis=0, keepdims=True), loads)

    size = slots // len(sends)
    for at, send in enumerate(sends):
        send[...] = loads[:STEPS, at * size : (at + 1) * size].astype(bf16)


def store_kernel(states, final_hbm, prior_hbm, sems):
    for copy in fetch(((states.at[0], final_hbm), (states.at[1], prior_hbm)), sems):
        copy.wait()


def turn_kernel(buckets, ready_ref, shapes_ref, area_ref, turned_ref, area_out):
    total = shapes_ref.shape[0]
    bucket = total // buckets
    me = lax.axis_index("tile")
    if bucket % 16 == 0:
        for k in range(buckets):
            first = pl.multiple_of((me ^ k) * bucket, 16)
            turned_ref[k * bucket : (k + 1) * bucket, :] = shapes_ref[pl.ds(first, bucket), :]
            area = jnp.zeros((1, bucket), f32)
            for part in range(buckets):
                area = jnp.where((me ^ k) == part, area_ref[:, part * bucket : (part + 1) * bucket], area)
            area_out[:, k * bucket : (k + 1) * bucket] = area
    else:
        entry = iota((total, 1), 0)
        part = entry // bucket
        wanted = entry + ((part ^ me) - part) * bucket
        picks = jnp.where(iota((total, total), 1) == wanted, 1.0, 0.0)
        turned_ref[...] = dot(picks.astype(bf16), shapes_ref[...], (1, 0)).astype(bf16)
        area_out[...] = lax.dot_general(
            area_ref[...], picks, (((1,), (1,)), ((), ())), precision=lax.Precision.HIGHEST, preferred_element_type=f32
        )


def flip_kernel(ready_ref, turned_ref, flipped_ref):
    flipped_ref[...] = turned_ref[...].astype(f32).T.astype(bf16)


def project_kernel(order, area_ref, turned_ref, *rest):
    *parts, out_ref = rest
    size = parts[0].shape[1]
    forces = 0.0
    for at, part in zip(order, parts):
        weighted = (part[...].astype(f32) * area_ref[:, at * size : (at + 1) * size]).astype(bf16)
        forces = forces + dot(weighted, turned_ref[at * size : (at + 1) * size, :], (1, 0))
    out_ref[...] = forces


def respond_kernel(addends, freq_ref, damp_ref, start_ref, flipped_ref, *rest):
    forces_in, rest = rest[:addends], rest[addends:]
    state_ref, *sends, accel = rest
    forces = forces_in[0][...]
    for ref in forces_in[1:]:
        forces = forces + ref[...].astype(f32)
    frequency, damping = freq_ref[...], damp_ref[...]
    drag, stiffness = 2.0 * damping * frequency, frequency * frequency
    displace, velocity = start_ref[0:1, :], start_ref[1:2, :]
    accel[...] = jnp.zeros_like(accel)
    for step in range(STEPS):
        acceleration = forces[step : step + 1, :] - drag * velocity - stiffness * displace
        velocity = velocity + acceleration
        displace = displace + velocity
        accel[step : step + 1, :] = acceleration
    state_ref[0:1, :] = displace
    state_ref[1:2, :] = velocity
    node = dot(accel[...].astype(bf16), flipped_ref[...], (1, 0))
    size = node.shape[1] // len(sends)
    for at, send in enumerate(sends):
        send[...] = node[:STEPS, at * size : (at + 1) * size].astype(bf16)


def return_kernel(order, route_ref, *rest):
    *parts, out_ref = rest
    size = parts[0].shape[1]
    surface = 0.0
    for at, part in zip(order, parts):
        surface = surface + dot(part[...], route_ref[at * size : (at + 1) * size, :], (1, 0))
    out_ref[...] = surface.astype(bf16)


def exchange(parts, order, crossed):
    buckets = lax.axis_size("tile")
    if len(parts) == buckets:
        own = lax.ppermute(parts[0], "rep", swaps(2, 1)) if crossed else parts[0]
        return [send(parts[k], "tile", swaps(buckets, k), crossed) if k else own for k in order]
    tiles = jnp.arange(buckets) ^ lax.axis_index("tile")
    (whole,) = parts
    steps, total = whole.shape
    stacked = whole.reshape(steps, buckets, total // buckets).transpose(1, 0, 2)
    stacked = lax.all_to_all(stacked[tiles], "tile", 0, 0, tiled=True)
    return [stacked[tiles].transpose(1, 0, 2).reshape(steps, total)]


def body(
    pressure,
    previous_pressure,
    courant_square,
    node_area,
    mode_shapes,
    frequency,
    damping_ratio,
    modal_start,
    slot_cell,
    slot_owner,
    surface_count,
):
    buckets, subs, reps = (lax.axis_size(axis) for axis in ("tile", "sub", "rep"))
    layers, rows, lanes = pressure.shape
    slots = slot_cell.shape[-1]
    modes = mode_shapes.shape[1]
    bucket = slots // buckets
    parts = buckets if buckets in (2, 4) and bucket % 16 == 0 else 1
    total = layers + 2 * STEPS
    wide_rows = rows + 2 * STEPS
    crossed = parts > 1 and reps == 2
    if crossed:
        mode_shapes, node_area = (lax.ppermute(value, "rep", swaps(2, 1)) for value in (mode_shapes, node_area))

    cells = layers * rows
    fields = jnp.stack([pressure, previous_pressure, courant_square])
    sides = 1 if subs == 2 else 2
    slab = shape_of((FIELDS * STEPS - 1, rows, lanes), bf16)
    held = shape_of((FIELDS, layers * STEPS, lanes), bf16)
    ahead, behind, *ends = call(pack_tile_kernel, (slab, slab) + (held,) * sides, (fields,))
    route, place = call(
        functools.partial(route_kernel, buckets, lanes, cells),
        (shape_of((slots, slots), bf16), shape_of((cells + lanes, slots), bf16)),
        (ahead, slot_owner.reshape(1, slots), slot_cell.reshape(1, slots), surface_count.reshape(1, 1)),
    )
    two = reps == 2
    tile_halo = [send(value, "tile", shift(buckets, by), two) for value, by in ((ahead, 1), (behind, -1))]
    if two:
        ends = [lax.ppermute(value, "rep", swaps(2, 1)) for value in ends]
    slab = shape_of((FIELDS, layers * STEPS + 2 * SUBLANES, lanes), bf16)
    packed = call(functools.partial(pack_sub_kernel, sides), (slab,) * sides, (*tile_halo, route, *ends))
    if sides == 1:
        sub_halo = (send(packed[0], "sub", swaps(2, 1), two),) * 2
    else:
        sub_halo = both_ways("sub", *packed, two)
    if two:
        tile_halo = [lax.ppermute(value, "rep", swaps(2, 1)) for value in tile_halo]

    turned, area = call(
        functools.partial(turn_kernel, buckets),
        (shape_of(mode_shapes.shape, bf16), shape_of((1, slots), f32)),
        (packed[0], mode_shapes, node_area.reshape(1, slots)),
    )

    ends = call(
        pack_rep_kernel,
        shape_of((FIELDS, wide_rows, lanes), f32),
        (fields, *tile_halo, *sub_halo, area),
    )
    if reps == 2:
        rep_halo = (lax.ppermute(ends, "rep", swaps(2, 1)),) * 2
    else:
        rep_halo = both_ways("rep", ends, ends)

    wide = shape_of((total, wide_rows, lanes), f32)
    assembled = call(assemble_kernel, (wide,) * 5, (fields, *tile_halo, *sub_halo, ends))
    wide = pltpu.VMEM(wide.shape, f32)
    part = shape_of((STEPS, slots // parts), bf16)
    block = shape_of(pressure.shape, f32)
    states, *sends = call(
        window_kernel,
        (shape_of((2, layers, rows, lanes), f32),) + (part,) * parts,
        (*assembled, ends, *rep_halo, place),
        scratch=[wide] * 3,
        micros=2.0,
    )
    final_field, prior_field = call(
        store_kernel, (block, block), (states,), out_specs=(HBM, HBM), scratch=[pltpu.SemaphoreType.DMA((2,))]
    )

    order = [k for k in (0, 2, 3, 1) if k < parts]
    forces = call(
        functools.partial(project_kernel, order),
        shape_of((STEPS, modes), f32),
        (area, turned, *exchange(sends, order, crossed)),
    )
    addends = [forces]
    for axis in ("rep", "sub", "tile"):
        count = lax.axis_size(axis)
        forces = functools.reduce(jnp.add, addends)
        if count in (2, 4):
            sent = forces.astype(bf16) if axis != "rep" else forces
            if axis == "sub":
                flipped = call(flip_kernel, shape_of(mode_shapes.shape[::-1], bf16), (sent, turned))
            places = [swaps(count, k) for k in (2, 3, 1) if k < count]
            addends = [forces] + [send(sent, axis, swap, reps == 2 and axis != "rep") for swap in places]
        else:
            addends = [lax.psum(forces, axis)]

    state, *sends = call(
        functools.partial(respond_kernel, len(addends)),
        (shape_of((2, modes), f32),) + (part,) * parts,
        (frequency.reshape(1, modes), damping_ratio.reshape(1, modes), modal_start, flipped, *addends),
        scratch=[pltpu.VMEM((SUBLANES, modes), f32)],
    )
    share = modes // (buckets * subs * reps)
    modal_state = lax.dynamic_slice_in_dim(state, lax.axis_index(("tile", "sub", "rep")) * share, share, 1)
    order = [k for k in (2, 3, 1, 0) if k < parts]
    surface = call(
        functools.partial(return_kernel, order), shape_of((STEPS, slots), bf16), (route, *exchange(sends, order, crossed))
    )
    return (final_field, prior_field, surface.reshape(1, 1, 1, STEPS, slots), modal_state)


def solution(mesh):
    in_specs = (
        P(("groups", "tile"), "sub", "rep"),
        P(("groups", "tile"), "sub", "rep"),
        P(("groups", "tile"), "sub", "rep"),
        P(("groups", "tile", "sub", "rep")),
        P(("groups", "tile", "sub", "rep"), None),
        P("groups"),
        P("groups"),
        P(None, "groups"),
        P(("groups", "tile"), "sub", "rep", None),
        P(("groups", "tile"), "sub", "rep", None, None),
        P(("groups", "sub"), "rep", "tile"),
    )
    out_specs = (
        P(("groups", "tile"), "sub", "rep"),
        P(("groups", "tile"), "sub", "rep"),
        P(("groups", "tile"), "sub", "rep", None, None),
        P(None, ("groups", "tile", "sub", "rep")),
    )
    return jax.shard_map(body, mesh=mesh, in_specs=in_specs, out_specs=out_specs, check_vma=False)
```
